32 devices in a mesh: pole: 2 (over core), row: 4 (over y, x), col: 4 (over z).
Axes of the slice: x: 2, y: 2, z: 4, core: 2. Of those that a mesh axis runs over, the one named last changes fastest.
Arguments:
- inverse_block: bfloat16 [2, 2, 4, 4, 256, 4096], P('pole', None, None, 'row', None, 'col'), may hold values from -5 to 5
- panels: bfloat16 [2, 3, 2, 4, 4, 256, 256], P('pole', None, None, 'col', 'row'), may hold values from -0.09375 to 0.09375
- panel_mask: int32 [3, 4, 4], P(None, 'col', 'row'), may hold values 0 or 1
- parent_panels: float32 [2, 2, 2, 256, 256], P('pole'), may hold values from -0.25 to 0.25
- diag_inverse: float32 [2, 3, 2, 256, 256], P('pole'), may hold values from -6 to 6
- pole_weights: float32 [2, 2], P('pole'), may hold values from 0.5 to 1.5
Outputs:
- density_panel: float32 [3, 4, 4, 256, 256], P(None, 'col', 'row', None, 'pole')
- density_diag: float32 [3, 256, 256], replicated
The draws below stay inside these ranges and needn't reach their ends.
Inputs may be any that keep to these rules, and one draw needn't show every extreme that they name: panel_mask[k, a, b] is 1 where the block of 256 ancestor rows (a, b) of supernode k's factor panel may be nonzero, 0 where it is structurally zero.
All inputs are finite; a program needn't handle non-finite values.
Results may differ from the reference program's by a relative error of at most 0.0003.
Values may be sent and summed in bfloat16 or wider, within the bound.
No kernel may reach another device: no remote copies, remote signals or barrier semaphores. Data moves between devices by JAX's collectives and lax.ppermute only.
A program may use at most 64 MiB of HBM per device.

```python
import jax
import jax.numpy as jnp
from jax import lax

M = 4096
S = 256
NSUP = 3
POLES = 2
GRID_ROWS = 4
GRID_COLS = 4
BLK = 256


def plant(values, own_key, least, top_value):
    index_at = [jax.random.randint(jax.random.fold_in(own_key, axis), (), 0, length) for axis, length in enumerate(values.shape)]
    main_axis = values.shape.index(max(values.shape))
    neighbour = index_at[:main_axis] + [(index_at[main_axis] + 1) % values.shape[main_axis]] + index_at[main_axis + 1:]
    return values.at[tuple(index_at)].set(least).at[tuple(neighbour)].set(top_value)


def block_levels(rng, extent, split, low, top_value):
    level, own = 1.0, jax.random.fold_in(rng, 6)
    for dim, parts in split:
        steps = jnp.exp(jax.random.uniform(jax.random.fold_in(own, dim), (parts,), jnp.float32, low / len(split), top_value / len(split)))
        level = level * jnp.repeat(steps, extent[dim] // parts).reshape([-1 if axis == dim else 1 for axis in range(len(extent))])
    return level


def normal_values(rng, dims, scale, most, pieces=(), held_as=jnp.bfloat16):
    factor_of = block_levels(rng, dims, pieces, -0.22, 0.18) if pieces else 1.0
    values = jax.random.normal(rng, dims, jnp.float32) * scale * factor_of
    return jnp.minimum(jnp.maximum(values, -most), most).astype(held_as)


def setup_inputs(seed: int = 0) -> dict:
    key_of = jax.random.split(jax.random.key(seed), 7)
    return {
        "inverse_block": normal_values(key_of[0], (POLES, 2, GRID_COLS, GRID_ROWS, BLK, M), 0.8, 5.0, ((0, 2), (3, 4), (5, 4))),
        "panels": normal_values(key_of[1], (POLES, NSUP, 2, GRID_COLS, GRID_ROWS, BLK, S), M ** -0.5, 0.09375, ((0, 2), (3, 4), (4, 4))),
        "panel_mask": plant((jax.random.randint(key_of[2], (NSUP, GRID_COLS, GRID_ROWS), 0, 4) < 3).astype(jnp.int32), jax.random.fold_in(key_of[2], 1), 0, 1),
        "parent_panels": normal_values(key_of[3], (POLES, NSUP - 1, 2, S, S), (2 * S) ** -0.5, 0.25, ((0, 2),), jnp.float32),
        "diag_inverse": normal_values(key_of[4], (POLES, NSUP, 2, S, S), 1.0, 6.0, ((0, 2),), jnp.float32),
        "pole_weights": jnp.clip(0.5 + 1.0 * jax.random.uniform(key_of[5], (POLES, 2), jnp.float32) ** block_levels(key_of[5], (POLES, 2), ((0, 2),), -0.2, 0.2), 0.5, 1.5),
    }


def matmul_high(left_side, right_side):
    return jnp.dot(left_side, right_side, precision=lax.Precision.HIGHEST, preferred_element_type=jnp.float32)


def complex_dot(left_real, left_imag, right_real, right_imag):
    real_part = matmul_high(left_real, right_real) - matmul_high(left_imag, right_imag)
    imag_part = matmul_high(left_real, right_imag) + matmul_high(left_imag, right_real)
    return real_part, imag_part


def panel_columns(flat_panels):
    stack_depth = flat_panels.shape[0]
    row_count = flat_panels.shape[2]
    panel_width = flat_panels.shape[3]
    upper_rows = jnp.concatenate([flat_panels[:, 0], flat_panels[:, 1]], axis=-1)
    lower_rows = jnp.concatenate([-flat_panels[:, 1], flat_panels[:, 0]], axis=-1)
    upper_rows = jnp.moveaxis(upper_rows, 0, 1).reshape(row_count, stack_depth * 2 * panel_width)
    lower_rows = jnp.moveaxis(lower_rows, 0, 1).reshape(row_count, stack_depth * 2 * panel_width)
    return upper_rows, lower_rows


def column_product(stored_columns, upper_rows, lower_rows):
    contract_dims = (((0,), (0,)), ((), ()))
    first_term = lax.dot_general(stored_columns[0], upper_rows, contract_dims, preferred_element_type=jnp.float32)
    second_term = lax.dot_general(stored_columns[1], lower_rows, contract_dims, preferred_element_type=jnp.float32)
    return first_term + second_term


def reference(inverse_block, panels, panel_mask, parent_panels, diag_inverse, pole_weights):
    block_flags = jnp.repeat(panel_mask.reshape(NSUP, GRID_COLS * GRID_ROWS), BLK, axis=1).astype(jnp.bfloat16)

    def one_pole(carried, inputs):
        block_part, panel_part, parent, diag_blocks, weight = inputs
        ancestor = block_part.reshape(2, M, M)
        masked = panel_part.reshape(NSUP, 2, M, S) * block_flags[:, None, :, None]
        upper_rows, lower_rows = panel_columns(masked)
        products = column_product(ancestor, upper_rows, lower_rows)
        panel_terms = []
        diag_terms = []
        x_real = None
        x_imag = None
        z_real = None
        z_imag = None
        for level in range(NSUP):
            base_real = products[:, level * 2 * S:level * 2 * S + S]
            base_imag = products[:, level * 2 * S + S:(level + 1) * 2 * S]
            if level == 0:
                x_real = -base_real
                x_imag = -base_imag
            else:
                carry_real, carry_imag = complex_dot(x_real, x_imag, parent[level - 1, 0], parent[level - 1, 1])
                x_real = -(base_real + carry_real)
                x_imag = -(base_imag + carry_imag)
            own_real = masked[level, 0].astype(jnp.float32)
            own_imag = masked[level, 1].astype(jnp.float32)
            sum_real, sum_imag = complex_dot(own_real.T, own_imag.T, x_real, x_imag)
            y_real = diag_blocks[level, 0] - sum_real
            y_imag = diag_blocks[level, 1] - sum_imag
            if level > 0:
                back_real, back_imag = complex_dot(parent[level - 1, 0].T, parent[level - 1, 1].T, z_real, z_imag)
                y_real = y_real - back_real
                y_imag = y_imag - back_imag
            if level + 1 < NSUP:
                next_real = masked[level + 1, 0].astype(jnp.float32)
                next_imag = masked[level + 1, 1].astype(jnp.float32)
                follow_real, follow_imag = complex_dot(next_real.T, next_imag.T, x_real, x_imag)
                mix_real, mix_imag = complex_dot(y_real, y_imag, parent[level, 0], parent[level, 1])
                z_real = -(follow_real.T + mix_real)
                z_imag = -(follow_imag.T + mix_imag)
            panel_terms.append(weight[0] * x_imag + weight[1] * x_real)
            diag_terms.append(weight[0] * y_imag + weight[1] * y_real)
        return (carried[0] + jnp.stack(panel_terms), carried[1] + jnp.stack(diag_terms)), None

    initial = (jnp.zeros((NSUP, M, S), jnp.float32), jnp.zeros((NSUP, S, S), jnp.float32))
    totals, unused = lax.scan(one_pole, initial, (inverse_block, panels, parent_panels, diag_inverse, pole_weights))
    return totals[0].reshape(NSUP, GRID_COLS, GRID_ROWS, BLK, S), totals[1]
```

```python
import jax
import jax.numpy as jnp
from jax import lax
from jax.sharding import PartitionSpec as P

HIGH = lax.Precision.HIGH


def is_power_of_two(n):
    return n & (n - 1) == 0


def dot_high(left, right, dims=((1,), (0,))):
    return lax.dot_general(left, right, (dims, ((), ())), precision=HIGH, preferred_element_type=jnp.float32)


def right_block(real, imag):
    return jnp.concatenate(
        [jnp.concatenate([real, imag], axis=1), jnp.concatenate([-imag, real], axis=1)], axis=0
    )


def xor_order(stack, me, count):
    bits = count.bit_length() - 1
    rest = stack.shape[1:]
    values = stack.reshape((2,) * bits + rest)
    for axis in range(bits):
        bit = (me >> (bits - 1 - axis)) & 1
        values = jnp.where(bit == 1, jnp.flip(values, axis), values)
    return values.reshape((count,) + rest)


def exchange(value, axes, count, distance):
    return lax.ppermute(value, axes, [(i, i ^ distance) for i in range(count)])


def gather_line(piece, me, count, axis):
    received = []
    from_left = from_right = piece
    for step in range(1, count):
        if 2 * step > count + 1:
            moving = jnp.where(me >= step - 1, from_left, from_right)
            pairs = [(i, i + 1) for i in range(step - 1, count - 1)]
            pairs += [(i, i - 1) for i in range(1, count - step + 1)]
            from_left = from_right = lax.ppermute(moving, axis, pairs)
        else:
            from_left = lax.ppermute(from_left, axis, [(i, i + 1) for i in range(step - 1, count - 1)])
            from_right = lax.ppermute(from_right, axis, [(i, i - 1) for i in range(1, count - step + 1)])
        if 2 * step >= count:
            got = from_left if 2 * step > count + 1 else jnp.where(me >= step, from_left, from_right)
            owner = jnp.clip(jnp.where(me >= step, me - step, me + step), 0, count - 1)
            received.append((owner, got))
        else:
            received.append((jnp.maximum(me - step, 0), from_left))
            received.append((jnp.minimum(me + step, count - 1), from_right))
    return received


def scatter_sum(stack, axis, count):
    width = stack.shape[-1]
    bits = [1 << b for b in range(count.bit_length() - 1)]
    halves = [stack[..., : width // 2], stack[..., width // 2 :]]
    orders = [bits, bits[::-1]]
    held = [{t: half[t] for t in range(count)} for half in halves]
    for step in range(len(bits)):
        for h in range(2):
            bit = orders[h][step]
            away = sorted(t for t in held[h] if t & bit)
            sent = exchange(jnp.stack([held[h][t] for t in away]), axis, count, bit)
            held[h] = {t ^ bit: held[h][t ^ bit] + sent[n] for n, t in enumerate(away)}
    return jnp.concatenate([held[0][0], held[1][0]], axis=-1)


def tree_sum(values):
    while len(values) > 1:
        values = [values[i] + values[i + 1] for i in range(0, len(values), 2)]
    return values[0]


def sum_everywhere(value, sizes):
    poles, rows, cols = sizes
    group = poles * rows
    if group > 8 or not is_power_of_two(group) or not is_power_of_two(cols):
        return lax.psum(value, ("pole", "row", "col"))
    axes = ("pole", "row")
    me = lax.axis_index("pole") * rows + lax.axis_index("row")
    pieces = xor_order(value.reshape(group, value.shape[0] // group, value.shape[1]), me, group)
    mine = tree_sum([pieces[0]] + [exchange(pieces[t], axes, group, t) for t in range(1, group)])
    mine = tree_sum([mine] + [exchange(mine, "col", cols, t) for t in range(1, cols)])
    whole = jnp.stack([mine] + [exchange(mine, axes, group, t) for t in range(1, group)])
    return xor_order(whole, me, group).reshape(value.shape)


def pole_scatter(value, poles):
    if poles != 2:
        return lax.psum_scatter(value, "pole", scatter_dimension=1, tiled=True)
    half = value.shape[1] // 2
    low = lax.axis_index("pole") == 0
    kept = jnp.where(low, value[:, :half], value[:, half:])
    sent = jnp.where(low, value[:, half:], value[:, :half])
    return kept + exchange(sent, "pole", 2, 1)


def make_per_device(sizes):
    poles, rows, cols = sizes

    def per_device(inverse_block, panels, panel_mask, parent_panels, diag_inverse, pole_weights):
        levels = panels.shape[1]
        height = panels.shape[5]
        width = panels.shape[6]
        my_row = lax.axis_index("row")
        my_col = lax.axis_index("col")
        first = ((my_row == 0) & (my_col == 0)).astype(jnp.float32)
        blocks = inverse_block[0, :, :, 0]
        flags = panel_mask[:, 0, 0].astype(jnp.bfloat16)
        masked = [panels[0, k, :, 0, 0] * flags[k] for k in range(levels)]
        weight_real = pole_weights[0, 0]
        weight_imag = pole_weights[0, 1]
        parent_blocks = [
            right_block(parent_panels[0, k, 0], parent_panels[0, k, 1]) for k in range(levels - 1)
        ]

        def base(level):
            pieces = [(my_col, masked[level])] + gather_line(masked[level], my_col, cols, "col")
            total = 0.0
            for owner, piece in pieces:
                columns = lax.dynamic_index_in_dim(blocks, owner, 1, keepdims=False)
                columns = columns.reshape(2 * height, columns.shape[2])
                total = total + lax.dot_general(
                    columns,
                    right_block(piece[0], piece[1]),
                    (((0,), (0,)), ((), ())),
                    preferred_element_type=jnp.float32,
                )
            stack = total.reshape(rows, height, 2 * width)
            if not is_power_of_two(rows):
                return lax.psum_scatter(total, "row", scatter_dimension=0, tiled=True)
            return scatter_sum(xor_order(stack, my_row, rows), "row", rows)

        def left_product(panel, x):
            real = dot_high(panel[0].astype(jnp.float32), x, ((0,), (0,)))
            imag = dot_high(panel[1].astype(jnp.float32), x, ((0,), (0,)))
            return real[:, :width] - imag[:, width:], real[:, width:] + imag[:, :width]

        x = None
        z = None
        panel_terms = []
        diag_terms = []
        for level in range(levels):
            total = base(level)
            x = -total if level == 0 else -(total + dot_high(x, parent_blocks[level - 1]))
            own_real, own_imag = left_product(masked[level], x)
            y_real = diag_inverse[0, level, 0] * first - own_real
            y_imag = diag_inverse[0, level, 1] * first - own_imag
            if level > 0:
                q = parent_panels[0, level - 1]
                real = dot_high(q[0], z, ((0,), (0,)))
                imag = dot_high(q[1], z, ((0,), (0,)))
                y_real = y_real - (real[:, :width] - imag[:, width:])
                y_imag = y_imag - (real[:, width:] + imag[:, :width])
            if level + 1 < levels:
                follow_real, follow_imag = left_product(masked[level + 1], x)
                y = jnp.concatenate([y_real, y_imag], axis=1)
                follow = jnp.concatenate([follow_real.T, follow_imag.T], axis=1)
                z = -(follow + dot_high(y, parent_blocks[level]))
            panel_terms.append(
                pole_scatter(weight_real * x[:, width:] + weight_imag * x[:, :width], poles)
            )
            diag_terms.append(
                sum_everywhere(weight_real * y_imag + weight_imag * y_real, sizes)
            )
        return jnp.stack(panel_terms)[:, None, None], jnp.stack(diag_terms)

    return per_device


def solution(mesh):
    placed = (
        P("pole", None, None, "row", None, "col"),
        P("pole", None, None, "col", "row", None, None),
        P(None, "col", "row"),
        P("pole", None, None, None, None),
        P("pole", None, None, None, None),
        P("pole", None),
    )
    return jax.shard_map(
        make_per_device((mesh.shape["pole"], mesh.shape["row"], mesh.shape["col"])),
        mesh=mesh,
        in_specs=placed,
        out_specs=(P(None, "col", "row", None, "pole"), P()),
        check_vma=False,
    )
```

```python
import functools

import jax
import jax.numpy as jnp
from jax import lax
from jax.experimental import pallas as pl
from jax.experimental.pallas import tpu as pltpu
from jax.sharding import PartitionSpec as P

F32 = jnp.float32
BF16 = jnp.bfloat16
VMEM_LIMIT = 48 * 1024 * 1024
WHOLE = pl.BlockSpec(memory_space=pltpu.VMEM)
SCALARS = pl.BlockSpec(memory_space=pltpu.SMEM)
ANYWHERE = pl.BlockSpec(memory_space=pl.ANY)


def params():
    return pltpu.CompilerParams(vmem_limit_bytes=VMEM_LIMIT)


def mm(left, right):
    return jnp.dot(left, right, preferred_element_type=F32)


def mm_t(left, right):
    return lax.dot_general(left, right, (((1,), (1,)), ((), ())), preferred_element_type=F32)


def split(value):
    high = value.astype(BF16)
    return high, (value - high.astype(F32)).astype(BF16)


def exchange(value, axes, count, distance):
    return lax.ppermute(value, axes, [(i, i ^ distance) for i in range(count)])


def tree_sum(values):
    while len(values) > 1:
        values = [values[i] + values[i + 1] for i in range(0, len(values), 2)]
    return values[0]


def xor_order(stack, me, count):
    bits = count.bit_length() - 1
    rest = stack.shape[1:]
    values = stack.reshape((2,) * bits + rest)
    for axis in range(bits):
        bit = (me >> (bits - 1 - axis)) & 1
        values = jnp.where(bit == 1, jnp.flip(values, axis), values)
    return values.reshape((count,) + rest)


def mask_kernel(first_level, flag_ref, panel_ref, *out_refs):
    levels = panel_ref.shape[0]
    for k in range(levels):
        flag = flag_ref[first_level + k].astype(F32)
        for part in range(2):
            value = panel_ref[k, part].astype(F32) * flag
            out_refs[k][part] = value.T.astype(BF16)


def keep_kernel(flag_ref, panel_ref, out_ref):
    for k in range(panel_ref.shape[0]):
        flag = flag_ref[k].astype(F32)
        out_ref[k] = (panel_ref[k].astype(F32) * flag).astype(BF16)


def parent_kernel(parent_ref, high_ref, low_ref):
    width = parent_ref.shape[2]
    for k in range(parent_ref.shape[0]):
        real_high, real_low = split(parent_ref[k, 0].T)
        imag_high, imag_low = split(parent_ref[k, 1].T)
        for ref, real, imag in ((high_ref, real_high, imag_high), (low_ref, real_low, imag_low)):
            ref[k, :width, :width] = real
            ref[k, :width, width:] = -imag
            ref[k, width:, :width] = imag
            ref[k, width:, width:] = real


def make_level(rows, width, height, owners, slots, level, levels, packed):
    count = len(slots)
    has_prev = level > 0
    has_next = level + 1 < levels
    local = rows * height
    half = width // 2

    def kernel(*refs):
        refs = list(refs)

        def take(n=None):
            if n is None:
                return refs.pop(0)
            return [refs.pop(0) for _ in range(n)]

        place_ref, weight_ref = take(2)
        slot_refs = [take(n) for n in slots]
        block_ref = take()
        panel_refs = take(rows)
        rest_ref = take()
        if has_prev:
            prev_high_ref, prev_low_ref, parent_high_ref, parent_low_ref = take(4)
        if has_next:
            next_high_ref, next_low_ref, next_diag_ref = take(3)
            x_high_ref, x_low_ref, next_rest_ref = take(3)
        out_a, out_b = take(2)
        block_buf, panel_buf = take(2)
        if has_prev:
            prev_high, prev_low = take(2)
        term_buf, diag_buf, block_sem, panel_sem, prev_sem = take(5)
        assert not refs

        inner = place_ref[count]
        my_row = place_ref[count + 1]
        pole = place_ref[count + 2]
        first = (place_ref[count + 3]).astype(F32)

        block_copies = []
        for n in range(count):
            owner = place_ref[n]
            if not packed:
                block_copies.append(
                    pltpu.make_async_copy(
                        block_ref.at[:, owner], block_buf.at[n], block_sem.at[n, 0]
                    )
                )
                continue
            for t in range(rows):
                start = pl.multiple_of((my_row ^ t) * height, height)
                block_copies.append(
                    pltpu.make_async_copy(
                        block_ref.at[:, owner, :, pl.ds(start, height)],
                        block_buf.at[n, :, :, pl.ds(t * height, height)],
                        block_sem.at[n, t],
                    )
                )
        panel_copies = []
        for k in range(2 if has_next else 1):
            for t in range(rows):
                for part in range(2):
                    panel_copies.append(
                        pltpu.make_async_copy(
                            panel_refs[t].at[level + k, part],
                            panel_buf.at[k, pl.ds(t * height, height), pl.ds(part * width, width)],
                            panel_sem.at[k, t, part],
                        )
                    )
        prev_copies = []
        if has_prev:
            prev_copies = [
                pltpu.make_async_copy(prev_high_ref, prev_high, prev_sem.at[0]),
                pltpu.make_async_copy(prev_low_ref, prev_low, prev_sem.at[1]),
            ]
        for copy in block_copies + prev_copies + panel_copies:
            copy.start()

        total = None
        for n in range(count):
            if slots[n] == 2:
                piece = [
                    jnp.where(inner == 1, slot_refs[n][0][part], slot_refs[n][1][part])
                    for part in range(2)
                ]
            else:
                piece = [slot_refs[n][0][part] for part in range(2)]
            left = jnp.concatenate(
                [
                    jnp.concatenate([piece[0], -piece[1]], axis=1),
                    jnp.concatenate([piece[1], piece[0]], axis=1),
                ],
                axis=0,
            )
            each = len(block_copies) // count
            for copy in block_copies[n * each : (n + 1) * each]:
                copy.wait()
            term = mm(left, block_buf[n].reshape(2 * height, local))
            total = term if total is None else total + term
        if has_prev:
            for copy in prev_copies:
                copy.wait()
            total = total + mm(parent_high_ref[level - 1], prev_high[...])
            total = total + mm(parent_high_ref[level - 1], prev_low[...])
            total = total + mm(parent_low_ref[level - 1], prev_high[...])
        x = -total
        weight_real = weight_ref[0]
        weight_imag = weight_ref[1]
        term_buf[...] = weight_real * x[width:] + weight_imag * x[:width]
        x_high, x_low = split(x)
        if has_next:
            x_high_ref[...] = x_high
            x_low_ref[...] = x_low
        for copy in panel_copies:
            copy.wait()

        def transposed_times(k):
            panel = panel_buf[k]
            product = mm(x_high, panel) + mm(x_low, panel)
            real = product[:width, :width] - product[width:, width:]
            imag = product[:width, width:] + product[width:, :width]
            return real, imag

        own_real, own_imag = transposed_times(0)
        scale = first if level == 0 else 1.0
        y_real = rest_ref[0] * scale - own_real.T
        y_imag = rest_ref[1] * scale - own_imag.T
        diag_buf[...] = weight_real * y_imag + weight_imag * y_real
        if has_next:
            follow_real, follow_imag = transposed_times(1)
            y_high, y_low = split(jnp.concatenate([y_real, y_imag], axis=1))
            parent_high = next_high_ref[level]
            parent_low = next_low_ref[level]
            mixed = mm_t(y_high, parent_high) + mm_t(y_low, parent_high) + mm_t(y_high, parent_low)
            z = -jnp.concatenate(
                [follow_real + mixed[:, :width], follow_imag + mixed[:, width:]], axis=0
            )
            z_high, z_low = split(z)
            back = mm(parent_high, z_high) + mm(parent_high, z_low) + mm(parent_low, z_high)
            next_rest_ref[0] = next_diag_ref[0] * first - back[:width]
            next_rest_ref[1] = next_diag_ref[1] * first - back[width:]
        if packed:
            part = half // rows
            for ref, side in ((out_a, pole), (out_b, 1 - pole)):
                begin = pl.multiple_of(side * half, half)
                for t in range(rows):
                    ref[t, :half, :] = term_buf[pl.ds(begin, half), t * height : (t + 1) * height]
                    piece_at = pl.multiple_of(begin + (my_row ^ t) * part, part)
                    ref[t, half:, :] = diag_buf[pl.ds(piece_at, part), :]
        else:
            out_a[...] = term_buf[...]
            out_b[...] = diag_buf[...]

    def call(place, weights, pieces, blocks, panels, rest, prev, parents, next_diag):
        operands = [place, weights]
        specs = [SCALARS, SCALARS]
        for slot in pieces:
            operands += slot
            specs += [WHOLE] * len(slot)
        operands += [blocks] + panels + [rest]
        specs += [ANYWHERE] * (1 + rows) + [WHOLE]
        if has_prev:
            operands += list(prev) + list(parents)
            specs += [ANYWHERE, ANYWHERE, WHOLE, WHOLE]
        outs = []
        if has_next:
            operands += list(parents) + [next_diag]
            specs += [WHOLE] * 3
            outs += [
                jax.ShapeDtypeStruct((2 * width, local), BF16),
                jax.ShapeDtypeStruct((2 * width, local), BF16),
                jax.ShapeDtypeStruct((2, width, width), F32),
            ]
        if packed:
            outs += [jax.ShapeDtypeStruct((rows, half + half // rows, height), F32)] * 2
        else:
            outs += [
                jax.ShapeDtypeStruct((width, local), F32),
                jax.ShapeDtypeStruct((width, width), F32),
            ]
        scratch = [
            pltpu.VMEM((count, 2, height, local), BF16),
            pltpu.VMEM((2 if has_next else 1, local, 2 * width), BF16),
        ]
        if has_prev:
            scratch += [pltpu.VMEM((2 * width, local), BF16)] * 2
        scratch += [
            pltpu.VMEM((width, local), F32),
            pltpu.VMEM((width, width), F32),
            pltpu.SemaphoreType.DMA((count, rows)),
            pltpu.SemaphoreType.DMA((2, rows, 2)),
            pltpu.SemaphoreType.DMA((2,)),
        ]
        big = 2 * (2 * width) * local
        flops = big * (2 * height * count + (6 * width if has_prev else 0) + 4 * width * (2 if has_next else 1))
        return pl.pallas_call(
            kernel,
            out_shape=outs,
            in_specs=specs,
            out_specs=[WHOLE] * len(outs),
            scratch_shapes=scratch,
            compiler_params=params(),
            cost_estimate=pl.CostEstimate(flops=flops, bytes_accessed=8 << 20, transcendentals=0),
            name="level_%d" % level,
        )(*operands)

    return call


def gather_four(piece, me, axis):
    inner = (me == 1) | (me == 2)
    near = lax.ppermute(piece, axis, [(0, 1), (1, 0), (2, 3), (3, 2)])
    middle = lax.ppermute(piece, axis, [(1, 2), (2, 1)])
    outer_2 = lax.ppermute(middle, axis, [(1, 0), (2, 3)])
    middle_2 = lax.ppermute(near, axis, [(1, 2), (2, 1)])
    outer_3 = lax.ppermute(middle_2, axis, [(1, 0), (2, 3)])
    owners = [
        me,
        me ^ 1,
        jnp.where(inner, 3 - me, me ^ 2),
        jnp.where(inner, (3 - me) ^ 1, me ^ 3),
    ]
    return owners, [[piece], [near], [middle, outer_2], [middle_2, outer_3]]


def gather_line(piece, me, count, axis):
    owners, slots = [me], [[piece]]
    from_left = from_right = piece
    for step in range(1, count):
        from_left = lax.ppermute(from_left, axis, [(i, i + 1) for i in range(step - 1, count - 1)])
        from_right = lax.ppermute(from_right, axis, [(i, i - 1) for i in range(1, count - step + 1)])
        if 2 * step >= count:
            owners.append(jnp.clip(jnp.where(me >= step, me - step, me + step), 0, count - 1))
            slots.append([jnp.where(me >= step, from_left, from_right)])
        else:
            owners += [jnp.maximum(me - step, 0), jnp.minimum(me + step, count - 1)]
            slots += [[from_left], [from_right]]
    return owners, slots


def gather(piece, me, count, axis):
    if count == 4:
        return gather_four(piece, me, axis)
    return gather_line(piece, me, count, axis)


def make_per_device(sizes):
    poles, rows, cols = sizes

    def per_device(inverse_block, panels, panel_mask, parent_panels, diag_inverse, pole_weights):
        levels = panels.shape[1]
        height = panels.shape[5]
        width = panels.shape[6]
        half = width // 2
        part = half // rows
        packed = (
            poles == 2
            and rows & (rows - 1) == 0
            and cols & (cols - 1) == 0
            and height == width
            and height % 128 == 0
            and part % 8 == 0
        )
        my_pole = lax.axis_index("pole")
        my_row = lax.axis_index("row")
        my_col = lax.axis_index("col")
        first = ((my_row == 0) & (my_col == 0)).astype(jnp.int32)
        inner = ((my_col == 1) | (my_col == 2)).astype(jnp.int32)
        blocks = inverse_block[0, :, :, 0]
        local_panels = panels[0, :, :, 0, 0]
        flags = panel_mask[:, 0, 0]
        weights = pole_weights[0]
        flipped = (2, width, height)

        def masked_transposed(first_level, value):
            return pl.pallas_call(
                functools.partial(mask_kernel, first_level),
                out_shape=[jax.ShapeDtypeStruct(flipped, BF16)] * value.shape[0],
                in_specs=[SCALARS, WHOLE],
                out_specs=[WHOLE] * value.shape[0],
                compiler_params=params(),
                name="mask_%d" % first_level,
            )(flags, value)

        pieces = masked_transposed(0, local_panels[:1])
        pieces += masked_transposed(1, local_panels[1:])
        kept = pl.pallas_call(
            keep_kernel,
            out_shape=jax.ShapeDtypeStruct(local_panels.shape, BF16),
            in_specs=[SCALARS, WHOLE],
            out_specs=WHOLE,
            compiler_params=params(),
            name="mask_rows",
        )(flags, local_panels)
        parents = pl.pallas_call(
            parent_kernel,
            out_shape=[jax.ShapeDtypeStruct((levels - 1, 2 * width, 2 * width), BF16)] * 2,
            in_specs=[WHOLE],
            out_specs=[WHOLE] * 2,
            compiler_params=params(),
            name="parents",
        )(parent_panels[0])
        gathered = [gather(piece, my_col, cols, "col") for piece in pieces]
        if packed:
            row_panels = [kept] + [exchange(kept, "row", rows, t) for t in range(1, rows)]
        else:
            row_panels = list(lax.all_gather(kept, "row"))

        def sum_rows(stack):
            return tree_sum([stack[0]] + [exchange(stack[t], "row", rows, t) for t in range(1, rows)])

        def spread(piece):
            whole = tree_sum([piece] + [exchange(piece, "col", cols, t) for t in range(1, cols)])
            whole = jnp.stack([whole] + [exchange(whole, "row", rows, t) for t in range(1, rows)])
            whole = xor_order(whole, my_row, rows)
            other = exchange(whole, "pole", 2, 1)
            return xor_order(jnp.stack([whole, other]), my_pole, 2)

        rest = diag_inverse[0, 0]
        prev = None
        panel_parts = []
        diag_parts = []
        waiting = []
        for level in range(levels):
            owners, slots = gathered[level]
            place = jnp.stack(
                [jnp.asarray(v, jnp.int32) for v in owners + [inner, my_row, my_pole, first]]
            )
            call = make_level(
                rows, width, height, owners, [len(s) for s in slots], level, levels, packed
            )
            has_next = level + 1 < levels
            outs = call(
                place,
                weights,
                slots,
                blocks,
                row_panels,
                rest,
                prev,
                parents,
                diag_inverse[0, level + 1] if has_next else None,
            )
            if has_next:
                prev = outs[:2]
                rest = outs[2]
                outs = outs[3:]
            if packed:
                mine = sum_rows(outs[0] + exchange(outs[1], "pole", 2, 1))
                panel_parts.append(mine[:half].T)
                waiting.append(mine[half:])
                if level >= levels - 2:
                    got = spread(jnp.stack(waiting))
                    for n in range(len(waiting)):
                        diag_parts.append(got[:, :, n].reshape(width, width))
                    waiting = []
            else:
                mine = lax.psum_scatter(outs[0], "row", scatter_dimension=1, tiled=True)
                mine = lax.psum_scatter(mine, "pole", scatter_dimension=0, tiled=True)
                panel_parts.append(mine.T)
                diag_parts.append(lax.psum(outs[1], ("pole", "row", "col")))
        return jnp.stack(panel_parts)[:, None, None], jnp.stack(diag_parts)

    return per_device


def solution(mesh):
    placed = (
        P("pole", None, None, "row", None, "col"),
        P("pole", None, None, "col", "row", None, None),
        P(None, "col", "row"),
        P("pole", None, None, None, None),
        P("pole", None, None, None, None),
        P("pole", None),
    )
    return jax.shard_map(
        make_per_device((mesh.shape["pole"], mesh.shape["row"], mesh.shape["col"])),
        mesh=mesh,
        in_specs=placed,
        out_specs=(P(None, "col", "row", None, "pole"), P()),
        check_vma=False,
    )
```

```python
import functools

import jax
import jax.numpy as jnp
from jax import lax
from jax.experimental import pallas as pl
from jax.experimental.pallas import tpu as pltpu
from jax.sharding import PartitionSpec as P

F32 = jnp.float32
BF16 = jnp.bfloat16
VMEM_LIMIT = 36 * 1024 * 1024
WHOLE = pl.BlockSpec(memory_space=pltpu.VMEM)
SCALARS = pl.BlockSpec(memory_space=pltpu.SMEM)
ANYWHERE = pl.BlockSpec(memory_space=pl.ANY)


def params():
    return pltpu.CompilerParams(vmem_limit_bytes=VMEM_LIMIT)


def mm(left, right):
    return jnp.dot(left, right, preferred_element_type=F32)


def mm_t(left, right):
    return lax.dot_general(left, right, (((1,), (1,)), ((), ())), preferred_element_type=F32)


def split(value):
    high = value.astype(BF16)
    return high, (value - high.astype(F32)).astype(BF16)


def exchange(value, axes, count, distance):
    return lax.ppermute(value, axes, [(i, i ^ distance) for i in range(count)])


def tree_sum(values):
    while len(values) > 1:
        values = [values[i] + values[i + 1] for i in range(0, len(values), 2)]
    return values[0]


def xor_order(stack, me, count):
    bits = count.bit_length() - 1
    rest = stack.shape[1:]
    values = stack.reshape((2,) * bits + rest)
    for axis in range(bits):
        bit = (me >> (bits - 1 - axis)) & 1
        values = jnp.where(bit == 1, jnp.flip(values, axis), values)
    return values.reshape((count,) + rest)


def mask_kernel(levels, keep, flag_ref, panel_ref, *refs):
    refs = list(refs)
    out_refs = [refs.pop(0) for _ in levels]
    kept_ref = refs.pop(0) if keep else None
    buf, sem = refs
    first = 0 if keep else levels[0]
    copy = pltpu.make_async_copy(panel_ref.at[pl.ds(first, buf.shape[0])], buf, sem)
    copy.start()
    copy.wait()
    for k in range(buf.shape[0]):
        flag = flag_ref[first + k].astype(F32)
        for part in range(2):
            value = buf[k, part].astype(F32) * flag
            if keep:
                kept_ref[k, part] = value.astype(BF16)
            if first + k in levels:
                out_refs[levels.index(first + k)][part] = value.T.astype(BF16)


def parent_kernel(parent_ref, high_ref, low_ref):
    width = parent_ref.shape[2]
    for k in range(parent_ref.shape[0]):
        real_high, real_low = split(parent_ref[k, 0].T)
        imag_high, imag_low = split(parent_ref[k, 1].T)
        for ref, real, imag in ((high_ref, real_high, imag_high), (low_ref, real_low, imag_low)):
            ref[k, :width, :width] = real
            ref[k, :width, width:] = -imag
            ref[k, width:, :width] = imag
            ref[k, width:, width:] = real


def left_block(real, imag):
    return jnp.concatenate(
        [jnp.concatenate([real, -imag], axis=1), jnp.concatenate([imag, real], axis=1)], axis=0
    )


class Slots:
    def __init__(self, slots):
        self.operands = []
        self.slots = []
        for slot in slots:
            self.slots.append([(self.place(array), index) for array, index in slot])

    def place(self, array):
        for n, operand in enumerate(self.operands):
            if operand is array:
                return n
        self.operands.append(array)
        return len(self.operands) - 1

    def left(self, refs, n, inner):
        parts = []
        for part in range(2):
            values = [
                refs[at][part] if index is None else refs[at][index, part]
                for at, index in self.slots[n]
            ]
            parts.append(values[0] if len(values) == 1 else jnp.where(inner == 1, *values))
        return left_block(*parts)


def block_copies(block_ref, buf, sem, owners, my_row, rows, height, ordered):
    copies = []
    for n, owner in enumerate(owners):
        if not ordered:
            copies.append([pltpu.make_async_copy(block_ref.at[:, owner], buf.at[n], sem.at[n, 0])])
            continue
        copies.append(
            [
                pltpu.make_async_copy(
                    block_ref.at[
                        :, owner, :, pl.ds(pl.multiple_of((my_row ^ t) * height, height), height)
                    ],
                    buf.at[n, :, :, pl.ds(t * height, height)],
                    sem.at[n, t],
                )
                for t in range(rows)
            ]
        )
    return copies


def early_products(rows, width, height, ordered, place, level_slots, blocks):
    levels = len(level_slots)
    count = len(level_slots[0])
    slots = Slots([slot for level in level_slots for slot in level])
    local = rows * height

    def kernel(place_ref, block_ref, *refs):
        piece_refs = refs[: len(slots.operands)]
        out_refs = refs[len(slots.operands) :][:levels]
        buf, left_buf, sem = refs[-3:]
        owners = [place_ref[4 + n] for n in range(count)]
        copies = block_copies(block_ref, buf, sem, owners, place_ref[1], rows, height, ordered)
        for group in copies:
            for copy in group:
                copy.start()
        for level in range(levels):
            for n in range(count):
                left_buf[
                    level * 2 * width : (level + 1) * 2 * width,
                    n * 2 * height : (n + 1) * 2 * height,
                ] = slots.left(piece_refs, level * count + n, place_ref[0])
        for group in copies:
            for copy in group:
                copy.wait()
        right = buf[...].reshape(count * 2 * height, local)
        for level in range(levels):
            left = left_buf[level * 2 * width : (level + 1) * 2 * width, :]
            out_refs[level][...] = mm(left, right)

    return pl.pallas_call(
        kernel,
        out_shape=[jax.ShapeDtypeStruct((2 * width, local), F32)] * levels,
        in_specs=[SCALARS, ANYWHERE] + [WHOLE] * len(slots.operands),
        out_specs=[WHOLE] * levels,
        scratch_shapes=[
            pltpu.VMEM((count, 2, height, local), BF16),
            pltpu.VMEM((levels * 2 * width, count * 2 * height), BF16),
            pltpu.SemaphoreType.DMA((count, rows)),
        ],
        compiler_params=params(),
        cost_estimate=pl.CostEstimate(
            flops=2 * levels * 2 * width * local * count * 2 * height,
            bytes_accessed=12 << 20,
            transcendentals=0,
        ),
        name="early",
    )(place, blocks, *slots.operands)


def level_products(
    rows, width, height, packed, natural, level, early, place, weights, level_slots, blocks, panels,
    total, rest, next_total, parents, next_diag,
):
    count = len(level_slots)
    slots = Slots(level_slots)
    has_next = next_total is not None
    local = rows * height
    half = width // 2
    part = half // rows
    with_diag = packed and not natural

    def kernel(*refs):
        refs = list(refs)

        def take(n):
            return [refs.pop(0) for _ in range(n)]

        place_ref, weight_ref = take(2)
        piece_refs = take(len(slots.operands))
        (block_ref,) = take(1)
        panel_refs = take(rows)
        total_ref, rest_ref = take(2)
        if has_next:
            next_total_ref, high_ref, low_ref, next_diag_ref = take(4)
            next_out_ref, next_rest_ref = take(2)
        if packed:
            keep_ref, send_ref = take(2)
        else:
            (term_out_ref,) = take(1)
        if not with_diag:
            (diag_out_ref,) = take(1)
        buf, left_buf, panel_buf, total_buf, next_buf, term_buf, diag_buf = take(7)
        block_sem, panel_sem, total_sem = take(3)
        assert not refs

        inner, my_row, pole = place_ref[0], place_ref[1], place_ref[2]
        first = place_ref[3].astype(F32)
        owners = [place_ref[4 + early + n] for n in range(count)]
        copies = block_copies(block_ref, buf, block_sem, owners, my_row, rows, height, packed)
        total_copies = [pltpu.make_async_copy(total_ref, total_buf, total_sem.at[0])]
        if has_next:
            total_copies.append(pltpu.make_async_copy(next_total_ref, next_buf, total_sem.at[1]))
        panel_copies = []
        for k in range(2 if has_next else 1):
            for t in range(rows):
                for p in range(2):
                    panel_copies.append(
                        pltpu.make_async_copy(
                            panel_refs[t].at[level + k, p],
                            panel_buf.at[k, pl.ds(t * height, height), pl.ds(p * width, width)],
                            panel_sem.at[k, t, p],
                        )
                    )
        for copy in sum(copies, []) + total_copies + panel_copies:
            copy.start()

        for n in range(count):
            left_buf[:, n * 2 * height : (n + 1) * 2 * height] = slots.left(piece_refs, n, inner)
        for copy in sum(copies, []):
            copy.wait()
        late = mm(left_buf[...], buf[...].reshape(count * 2 * height, local))
        total_copies[0].wait()
        x = -(total_buf[...] + late)
        weight_real = weight_ref[0]
        weight_imag = weight_ref[1]
        term_buf[...] = weight_real * x[width:] + weight_imag * x[:width]
        x_high, x_low = split(x)
        for copy in panel_copies:
            copy.wait()

        def transposed_times(k):
            panel = panel_buf[k]
            product = mm(x_high, panel) + mm(x_low, panel)
            real = product[:width, :width] - product[width:, width:]
            imag = product[:width, width:] + product[width:, :width]
            return real, imag

        own_real, own_imag = transposed_times(0)
        scale = first if level == 0 else 1.0
        y_real = rest_ref[0] * scale - own_real.T
        y_imag = rest_ref[1] * scale - own_imag.T
        diag_buf[...] = weight_real * y_imag + weight_imag * y_real
        if packed:
            for ref, side in ((keep_ref, pole), (send_ref, 1 - pole)):
                begin = pl.multiple_of(side * half, half)
                for t in range(rows):
                    at = my_row ^ t if natural else t
                    ref[at, :half, :] = term_buf[pl.ds(begin, half), t * height : (t + 1) * height]
                    if with_diag:
                        piece_at = pl.multiple_of(begin + (my_row ^ t) * part, part)
                        ref[at, half:, :] = diag_buf[pl.ds(piece_at, part), :]
        else:
            term_out_ref[...] = term_buf[...]
        if not with_diag:
            diag_out_ref[...] = diag_buf[...]
        if has_next:
            parent_high = high_ref[level]
            parent_low = low_ref[level]
            follow_real, follow_imag = transposed_times(1)
            total_copies[1].wait()
            next_out_ref[...] = next_buf[...] + (
                mm(parent_high, x_high) + mm(parent_high, x_low) + mm(parent_low, x_high)
            )
            y_high, y_low = split(jnp.concatenate([y_real, y_imag], axis=1))
            mixed = mm_t(y_high, parent_high) + mm_t(y_low, parent_high) + mm_t(y_high, parent_low)
            z = -jnp.concatenate(
                [follow_real + mixed[:, :width], follow_imag + mixed[:, width:]], axis=0
            )
            z_high, z_low = split(z)
            back = mm(parent_high, z_high) + mm(parent_high, z_low) + mm(parent_low, z_high)
            next_rest_ref[0] = next_diag_ref[0] * first - back[:width]
            next_rest_ref[1] = next_diag_ref[1] * first - back[width:]

    operands = [place, weights] + slots.operands + [blocks] + panels + [total, rest]
    specs = [SCALARS, SCALARS] + [WHOLE] * len(slots.operands)
    specs += [ANYWHERE] * (1 + rows) + [ANYWHERE, WHOLE]
    outs = []
    if has_next:
        operands += [next_total] + list(parents) + [next_diag]
        specs += [ANYWHERE] + [WHOLE] * 3
        outs += [
            jax.ShapeDtypeStruct((2 * width, local), F32),
            jax.ShapeDtypeStruct((2, width, width), F32),
        ]
    if packed:
        held = half + part if with_diag else half
        outs += [jax.ShapeDtypeStruct((rows, held, height), F32)] * 2
    else:
        outs += [jax.ShapeDtypeStruct((width, local), F32)]
    if not with_diag:
        outs += [jax.ShapeDtypeStruct((width, width), F32)]
    wide = 2 * width
    small = 8
    flops = 2 * wide * local * (2 * height * count + 2 * wide * (2 if has_next else 1))
    return pl.pallas_call(
        kernel,
        out_shape=outs,
        in_specs=specs,
        out_specs=[WHOLE] * len(outs),
        scratch_shapes=[
            pltpu.VMEM((count, 2, height, local), BF16),
            pltpu.VMEM((wide, count * 2 * height), BF16),
            pltpu.VMEM((2 if has_next else 1, local, wide), BF16),
            pltpu.VMEM((wide, local), F32),
            pltpu.VMEM((wide, local) if has_next else (small, 128), F32),
            pltpu.VMEM((width, local), F32),
            pltpu.VMEM((width, width), F32),
            pltpu.SemaphoreType.DMA((count, rows)),
            pltpu.SemaphoreType.DMA((2, rows, 2)),
            pltpu.SemaphoreType.DMA((2,)),
        ],
        compiler_params=params(),
        cost_estimate=pl.CostEstimate(flops=flops, bytes_accessed=12 << 20, transcendentals=0),
        name="level_%d" % level,
    )(*operands)


def gather_four(piece, me, axis):
    inner = (me == 1) | (me == 2)
    near = lax.ppermute(piece, axis, [(0, 1), (1, 0), (2, 3), (3, 2)])
    middle = lax.ppermute(jnp.stack([piece, near]), axis, [(1, 2), (2, 1)])
    outer = lax.ppermute(middle, axis, [(1, 0), (2, 3)])
    owners = [
        me,
        me ^ 1,
        jnp.where(inner, 3 - me, me ^ 2),
        jnp.where(inner, (3 - me) ^ 1, me ^ 3),
    ]
    far = [[(middle, n), (outer, n)] for n in range(2)]
    return owners, [[(piece, None)], [(near, None)]], far


def gather_line(piece, me, count, axis):
    owners, slots = [me], [[(piece, None)]]
    from_left = from_right = piece
    for step in range(1, count):
        from_left = lax.ppermute(from_left, axis, [(i, i + 1) for i in range(step - 1, count - 1)])
        from_right = lax.ppermute(from_right, axis, [(i, i - 1) for i in range(1, count - step + 1)])
        if 2 * step >= count:
            owners.append(jnp.clip(jnp.where(me >= step, me - step, me + step), 0, count - 1))
            slots.append([(jnp.where(me >= step, from_left, from_right), None)])
        else:
            owners += [jnp.maximum(me - step, 0), jnp.minimum(me + step, count - 1)]
            slots += [[(from_left, None)], [(from_right, None)]]
    return owners, slots[:1], slots[1:]


def gather(piece, me, count, axis):
    if count == 4:
        return gather_four(piece, me, axis)
    return gather_line(piece, me, count, axis)


def make_per_device(sizes):
    poles, rows, cols = sizes

    def per_device(inverse_block, panels, panel_mask, parent_panels, diag_inverse, pole_weights):
        levels = panels.shape[1]
        height = panels.shape[5]
        width = panels.shape[6]
        half = width // 2
        part = half // rows
        packed = (
            poles == 2
            and rows & (rows - 1) == 0
            and cols & (cols - 1) == 0
            and height == width
            and height % 128 == 0
            and part % 8 == 0
        )
        my_pole = lax.axis_index("pole")
        my_row = lax.axis_index("row")
        my_col = lax.axis_index("col")
        first = ((my_row == 0) & (my_col == 0)).astype(jnp.int32)
        inner = ((my_col == 1) | (my_col == 2)).astype(jnp.int32)
        blocks = inverse_block[0, :, :, 0]
        local_panels = panels[0, :, :, 0, 0]
        flags = panel_mask[:, 0, 0]
        weights = pole_weights[0]
        flipped = (2, width, height)

        def masked(which, keep):
            outs = [jax.ShapeDtypeStruct(flipped, BF16)] * len(which)
            if keep:
                outs.append(jax.ShapeDtypeStruct(local_panels.shape, BF16))
            return pl.pallas_call(
                functools.partial(mask_kernel, which, keep),
                out_shape=outs,
                in_specs=[SCALARS, ANYWHERE],
                out_specs=[WHOLE] * len(outs),
                scratch_shapes=[
                    pltpu.VMEM((levels if keep else len(which),) + local_panels.shape[1:], BF16),
                    pltpu.SemaphoreType.DMA,
                ],
                compiler_params=params(),
                name="mask_rows" if keep else "mask",
            )(flags, local_panels)

        pieces = list(masked([0], False))
        *more, kept = masked(list(range(1, levels)), True)
        pieces += more
        parents = pl.pallas_call(
            parent_kernel,
            out_shape=[jax.ShapeDtypeStruct((levels - 1, 2 * width, 2 * width), BF16)] * 2,
            in_specs=[WHOLE],
            out_specs=[WHOLE] * 2,
            compiler_params=params(),
            name="parents",
        )(parent_panels[0])
        gathered = [gather(piece, my_col, cols, "col") for piece in pieces]
        if packed:
            row_panels = [kept] + [exchange(kept, "row", rows, t) for t in range(1, rows)]
        else:
            row_panels = list(lax.all_gather(kept, "row"))

        def sum_rows(stack):
            return tree_sum([stack[0]] + [exchange(stack[t], "row", rows, t) for t in range(1, rows)])

        def spread(piece):
            whole = tree_sum([piece] + [exchange(piece, "col", cols, t) for t in range(1, cols)])
            whole = jnp.stack([whole] + [exchange(whole, "row", rows, t) for t in range(1, rows)])
            whole = xor_order(whole, my_row, rows)
            other = exchange(whole, "pole", 2, 1)
            return xor_order(jnp.stack([whole, other]), my_pole, 2)

        owners, early_slots, _ = gathered[0]
        early = len(early_slots)
        place = jnp.stack(
            [jnp.asarray(v, jnp.int32) for v in [inner, my_row, my_pole, first] + owners]
        )
        totals = list(
            early_products(rows, width, height, packed, place, [g[1] for g in gathered], blocks)
        )
        everyone = ("pole", "row", "col")
        devices = poles * rows * cols
        rest = diag_inverse[0, 0]
        panel_parts = []
        diag_parts = []
        waiting = []
        for level in range(levels):
            has_next = level + 1 < levels
            natural = packed and not has_next and width % (8 * devices) == 0
            outs = level_products(
                rows,
                width,
                height,
                packed,
                natural,
                level,
                early,
                place,
                weights,
                gathered[level][2],
                blocks,
                row_panels,
                totals[level],
                rest,
                totals[level + 1] if has_next else None,
                parents,
                diag_inverse[0, level + 1] if has_next else None,
            )
            if has_next:
                totals[level + 1] = outs[0]
                rest = outs[1]
                outs = outs[2:]
            if natural:
                term = outs[2].reshape(devices, width // devices, width)
                term = lax.all_to_all(term, everyone, 0, 0, tiled=True)
                term = jnp.sum(term, axis=0, keepdims=True)
                term = jnp.broadcast_to(term, (devices,) + term.shape[1:])
                term = lax.all_to_all(term, everyone, 0, 0, tiled=True)
                diag_parts.append(term.reshape(width, width))
                mine = outs[0] + exchange(outs[1], "pole", 2, 1)
                mine = lax.all_to_all(mine, "row", 0, 0, tiled=True)
                panel_parts.append(jnp.sum(mine, axis=0).T)
            elif packed:
                mine = sum_rows(outs[0] + exchange(outs[1], "pole", 2, 1))
                panel_parts.append(mine[:half].T)
                waiting.append(mine[half:])
                if level >= levels - 2:
                    got = spread(jnp.stack(waiting))
                    for n in range(len(waiting)):
                        diag_parts.append(got[:, :, n].reshape(width, width))
                    waiting = []
            else:
                mine = lax.psum_scatter(outs[0], "row", scatter_dimension=1, tiled=True)
                mine = lax.psum_scatter(mine, "pole", scatter_dimension=0, tiled=True)
                panel_parts.append(mine.T)
                diag_parts.append(lax.psum(outs[1], everyone))
        return jnp.stack(panel_parts)[:, None, None], jnp.stack(diag_parts)

    return per_device


def solution(mesh):
    placed = (
        P("pole", None, None, "row", None, "col"),
        P("pole", None, None, "col", "row", None, None),
        P(None, "col", "row"),
        P("pole", None, None, None, None),
        P("pole", None, None, None, None),
        P("pole", None),
    )
    return jax.shard_map(
        make_per_device((mesh.shape["pole"], mesh.shape["row"], mesh.shape["col"])),
        mesh=mesh,
        in_specs=placed,
        out_specs=(P(None, "col", "row", None, "pole"), P()),
        check_vma=False,
    )
```

```python
import functools

import jax
import jax.numpy as jnp
from jax import lax
from jax.experimental import pallas as pl
from jax.experimental.pallas import tpu as pltpu
from jax.sharding import PartitionSpec as P

F32 = jnp.float32
BF16 = jnp.bfloat16
WHOLE = pl.BlockSpec(memory_space=pltpu.VMEM)
SCALARS = pl.BlockSpec(memory_space=pltpu.SMEM)
ANYWHERE = pl.BlockSpec(memory_space=pl.ANY)
FAR = pl.BlockSpec(memory_space=pltpu.HBM)


def params(mebibytes):
    return pltpu.CompilerParams(vmem_limit_bytes=mebibytes << 20)


def small_cost():
    return pl.CostEstimate(flops=1, bytes_accessed=1, transcendentals=0)


def mm(left, right):
    return jnp.dot(left, right, preferred_element_type=F32)


def mm_t(left, right):
    return lax.dot_general(left, right, (((1,), (1,)), ((), ())), preferred_element_type=F32)


def split(value):
    high = value.astype(BF16)
    return high, (value - high.astype(F32)).astype(BF16)


def exchange(value, axes, count, distance):
    return lax.ppermute(value, axes, [(i, i ^ distance) for i in range(count)])


def tree_sum(values):
    while len(values) > 1:
        values = [values[i] + values[i + 1] for i in range(0, len(values), 2)]
    return values[0]


def xor_order(stack, me, count):
    bits = count.bit_length() - 1
    rest = stack.shape[1:]
    values = stack.reshape((2,) * bits + rest)
    for axis in range(bits):
        bit = (me >> (bits - 1 - axis)) & 1
        values = jnp.where(bit == 1, jnp.flip(values, axis), values)
    return values.reshape((count,) + rest)


def mask_kernel(levels, keep, flag_ref, panel_ref, *refs):
    refs = list(refs)
    if keep:
        refs.pop(0)
    out_refs = [refs.pop(0) for _ in levels]
    kept_ref = refs.pop(0) if keep else None
    buf, flags, sems = refs
    first = 0 if keep else levels[0]
    copies = [
        pltpu.make_async_copy(panel_ref.at[pl.ds(first, buf.shape[0])], buf, sems.at[0]),
        pltpu.make_async_copy(flag_ref, flags, sems.at[1]),
    ]
    for copy in copies:
        copy.start()
    for copy in copies:
        copy.wait()
    for k in range(buf.shape[0]):
        flag = flags[first + k].astype(F32)
        for part in range(2):
            value = buf[k, part].astype(F32) * flag
            if keep:
                kept_ref[k, part] = value.astype(BF16)
            if first + k in levels:
                out_refs[levels.index(first + k)][part] = value.T.astype(BF16)


def parent_kernel(parent_ref, out_ref):
    for k in range(parent_ref.shape[0]):
        real_high, real_low = split(parent_ref[k, 0].T)
        imag_high, imag_low = split(parent_ref[k, 1].T)
        high = left_block(real_high, imag_high)
        wide = high.shape[1]
        out_ref[k, :, :wide] = high
        out_ref[k, :, wide : 2 * wide] = high
        out_ref[k, :, 2 * wide :] = left_block(real_low, imag_low)


def left_block(real, imag):
    return jnp.concatenate(
        [jnp.concatenate([real, -imag], axis=1), jnp.concatenate([imag, real], axis=1)], axis=0
    )


class Slots:
    def __init__(self, slots):
        self.operands = []
        self.slots = []
        for slot in slots:
            self.slots.append([(self.place(array), index) for array, index in slot])

    def place(self, array):
        for n, operand in enumerate(self.operands):
            if operand is array:
                return n
        self.operands.append(array)
        return len(self.operands) - 1

    def left(self, refs, n, inner):
        parts = []
        for part in range(2):
            values = [
                refs[at][part] if index is None else refs[at][index, part]
                for at, index in self.slots[n]
            ]
            parts.append(values[0] if len(values) == 1 else jnp.where(inner == 1, *values))
        return left_block(*parts)


def block_copies(block_ref, buf, sem, owners, my_row, rows, height, ordered):
    copies = []
    for n, owner in enumerate(owners):
        if not ordered:
            copies.append([pltpu.make_async_copy(block_ref.at[:, owner], buf.at[n], sem.at[n, 0])])
            continue
        copies.append(
            [
                pltpu.make_async_copy(
                    block_ref.at[
                        :, owner, :, pl.ds(pl.multiple_of((my_row ^ t) * height, height), height)
                    ],
                    buf.at[n, :, :, pl.ds(t * height, height)],
                    sem.at[n, t],
                )
                for t in range(rows)
            ]
        )
    return copies


def early_products(rows, width, height, ordered, place, level_slots, blocks):
    levels = len(level_slots)
    count = len(level_slots[0])
    slots = Slots([slot for level in level_slots for slot in level])
    local = rows * height

    def kernel(place_ref, block_ref, *refs):
        piece_refs = refs[: len(slots.operands)]
        out_refs = refs[len(slots.operands) :][:levels]
        buf, left_buf, sem = refs[-3:]
        owners = [place_ref[4 + n] for n in range(count)]
        copies = block_copies(block_ref, buf, sem, owners, place_ref[1], rows, height, ordered)
        for group in copies:
            for copy in group:
                copy.start()
        for level in range(levels):
            for n in range(count):
                left_buf[
                    level * 2 * width : (level + 1) * 2 * width,
                    n * 2 * height : (n + 1) * 2 * height,
                ] = slots.left(piece_refs, level * count + n, place_ref[0])
        for group in copies:
            for copy in group:
                copy.wait()
        right = buf[...].reshape(count * 2 * height, local)
        for level in range(levels):
            left = left_buf[level * 2 * width : (level + 1) * 2 * width, :]
            out_refs[level][...] = mm(left, right)

    return pl.pallas_call(
        kernel,
        out_shape=[jax.ShapeDtypeStruct((2 * width, local), F32)] * levels,
        in_specs=[SCALARS, ANYWHERE] + [WHOLE] * len(slots.operands),
        out_specs=[WHOLE] * levels,
        scratch_shapes=[
            pltpu.VMEM((count, 2, height, local), BF16),
            pltpu.VMEM((levels * 2 * width, count * 2 * height), BF16),
            pltpu.SemaphoreType.DMA((count, rows)),
        ],
        compiler_params=params(24),
        cost_estimate=small_cost(),
        name="early",
    )(place, blocks, *slots.operands)


def level_products(
    rows, width, height, packed, level, early, place, weights, level_slots, blocks, panels,
    total, rest, next_total, parents, next_diag, after,
):
    count = len(level_slots)
    slots = Slots(level_slots)
    has_next = next_total is not None
    chunks = rows if packed else 1
    chunk = height if packed else rows * height
    local = rows * height
    half = width // 2
    part = half // rows
    wide = 2 * width
    kinds = 2 if has_next else 1

    def kernel(*refs):
        refs = list(refs)

        def take(n):
            return [refs.pop(0) for _ in range(n)]

        place_ref, weight_ref = take(2)
        piece_refs = take(len(slots.operands))
        (block_ref,) = take(1)
        panel_refs = take(rows)
        total_ref, rest_ref = take(2)
        if has_next:
            next_total_ref, parent_ref, next_diag_ref = take(3)
        take(len(after))
        if has_next:
            next_out_ref, next_rest_ref = take(2)
        out_refs = take(2)
        buf, left_buf, panel_buf, sums, diag_buf, block_sem, panel_sem = take(7)
        assert not refs

        inner, my_row, pole = place_ref[0], place_ref[1], place_ref[2]
        first = place_ref[3].astype(F32)
        weight_real = weight_ref[0]
        weight_imag = weight_ref[1]

        def block_copy(n, t):
            owner = place_ref[4 + early + n]
            if not packed:
                return pltpu.make_async_copy(
                    block_ref.at[:, owner], buf.at[t, n], block_sem.at[n, t]
                )
            start = pl.multiple_of((my_row ^ t) * height, height)
            return pltpu.make_async_copy(
                block_ref.at[:, owner, :, pl.ds(start, height)], buf.at[t, n], block_sem.at[n, t]
            )

        def panel_copies(t):
            copies = []
            for k in range(kinds):
                for r in [t] if packed else range(rows):
                    for p in range(2):
                        copies.append(
                            pltpu.make_async_copy(
                                panel_refs[r].at[level + k, p],
                                panel_buf.at[
                                    t, pl.ds(0 if packed else r * height, height),
                                    pl.ds(k * wide + p * width, width),
                                ],
                                panel_sem.at[k, r, p],
                            )
                        )
            return copies

        for t in range(chunks):
            for n in range(count):
                block_copy(n, t).start()
            for copy in panel_copies(t):
                copy.start()
        for n in range(count):
            left_buf[:, n * 2 * height : (n + 1) * 2 * height] = slots.left(piece_refs, n, inner)
        for t in range(chunks):
            for copy in panel_copies(t):
                copy.wait()

        def step(t, _):
            for n in range(count):
                block_copy(n, t).wait()
            columns = pl.ds(pl.multiple_of(t * chunk, chunk), chunk)
            late = mm(left_buf[...], buf[t].reshape(count * 2 * height, chunk))
            x = -(total_ref[:, columns] + late)
            term = weight_real * x[width:] + weight_imag * x[:width]
            if packed:
                low, upper = term[:half], term[half:]
                out_refs[0][t, :half, :] = jnp.where(pole == 0, low, upper)
                out_refs[1][t, :half, :] = jnp.where(pole == 0, upper, low)
            else:
                out_refs[0][:, columns] = term
            x_high, x_low = split(x)
            both = mm(jnp.concatenate([x_high, x_low], axis=0), panel_buf[t])
            both = both[:wide] + both[wide:]
            sums[...] = jnp.where(t == 0, both, sums[...] + both)
            if has_next:
                stacked = jnp.concatenate([x_high, x_low, x_high], axis=0)
                next_out_ref[:, columns] = next_total_ref[:, columns] + mm(
                    parent_ref[level], stacked
                )
            return 0

        lax.fori_loop(0, chunks, step, 0)

        def complex_sum(k):
            at = k * wide
            real = sums[:width, at : at + width] - sums[width:, at + width : at + wide]
            imag = sums[:width, at + width : at + wide] + sums[width:, at : at + width]
            return real, imag

        own_real, own_imag = complex_sum(0)
        scale = first if level == 0 else 1.0
        y_real = rest_ref[0] * scale - own_real.T
        y_imag = rest_ref[1] * scale - own_imag.T
        diag_buf[...] = weight_real * y_imag + weight_imag * y_real
        if packed:
            for ref, side in ((out_refs[0], pole), (out_refs[1], 1 - pole)):
                for t in range(rows):
                    at = pl.multiple_of(side * half + (my_row ^ t) * part, part)
                    ref[t, half:, :] = diag_buf[pl.ds(at, part), :]
        else:
            out_refs[1][...] = diag_buf[...]
        if has_next:
            parent = parent_ref[level]
            parent_high, parent_low = parent[:, :wide], parent[:, 2 * wide :]
            follow_real, follow_imag = complex_sum(1)
            y_high, y_low = split(jnp.concatenate([y_real, y_imag], axis=1))
            mixed = mm_t(y_high, parent_high) + mm_t(y_low, parent_high) + mm_t(y_high, parent_low)
            z = -jnp.concatenate(
                [follow_real + mixed[:, :width], follow_imag + mixed[:, width:]], axis=0
            )
            z_high, z_low = split(z)
            back = mm(parent, jnp.concatenate([z_high, z_low, z_high], axis=0))
            next_rest_ref[0] = next_diag_ref[0] * first - back[:width]
            next_rest_ref[1] = next_diag_ref[1] * first - back[width:]

    operands = [place, weights] + slots.operands + [blocks] + panels + [total, rest]
    specs = [SCALARS, SCALARS] + [WHOLE] * len(slots.operands)
    specs += [ANYWHERE] * (1 + rows) + [WHOLE] * 2
    outs = []
    aliases = {}
    if has_next:
        aliases = {len(operands): 0}
        operands += [next_total, parents, next_diag]
        specs += [WHOLE] * 3
        outs += [
            jax.ShapeDtypeStruct((wide, local), F32),
            jax.ShapeDtypeStruct((2, width, width), F32),
        ]
    operands += after
    specs += [ANYWHERE] * len(after)
    if packed:
        outs += [jax.ShapeDtypeStruct((rows, half + part, height), F32)] * 2
    else:
        outs += [
            jax.ShapeDtypeStruct((width, local), F32),
            jax.ShapeDtypeStruct((width, width), F32),
        ]
    return pl.pallas_call(
        kernel,
        out_shape=outs,
        in_specs=specs,
        out_specs=[WHOLE] * len(outs),
        input_output_aliases=aliases,
        scratch_shapes=[
            pltpu.VMEM((chunks, count, 2, height, chunk), BF16),
            pltpu.VMEM((wide, count * 2 * height), BF16),
            pltpu.VMEM((chunks, chunk, kinds * wide), BF16),
            pltpu.VMEM((wide, kinds * wide), F32),
            pltpu.VMEM((width, width), F32),
            pltpu.SemaphoreType.DMA((count, chunks)),
            pltpu.SemaphoreType.DMA((2, rows, 2)),
        ],
        compiler_params=params(28),
        cost_estimate=pl.CostEstimate(flops=1, bytes_accessed=8 << 20, transcendentals=0),
        name="level_%d" % level,
    )(*operands)


def gather_four(piece, me, axis, singly):
    inner = (me == 1) | (me == 2)
    pairs = [(0, 1), (1, 0), (2, 3), (3, 2)]
    middle_pairs = [(1, 2), (2, 1)]
    outer_pairs = [(1, 0), (2, 3)]
    owners = [
        me,
        me ^ 1,
        jnp.where(inner, 3 - me, me ^ 2),
        jnp.where(inner, (3 - me) ^ 1, me ^ 3),
    ]
    near = lax.ppermute(piece, axis, pairs)
    if singly:
        middles = [lax.ppermute(value, axis, middle_pairs) for value in (piece, near)]
        far = [[(m, None), (lax.ppermute(m, axis, outer_pairs), None)] for m in middles]
    else:
        middle = lax.ppermute(jnp.stack([piece, near]), axis, middle_pairs)
        outer = lax.ppermute(middle, axis, outer_pairs)
        far = [[(middle, n), (outer, n)] for n in range(2)]
    return owners, [[(piece, None)], [(near, None)]], far


def gather_line(piece, me, count, axis):
    owners, slots = [me], [[(piece, None)]]
    from_left = from_right = piece
    for step in range(1, count):
        from_left = lax.ppermute(from_left, axis, [(i, i + 1) for i in range(step - 1, count - 1)])
        from_right = lax.ppermute(from_right, axis, [(i, i - 1) for i in range(1, count - step + 1)])
        if 2 * step >= count:
            owners.append(jnp.clip(jnp.where(me >= step, me - step, me + step), 0, count - 1))
            slots.append([(jnp.where(me >= step, from_left, from_right), None)])
        else:
            owners += [jnp.maximum(me - step, 0), jnp.minimum(me + step, count - 1)]
            slots += [[(from_left, None)], [(from_right, None)]]
    return owners, slots[:1], slots[1:]


def gather(piece, me, count, axis, singly):
    if count == 4:
        return gather_four(piece, me, axis, singly)
    return gather_line(piece, me, count, axis)


def make_per_device(sizes):
    poles, rows, cols = sizes

    def per_device(inverse_block, panels, panel_mask, parent_panels, diag_inverse, pole_weights):
        levels = panels.shape[1]
        height = panels.shape[5]
        width = panels.shape[6]
        half = width // 2
        part = half // rows
        packed = (
            poles == 2
            and rows & (rows - 1) == 0
            and cols & (cols - 1) == 0
            and height == width
            and height % 128 == 0
            and part % 8 == 0
        )
        my_pole = lax.axis_index("pole")
        my_row = lax.axis_index("row")
        my_col = lax.axis_index("col")
        first = ((my_row == 0) & (my_col == 0)).astype(jnp.int32)
        inner = ((my_col == 1) | (my_col == 2)).astype(jnp.int32)
        blocks = inverse_block[0, :, :, 0]
        local_panels = panels[0, :, :, 0, 0]
        flags = panel_mask[:, 0, 0]
        weights = pole_weights[0]
        flipped = (2, width, height)

        def masked(which, after):
            keep = bool(after)
            outs = [jax.ShapeDtypeStruct(flipped, BF16)] * len(which)
            if keep:
                outs.append(jax.ShapeDtypeStruct(local_panels.shape, BF16))
            return pl.pallas_call(
                functools.partial(mask_kernel, which, keep),
                out_shape=outs,
                in_specs=[FAR, FAR] + [ANYWHERE] * len(after),
                out_specs=[WHOLE] * len(outs),
                scratch_shapes=[
                    pltpu.VMEM((levels if keep else len(which),) + local_panels.shape[1:], BF16),
                    pltpu.SMEM((levels,), jnp.int32),
                    pltpu.SemaphoreType.DMA((2,)),
                ],
                compiler_params=params(8),
                cost_estimate=small_cost(),
                name="mask_rows" if keep else "mask",
            )(flags, local_panels, *after)

        pieces = list(masked([0], []))
        *more, kept = masked(list(range(1, levels)), pieces)
        pieces += more
        parents = pl.pallas_call(
            parent_kernel,
            out_shape=jax.ShapeDtypeStruct((levels - 1, 2 * width, 6 * width), BF16),
            in_specs=[WHOLE],
            out_specs=WHOLE,
            compiler_params=params(12),
            cost_estimate=small_cost(),
            name="parents",
        )(parent_panels[0])
        gathered = [gather(piece, my_col, cols, "col", k == 0) for k, piece in enumerate(pieces)]
        if packed:
            row_panels = [kept] + [exchange(kept, "row", rows, t) for t in range(1, rows)]
        else:
            row_panels = list(lax.all_gather(kept, "row"))

        def sum_rows(stack):
            return tree_sum([stack[0]] + [exchange(stack[t], "row", rows, t) for t in range(1, rows)])

        def spread(piece):
            whole = tree_sum([piece] + [exchange(piece, "col", cols, t) for t in range(1, cols)])
            whole = jnp.stack([whole] + [exchange(whole, "row", rows, t) for t in range(1, rows)])
            whole = xor_order(whole, my_row, rows)
            other = exchange(whole, "pole", 2, 1)
            return xor_order(jnp.stack([whole, other]), my_pole, 2)

        owners, early_slots, _ = gathered[0]
        early = len(early_slots)
        place = jnp.stack(
            [jnp.asarray(v, jnp.int32) for v in [inner, my_row, my_pole, first] + owners]
        )
        totals = list(
            early_products(rows, width, height, packed, place, [g[1] for g in gathered], blocks)
        )
        rest = diag_inverse[0, 0]
        panel_parts = []
        diag_parts = []
        waiting = []
        first_sum = []
        ordered = [g[2][0][0][0] for g in gathered[1:] if len(g[2][0]) == 2]
        for level in range(levels):
            has_next = level + 1 < levels
            outs = level_products(
                rows,
                width,
                height,
                packed,
                level,
                early,
                place,
                weights,
                gathered[level][2],
                blocks,
                row_panels,
                totals[level],
                rest,
                totals[level + 1] if has_next else None,
                parents,
                diag_inverse[0, level + 1] if has_next else None,
                first_sum if level == levels - 1 else ordered if level == 0 else [],
            )
            if has_next:
                totals[level + 1] = outs[0]
                rest = outs[1]
                outs = outs[2:]
            if packed:
                both = outs[0] + exchange(outs[1], "pole", 2, 1)
                if level == 0:
                    first_sum = [both]
                mine = sum_rows(both)
                panel_parts.append(mine[:half].T)
                waiting.append(mine[half:])
                if level >= levels - 2:
                    got = spread(jnp.stack(waiting))
                    for n in range(len(waiting)):
                        diag_parts.append(got[:, :, n].reshape(width, width))
                    waiting = []
            else:
                mine = lax.psum_scatter(outs[0], "row", scatter_dimension=1, tiled=True)
                mine = lax.psum_scatter(mine, "pole", scatter_dimension=0, tiled=True)
                panel_parts.append(mine.T)
                diag_parts.append(lax.psum(outs[1], ("pole", "row", "col")))
        return jnp.stack(panel_parts)[:, None, None], jnp.stack(diag_parts)

    return per_device


def solution(mesh):
    placed = (
        P("pole", None, None, "row", None, "col"),
        P("pole", None, None, "col", "row", None, None),
        P(None, "col", "row"),
        P("pole", None, None, None, None),
        P("pole", None, None, None, None),
        P("pole", None),
    )
    return jax.shard_map(
        make_per_device((mesh.shape["pole"], mesh.shape["row"], mesh.shape["col"])),
        mesh=mesh,
        in_specs=placed,
        out_specs=(P(None, "col", "row", None, "pole"), P()),
        check_vma=False,
    )
```

```python
import functools

import jax
import jax.numpy as jnp
from jax import lax
from jax.experimental import pallas as pl
from jax.experimental.pallas import tpu as pltpu
from jax.sharding import PartitionSpec as P

F32 = jnp.float32
BF16 = jnp.bfloat16
WHOLE = pl.BlockSpec(memory_space=pltpu.VMEM)
SCALARS = pl.BlockSpec(memory_space=pltpu.SMEM)
ANYWHERE = pl.BlockSpec(memory_space=pl.ANY)
FAR = pl.BlockSpec(memory_space=pltpu.HBM)


def params(mebibytes):
    return pltpu.CompilerParams(vmem_limit_bytes=mebibytes << 20)


def small_cost():
    return pl.CostEstimate(flops=1, bytes_accessed=1, transcendentals=0)


def mm(left, right):
    return jnp.dot(left, right, preferred_element_type=F32)


def mm_t(left, right):
    return lax.dot_general(left, right, (((1,), (1,)), ((), ())), preferred_element_type=F32)


def split(value):
    high = value.astype(BF16)
    return high, (value - high.astype(F32)).astype(BF16)


def exchange(value, axes, count, distance):
    return lax.ppermute(value, axes, [(i, i ^ distance) for i in range(count)])


def tree_sum(values):
    while len(values) > 1:
        values = [values[i] + values[i + 1] for i in range(0, len(values), 2)]
    return values[0]


def xor_order(stack, me, count):
    bits = count.bit_length() - 1
    rest = stack.shape[1:]
    values = stack.reshape((2,) * bits + rest)
    for axis in range(bits):
        bit = (me >> (bits - 1 - axis)) & 1
        values = jnp.where(bit == 1, jnp.flip(values, axis), values)
    return values.reshape((count,) + rest)


def mask_kernel(levels, keep, flag_ref, panel_ref, *refs):
    refs = list(refs)
    if keep:
        refs.pop(0)
    out_refs = [refs.pop(0) for _ in levels]
    kept_refs = [refs.pop(0) for _ in range(2)] if keep else None
    buf, flags, sems = refs
    first = 0 if keep else levels[0]
    copies = [
        pltpu.make_async_copy(panel_ref.at[pl.ds(first, buf.shape[0])], buf, sems.at[0]),
        pltpu.make_async_copy(flag_ref, flags, sems.at[1]),
    ]
    for copy in copies:
        copy.start()
    for copy in copies:
        copy.wait()
    for k in range(buf.shape[0]):
        flag = flags[first + k].astype(F32)
        for part in range(2):
            value = buf[k, part].astype(F32) * flag
            if keep:
                kept_refs[part][k] = value.astype(BF16)
            if first + k in levels:
                out_refs[levels.index(first + k)][part] = value.T.astype(BF16)


def parent_kernel(parent_ref, out_ref):
    for k in range(parent_ref.shape[0]):
        real_high, real_low = split(parent_ref[k, 0].T)
        imag_high, imag_low = split(parent_ref[k, 1].T)
        high = left_block(real_high, imag_high)
        wide = high.shape[1]
        out_ref[k, :, :wide] = high
        out_ref[k, :, wide : 2 * wide] = high
        out_ref[k, :, 2 * wide :] = left_block(real_low, imag_low)


def left_block(real, imag):
    return jnp.concatenate(
        [jnp.concatenate([real, -imag], axis=1), jnp.concatenate([imag, real], axis=1)], axis=0
    )


class Slots:
    def __init__(self, slots):
        self.operands = []
        self.slots = []
        for slot in slots:
            self.slots.append([(self.place(array), index) for array, index in slot])

    def place(self, array):
        for n, operand in enumerate(self.operands):
            if operand is array:
                return n
        self.operands.append(array)
        return len(self.operands) - 1

    def left(self, refs, n, inner):
        parts = []
        for part in range(2):
            values = [
                refs[at][part] if index is None else refs[at][index, part]
                for at, index in self.slots[n]
            ]
            parts.append(values[0] if len(values) == 1 else jnp.where(inner == 1, *values))
        return left_block(*parts)


def block_copies(block_ref, buf, sem, owners, my_row, rows, height, ordered):
    copies = []
    for n, owner in enumerate(owners):
        if not ordered:
            copies.append([pltpu.make_async_copy(block_ref.at[:, owner], buf.at[n], sem.at[n, 0])])
            continue
        copies.append(
            [
                pltpu.make_async_copy(
                    block_ref.at[
                        :, owner, :, pl.ds(pl.multiple_of((my_row ^ t) * height, height), height)
                    ],
                    buf.at[n, :, :, pl.ds(t * height, height)],
                    sem.at[n, t],
                )
                for t in range(rows)
            ]
        )
    return copies


def early_products(rows, width, height, ordered, place, level_slots, late, blocks, after):
    levels = len(level_slots)
    count = len(level_slots[0])
    slots = Slots([slot for level in level_slots for slot in level])
    local = rows * height
    chunks = rows if ordered else 1
    chunk = height if ordered else local

    def kernel(place_ref, block_ref, *refs):
        piece_refs = refs[: len(slots.operands)]
        out_refs = refs[len(slots.operands) + len(after) :][:levels]
        late_ref, buf, left_buf, sem, late_sem = refs[-5:]
        my_row = place_ref[1]
        owners = [place_ref[4 + n] for n in range(count)]
        copies = block_copies(block_ref, buf, sem, owners, my_row, rows, height, ordered)
        late_copies = []
        for n in range(late):
            owner = place_ref[4 + count + n]
            for t in range(chunks):
                start = pl.multiple_of((my_row ^ t) * chunk, chunk) if ordered else 0
                late_copies.append(
                    pltpu.make_async_copy(
                        block_ref.at[:, owner, :, pl.ds(start, chunk)],
                        late_ref.at[t, n],
                        late_sem.at[n, t],
                    )
                )
        for copy in sum(copies, []) + late_copies:
            copy.start()
        for level in range(levels):
            for n in range(count):
                left_buf[
                    level * 2 * width : (level + 1) * 2 * width,
                    n * 2 * height : (n + 1) * 2 * height,
                ] = slots.left(piece_refs, level * count + n, place_ref[0])
        for copy in sum(copies, []):
            copy.wait()
        right = buf[...].reshape(count * 2 * height, local)
        for level in range(levels):
            left = left_buf[level * 2 * width : (level + 1) * 2 * width, :]
            out_refs[level][...] = mm(left, right)
        for copy in late_copies:
            copy.wait()

    outs = [jax.ShapeDtypeStruct((2 * width, local), F32)] * levels
    outs.append(jax.ShapeDtypeStruct((chunks, late, 2, height, chunk), BF16))
    return pl.pallas_call(
        kernel,
        out_shape=outs,
        in_specs=[SCALARS, FAR] + [WHOLE] * len(slots.operands) + [ANYWHERE] * len(after),
        out_specs=[WHOLE] * len(outs),
        scratch_shapes=[
            pltpu.VMEM((count, 2, height, local), BF16),
            pltpu.VMEM((levels * 2 * width, count * 2 * height), BF16),
            pltpu.SemaphoreType.DMA((count, rows)),
            pltpu.SemaphoreType.DMA((late, chunks)),
        ],
        compiler_params=params(24),
        cost_estimate=small_cost(),
        name="early",
    )(place, blocks, *slots.operands, *after)


def pack_panels(levels, rows, width, height, packed, reals, imags):
    chunks = rows if packed else 1
    chunk = height if packed else rows * height
    slots = Slots([reals, imags])

    def kernel(*refs):
        panel_refs = refs[: len(slots.operands)]
        out_ref, sem = refs[len(slots.operands) :]
        copies = []
        for p in range(2):
            for r in range(rows):
                at, index = slots.slots[p][r]
                source = panel_refs[at] if index is None else panel_refs[at].at[index]
                target = out_ref.at[
                    :, r if packed else 0,
                    pl.ds(0 if packed else r * height, height),
                    pl.ds(p * width, width),
                ]
                copies.append(pltpu.make_async_copy(source, target, sem.at[r, p]))
        for copy in copies:
            copy.start()
        for copy in copies:
            copy.wait()

    return pl.pallas_call(
        kernel,
        out_shape=jax.ShapeDtypeStruct((levels, chunks, chunk, 2 * width), BF16),
        in_specs=[ANYWHERE] * len(slots.operands),
        out_specs=WHOLE,
        scratch_shapes=[pltpu.SemaphoreType.DMA((rows, 2))],
        compiler_params=params(8),
        cost_estimate=pl.CostEstimate(flops=10**11, bytes_accessed=1, transcendentals=0),
        name="pack_rows",
    )(*slots.operands)


def level_products(
    rows, width, height, packed, level, place, weights, level_slots, blocks, panels,
    total, rest, next_total, parents, next_diag, after,
):
    count = len(level_slots)
    slots = Slots(level_slots)
    has_next = next_total is not None
    chunks = rows if packed else 1
    chunk = height if packed else rows * height
    local = rows * height
    half = width // 2
    part = half // rows
    wide = 2 * width
    kinds = 2 if has_next else 1

    def kernel(*refs):
        refs = list(refs)

        def take(n):
            return [refs.pop(0) for _ in range(n)]

        place_ref, weight_ref = take(2)
        piece_refs = take(len(slots.operands))
        block_ref, panel_ref, total_ref, rest_ref = take(4)
        if has_next:
            next_total_ref, parent_ref, next_diag_ref = take(3)
        take(len(after))
        if has_next:
            next_out_ref, next_rest_ref = take(2)
        out_refs = take(2)
        left_buf, sums, diag_buf = take(3)
        assert not refs

        inner, my_row, pole = place_ref[0], place_ref[1], place_ref[2]
        first = place_ref[3].astype(F32)
        weight_real = weight_ref[0]
        weight_imag = weight_ref[1]

        for n in range(count):
            left_buf[:, n * 2 * height : (n + 1) * 2 * height] = slots.left(piece_refs, n, inner)

        def step(t, _):
            columns = pl.ds(pl.multiple_of(t * chunk, chunk), chunk)
            late = mm(left_buf[...], block_ref[t].reshape(count * 2 * height, chunk))
            x = -(total_ref[:, columns] + late)
            term = weight_real * x[width:] + weight_imag * x[:width]
            if packed:
                low, upper = term[:half], term[half:]
                out_refs[0][t, :half, :] = jnp.where(pole == 0, low, upper)
                out_refs[1][t, :half, :] = jnp.where(pole == 0, upper, low)
            else:
                out_refs[0][:, columns] = term
            x_high, x_low = split(x)
            x_both = jnp.concatenate([x_high, x_low], axis=0)
            for k in range(kinds):
                both = mm(x_both, panel_ref[level + k, t])
                sums[:, k * wide : (k + 1) * wide] += both[:wide] + both[wide:]
            if has_next:
                stacked = jnp.concatenate([x_high, x_low, x_high], axis=0)
                next_out_ref[:, columns] = next_total_ref[:, columns] + mm(
                    parent_ref[level], stacked
                )
            return 0

        sums[...] = jnp.zeros_like(sums)
        lax.fori_loop(0, chunks, step, 0)

        def complex_sum(k):
            at = k * wide
            real = sums[:width, at : at + width] - sums[width:, at + width : at + wide]
            imag = sums[:width, at + width : at + wide] + sums[width:, at : at + width]
            return real, imag

        own_real, own_imag = complex_sum(0)
        scale = first if level == 0 else 1.0
        y_real = rest_ref[0] * scale - own_real.T
        y_imag = rest_ref[1] * scale - own_imag.T
        diag_buf[...] = weight_real * y_imag + weight_imag * y_real
        if packed:
            for ref, side in ((out_refs[0], pole), (out_refs[1], 1 - pole)):
                for t in range(rows):
                    at = pl.multiple_of(side * half + (my_row ^ t) * part, part)
                    ref[t, half:, :] = diag_buf[pl.ds(at, part), :]
        else:
            out_refs[1][...] = diag_buf[...]
        if has_next:
            parent = parent_ref[level]
            parent_high, parent_low = parent[:, :wide], parent[:, 2 * wide :]
            follow_real, follow_imag = complex_sum(1)
            y_high, y_low = split(jnp.concatenate([y_real, y_imag], axis=1))
            mixed = mm_t(y_high, parent_high) + mm_t(y_low, parent_high) + mm_t(y_high, parent_low)
            z = -jnp.concatenate(
                [follow_real + mixed[:, :width], follow_imag + mixed[:, width:]], axis=0
            )
            z_high, z_low = split(z)
            back = mm(parent, jnp.concatenate([z_high, z_low, z_high], axis=0))
            next_rest_ref[0] = next_diag_ref[0] * first - back[:width]
            next_rest_ref[1] = next_diag_ref[1] * first - back[width:]

    operands = [place, weights] + slots.operands + [blocks, panels, total, rest]
    specs = [SCALARS, SCALARS] + [WHOLE] * (len(slots.operands) + 4)
    outs = []
    aliases = {}
    if has_next:
        aliases = {len(operands): 0}
        operands += [next_total, parents, next_diag]
        specs += [WHOLE] * 3
        outs += [
            jax.ShapeDtypeStruct((wide, local), F32),
            jax.ShapeDtypeStruct((2, width, width), F32),
        ]
    operands += after
    specs += [ANYWHERE] * len(after)
    if packed:
        outs += [jax.ShapeDtypeStruct((rows, half + part, height), F32)] * 2
    else:
        outs += [
            jax.ShapeDtypeStruct((width, local), F32),
            jax.ShapeDtypeStruct((width, width), F32),
        ]
    return pl.pallas_call(
        kernel,
        out_shape=outs,
        in_specs=specs,
        out_specs=[WHOLE] * len(outs),
        input_output_aliases=aliases,
        scratch_shapes=[
            pltpu.VMEM((wide, count * 2 * height), BF16),
            pltpu.VMEM((wide, kinds * wide), F32),
            pltpu.VMEM((width, width), F32),
        ],
        compiler_params=params(16),
        cost_estimate=pl.CostEstimate(flops=10**11, bytes_accessed=1, transcendentals=0),
        name="level_%d" % level,
    )(*operands)


def gather_four(piece, me, axis, singly):
    inner = (me == 1) | (me == 2)
    pairs = [(0, 1), (1, 0), (2, 3), (3, 2)]
    middle_pairs = [(1, 2), (2, 1)]
    outer_pairs = [(1, 0), (2, 3)]
    owners = [
        me,
        me ^ 1,
        jnp.where(inner, 3 - me, me ^ 2),
        jnp.where(inner, (3 - me) ^ 1, me ^ 3),
    ]
    near = lax.ppermute(piece, axis, pairs)
    if singly:
        middles = [lax.ppermute(value, axis, middle_pairs) for value in (piece, near)]
        far = [[(m, None), (lax.ppermute(m, axis, outer_pairs), None)] for m in middles]
    else:
        middle = lax.ppermute(jnp.stack([piece, near]), axis, middle_pairs)
        outer = lax.ppermute(middle, axis, outer_pairs)
        far = [[(middle, n), (outer, n)] for n in range(2)]
    return owners, [[(piece, None)], [(near, None)]], far


def gather_line(piece, me, count, axis):
    owners, slots = [me], [[(piece, None)]]
    from_left = from_right = piece
    for step in range(1, count):
        from_left = lax.ppermute(from_left, axis, [(i, i + 1) for i in range(step - 1, count - 1)])
        from_right = lax.ppermute(from_right, axis, [(i, i - 1) for i in range(1, count - step + 1)])
        if 2 * step >= count:
            owners.append(jnp.clip(jnp.where(me >= step, me - step, me + step), 0, count - 1))
            slots.append([(jnp.where(me >= step, from_left, from_right), None)])
        else:
            owners += [jnp.maximum(me - step, 0), jnp.minimum(me + step, count - 1)]
            slots += [[(from_left, None)], [(from_right, None)]]
    return owners, slots[:1], slots[1:]


def gather_rows(value, near, far):
    first = exchange(value, "row", 4, near)
    second = exchange(jnp.stack([value, first]), "row", 4, far)
    found = {0: (value, None), near: (first, None), far: (second, 0), 3: (second, 1)}
    return [found[t] for t in range(4)]


def gather(piece, me, count, axis, singly):
    if count == 4:
        return gather_four(piece, me, axis, singly)
    return gather_line(piece, me, count, axis)


def make_per_device(sizes):
    poles, rows, cols = sizes

    def per_device(inverse_block, panels, panel_mask, parent_panels, diag_inverse, pole_weights):
        levels = panels.shape[1]
        height = panels.shape[5]
        width = panels.shape[6]
        half = width // 2
        part = half // rows
        packed = (
            poles == 2
            and rows & (rows - 1) == 0
            and cols & (cols - 1) == 0
            and height == width
            and height % 128 == 0
            and part % 8 == 0
        )
        my_pole = lax.axis_index("pole")
        my_row = lax.axis_index("row")
        my_col = lax.axis_index("col")
        first = ((my_row == 0) & (my_col == 0)).astype(jnp.int32)
        inner = ((my_col == 1) | (my_col == 2)).astype(jnp.int32)
        blocks = inverse_block[0, :, :, 0]
        local_panels = panels[0, :, :, 0, 0]
        flags = panel_mask[:, 0, 0]
        weights = pole_weights[0]
        flipped = (2, width, height)

        def masked(which, after):
            keep = bool(after)
            outs = [jax.ShapeDtypeStruct(flipped, BF16)] * len(which)
            if keep:
                outs += [jax.ShapeDtypeStruct((levels, height, width), BF16)] * 2
            return pl.pallas_call(
                functools.partial(mask_kernel, which, keep),
                out_shape=outs,
                in_specs=[FAR, FAR] + [ANYWHERE] * len(after),
                out_specs=[WHOLE] * len(outs),
                scratch_shapes=[
                    pltpu.VMEM((levels if keep else len(which),) + local_panels.shape[1:], BF16),
                    pltpu.SMEM((levels,), jnp.int32),
                    pltpu.SemaphoreType.DMA((2,)),
                ],
                compiler_params=params(8),
                cost_estimate=small_cost(),
                name="mask_rows" if keep else "mask",
            )(flags, local_panels, *after)

        pieces = list(masked([0], []))
        *more, kept_real, kept_imag = masked(list(range(1, levels)), pieces)
        pieces += more
        parents = pl.pallas_call(
            parent_kernel,
            out_shape=jax.ShapeDtypeStruct((levels - 1, 2 * width, 6 * width), BF16),
            in_specs=[WHOLE],
            out_specs=WHOLE,
            compiler_params=params(12),
            cost_estimate=small_cost(),
            name="parents",
        )(parent_panels[0])
        gathered = [gather(piece, my_col, cols, "col", k == 0) for k, piece in enumerate(pieces)]
        if packed and rows == 4:
            reals = gather_rows(kept_real, 1, 2)
            imags = gather_rows(kept_imag, 2, 1)
        elif packed:
            reals, imags = [
                [(value, None)]
                + [(exchange(value, "row", rows, t), None) for t in range(1, rows)]
                for value in (kept_real, kept_imag)
            ]
        else:
            reals, imags = [
                [(piece, None) for piece in lax.all_gather(value, "row")]
                for value in (kept_real, kept_imag)
            ]

        def sum_rows(stack):
            return tree_sum([stack[0]] + [exchange(stack[t], "row", rows, t) for t in range(1, rows)])

        def spread(piece):
            whole = tree_sum([piece] + [exchange(piece, "col", cols, t) for t in range(1, cols)])
            whole = jnp.stack([whole] + [exchange(whole, "row", rows, t) for t in range(1, rows)])
            whole = xor_order(whole, my_row, rows)
            other = exchange(whole, "pole", 2, 1)
            return xor_order(jnp.stack([whole, other]), my_pole, 2)

        owners = gathered[0][0]
        place = jnp.stack(
            [jnp.asarray(v, jnp.int32) for v in [inner, my_row, my_pole, first] + owners]
        )
        late = len(gathered[0][2])
        *totals, late_blocks = early_products(
            rows,
            width,
            height,
            packed,
            place,
            [g[1] for g in gathered],
            late,
            blocks,
            [slot[1][0] for slot in gathered[0][2] if len(slot) == 2],
        )
        row_panels = pack_panels(levels, rows, width, height, packed, reals, imags)
        rest = diag_inverse[0, 0]
        panel_parts = []
        diag_parts = []
        waiting = []
        ordered = [g[2][0][0][0] for g in gathered[1:] if len(g[2][0]) == 2]
        for level in range(levels):
            has_next = level + 1 < levels
            outs = level_products(
                rows,
                width,
                height,
                packed,
                level,
                place,
                weights,
                gathered[level][2],
                late_blocks,
                row_panels,
                totals[level],
                rest,
                totals[level + 1] if has_next else None,
                parents,
                diag_inverse[0, level + 1] if has_next else None,
                ordered if level == 0 else [],
            )
            if has_next:
                totals[level + 1] = outs[0]
                rest = outs[1]
                outs = outs[2:]
            if packed:
                both = outs[0] + exchange(outs[1], "pole", 2, 1)
                mine = sum_rows(both)
                panel_parts.append(mine[:half].T)
                waiting.append(mine[half:])
                if level >= levels - 2:
                    got = spread(jnp.stack(waiting))
                    for n in range(len(waiting)):
                        diag_parts.append(got[:, :, n].reshape(width, width))
                    waiting = []
            else:
                mine = lax.psum_scatter(outs[0], "row", scatter_dimension=1, tiled=True)
                mine = lax.psum_scatter(mine, "pole", scatter_dimension=0, tiled=True)
                panel_parts.append(mine.T)
                diag_parts.append(lax.psum(outs[1], ("pole", "row", "col")))
        return jnp.stack(panel_parts)[:, None, None], jnp.stack(diag_parts)

    return per_device


def solution(mesh):
    placed = (
        P("pole", None, None, "row", None, "col"),
        P("pole", None, None, "col", "row", None, None),
        P(None, "col", "row"),
        P("pole", None, None, None, None),
        P("pole", None, None, None, None),
        P("pole", None),
    )
    return jax.shard_map(
        make_per_device((mesh.shape["pole"], mesh.shape["row"], mesh.shape["col"])),
        mesh=mesh,
        in_specs=placed,
        out_specs=(P(None, "col", "row", None, "pole"), P()),
        check_vma=False,
    )
```

```python
import functools

import jax
import jax.numpy as jnp
from jax import lax
from jax.experimental import pallas as pl
from jax.experimental.pallas import tpu as pltpu
from jax.sharding import PartitionSpec as P

F32 = jnp.float32
BF16 = jnp.bfloat16
WHOLE = pl.BlockSpec(memory_space=pltpu.VMEM)
SCALARS = pl.BlockSpec(memory_space=pltpu.SMEM)
ANYWHERE = pl.BlockSpec(memory_space=pl.ANY)
FAR = pl.BlockSpec(memory_space=pltpu.HBM)


def params(mebibytes):
    return pltpu.CompilerParams(vmem_limit_bytes=mebibytes << 20)


def small_cost():
    return pl.CostEstimate(flops=1, bytes_accessed=1, transcendentals=0)


def large_cost():
    return pl.CostEstimate(flops=10**11, bytes_accessed=1, transcendentals=0)


def mm(left, right):
    return jnp.dot(left, right, preferred_element_type=F32)


def mm_t(left, right):
    return lax.dot_general(left, right, (((1,), (1,)), ((), ())), preferred_element_type=F32)


def split(value):
    high = value.astype(BF16)
    return high, (value - high.astype(F32)).astype(BF16)


def exchange(value, axes, count, distance):
    return lax.ppermute(value, axes, [(i, i ^ distance) for i in range(count)])


def tree_sum(values):
    while len(values) > 1:
        values = [values[i] + values[i + 1] for i in range(0, len(values), 2)]
    return values[0]


def xor_order(stack, me, count):
    bits = count.bit_length() - 1
    rest = stack.shape[1:]
    values = stack.reshape((2,) * bits + rest)
    for axis in range(bits):
        bit = (me >> (bits - 1 - axis)) & 1
        values = jnp.where(bit == 1, jnp.flip(values, axis), values)
    return values.reshape((count,) + rest)


def mask_kernel(levels, keep, flag_ref, panel_ref, *refs):
    refs = list(refs)
    if keep:
        refs.pop(0)
    out_refs = [refs.pop(0) for _ in levels]
    kept_refs = [refs.pop(0) for _ in range(2)] if keep else None
    buf, flags, sems = refs
    first = 0 if keep else levels[0]
    copies = [
        pltpu.make_async_copy(panel_ref.at[pl.ds(first, buf.shape[0])], buf, sems.at[0]),
        pltpu.make_async_copy(flag_ref, flags, sems.at[1]),
    ]
    for copy in copies:
        copy.start()
    for copy in copies:
        copy.wait()
    for k in range(buf.shape[0]):
        flag = flags[first + k].astype(F32)
        for part in range(2):
            value = buf[k, part].astype(F32) * flag
            if keep:
                kept_refs[part][k] = value.astype(BF16)
            if first + k in levels:
                out_refs[levels.index(first + k)][part] = value.T.astype(BF16)


def parent_kernel(parent_ref, out_ref):
    for k in range(parent_ref.shape[0]):
        real_high, real_low = split(parent_ref[k, 0].T)
        imag_high, imag_low = split(parent_ref[k, 1].T)
        high = left_block(real_high, imag_high)
        wide = high.shape[1]
        out_ref[k, :, :wide] = high
        out_ref[k, :, wide : 2 * wide] = high
        out_ref[k, :, 2 * wide :] = left_block(real_low, imag_low)


def left_block(real, imag):
    return jnp.concatenate(
        [jnp.concatenate([real, -imag], axis=1), jnp.concatenate([imag, real], axis=1)], axis=0
    )


class Slots:
    def __init__(self, slots):
        self.operands = []
        self.slots = []
        for slot in slots:
            self.slots.append([(self.place(array), index) for array, index in slot])

    def place(self, array):
        for n, operand in enumerate(self.operands):
            if operand is array:
                return n
        self.operands.append(array)
        return len(self.operands) - 1

    def left(self, refs, n, inner):
        parts = []
        for part in range(2):
            values = [
                refs[at][part] if index is None else refs[at][index, part]
                for at, index in self.slots[n]
            ]
            parts.append(values[0] if len(values) == 1 else jnp.where(inner == 1, *values))
        return left_block(*parts)


def block_copies(block_ref, buf, sem, owners, my_row, rows, height, ordered):
    copies = []
    for n, owner in enumerate(owners):
        if not ordered:
            copies.append([pltpu.make_async_copy(block_ref.at[:, owner], buf.at[n], sem.at[n, 0])])
            continue
        copies.append(
            [
                pltpu.make_async_copy(
                    block_ref.at[
                        :, owner, :, pl.ds(pl.multiple_of((my_row ^ t) * height, height), height)
                    ],
                    buf.at[n, :, :, pl.ds(t * height, height)],
                    sem.at[n, t],
                )
                for t in range(rows)
            ]
        )
    return copies


def early_products(rows, width, height, ordered, place, level_slots, late, blocks, after):
    levels = len(level_slots)
    count = len(level_slots[0])
    slots = Slots([slot for level in level_slots for slot in level])
    local = rows * height
    chunks = rows if ordered else 1
    chunk = height if ordered else local

    def kernel(place_ref, block_ref, *refs):
        piece_refs = refs[: len(slots.operands)]
        out_refs = refs[len(slots.operands) + len(after) :][:levels]
        late_ref, buf, left_buf, sem, late_sem = refs[-5:]
        my_row = place_ref[1]
        owners = [place_ref[4 + n] for n in range(count)]
        copies = block_copies(block_ref, buf, sem, owners, my_row, rows, height, ordered)
        late_copies = []
        for n in range(late):
            owner = place_ref[4 + count + n]
            for t in range(chunks):
                start = pl.multiple_of((my_row ^ t) * chunk, chunk) if ordered else 0
                late_copies.append(
                    pltpu.make_async_copy(
                        block_ref.at[:, owner, :, pl.ds(start, chunk)],
                        late_ref.at[t, n],
                        late_sem.at[n, t],
                    )
                )
        for copy in sum(copies, []) + late_copies:
            copy.start()
        for level in range(levels):
            for n in range(count):
                left_buf[
                    level * 2 * width : (level + 1) * 2 * width,
                    n * 2 * height : (n + 1) * 2 * height,
                ] = slots.left(piece_refs, level * count + n, place_ref[0])
        for copy in sum(copies, []):
            copy.wait()
        right = buf[...].reshape(count * 2 * height, local)
        for level in range(levels):
            left = left_buf[level * 2 * width : (level + 1) * 2 * width, :]
            out_refs[level][...] = mm(left, right)
        for copy in late_copies:
            copy.wait()

    outs = [jax.ShapeDtypeStruct((2 * width, local), F32)] * levels
    outs.append(jax.ShapeDtypeStruct((chunks, late, 2, height, chunk), BF16))
    return pl.pallas_call(
        kernel,
        out_shape=outs,
        in_specs=[SCALARS, FAR] + [WHOLE] * len(slots.operands) + [ANYWHERE] * len(after),
        out_specs=[WHOLE] * len(outs),
        scratch_shapes=[
            pltpu.VMEM((count, 2, height, local), BF16),
            pltpu.VMEM((levels * 2 * width, count * 2 * height), BF16),
            pltpu.SemaphoreType.DMA((count, rows)),
            pltpu.SemaphoreType.DMA((late, chunks)),
        ],
        compiler_params=params(24),
        cost_estimate=small_cost(),
        name="early",
    )(place, blocks, *slots.operands, *after)


def pack_panels(levels, rows, width, height, packed, reals, imags):
    chunks = rows if packed else 1
    chunk = height if packed else rows * height
    slots = Slots([reals, imags])

    def kernel(*refs):
        panel_refs = refs[: len(slots.operands)]
        out_ref, sem = refs[len(slots.operands) :]
        copies = []
        for p in range(2):
            for r in range(rows):
                at, index = slots.slots[p][r]
                source = panel_refs[at] if index is None else panel_refs[at].at[index]
                target = out_ref.at[
                    :, r if packed else 0,
                    pl.ds(0 if packed else r * height, height),
                    pl.ds(p * width, width),
                ]
                copies.append(pltpu.make_async_copy(source, target, sem.at[r, p]))
        for copy in copies:
            copy.start()
        for copy in copies:
            copy.wait()

    return pl.pallas_call(
        kernel,
        out_shape=jax.ShapeDtypeStruct((levels, chunks, chunk, 2 * width), BF16),
        in_specs=[ANYWHERE] * len(slots.operands),
        out_specs=WHOLE,
        scratch_shapes=[pltpu.SemaphoreType.DMA((rows, 2))],
        compiler_params=params(8),
        cost_estimate=large_cost(),
        name="pack_rows",
    )(*slots.operands)


def level_products(
    rows, width, height, packed, level, place, weights, level_slots, blocks, panels,
    total, rest, next_total, parents, next_diag, after,
):
    count = len(level_slots)
    slots = Slots(level_slots)
    has_next = next_total is not None
    chunks = rows if packed else 1
    chunk = height if packed else rows * height
    local = rows * height
    half = width // 2
    part = half // rows
    wide = 2 * width
    kinds = 2 if has_next else 1

    def kernel(*refs):
        refs = list(refs)

        def take(n):
            return [refs.pop(0) for _ in range(n)]

        place_ref, weight_ref = take(2)
        piece_refs = take(len(slots.operands))
        block_ref, panel_ref, total_ref, rest_ref = take(4)
        if has_next:
            next_total_ref, parent_ref, next_diag_ref = take(3)
        take(len(after))
        if has_next:
            next_out_ref, next_rest_ref = take(2)
        out_refs = take(2)
        left_buf, sums, diag_buf = take(3)
        assert not refs

        inner, my_row, pole = place_ref[0], place_ref[1], place_ref[2]
        first = place_ref[3].astype(F32)
        weight_real = weight_ref[0]
        weight_imag = weight_ref[1]

        for n in range(count):
            left_buf[:, n * 2 * height : (n + 1) * 2 * height] = slots.left(piece_refs, n, inner)

        def step(t, _):
            columns = pl.ds(pl.multiple_of(t * chunk, chunk), chunk)
            late = mm(left_buf[...], block_ref[t].reshape(count * 2 * height, chunk))
            x = -(total_ref[:, columns] + late)
            term = weight_real * x[width:] + weight_imag * x[:width]
            if packed:
                low, upper = term[:half], term[half:]
                out_refs[0][t, :half, :] = jnp.where(pole == 0, low, upper)
                out_refs[1][t, :half, :] = jnp.where(pole == 0, upper, low)
            else:
                out_refs[0][:, columns] = term
            x_high, x_low = split(x)
            x_both = jnp.concatenate([x_high, x_low], axis=0)
            for k in range(kinds):
                both = mm(x_both, panel_ref[level + k, t])
                sums[:, k * wide : (k + 1) * wide] += both[:wide] + both[wide:]
            if has_next:
                stacked = jnp.concatenate([x_high, x_low, x_high], axis=0)
                next_out_ref[:, columns] = next_total_ref[:, columns] + mm(
                    parent_ref[level], stacked
                )
            return 0

        sums[...] = jnp.zeros_like(sums)
        lax.fori_loop(0, chunks, step, 0)

        def complex_sum(k):
            at = k * wide
            real = sums[:width, at : at + width] - sums[width:, at + width : at + wide]
            imag = sums[:width, at + width : at + wide] + sums[width:, at : at + width]
            return real, imag

        own_real, own_imag = complex_sum(0)
        scale = first if level == 0 else 1.0
        y_real = rest_ref[0] * scale - own_real.T
        y_imag = rest_ref[1] * scale - own_imag.T
        diag_buf[...] = weight_real * y_imag + weight_imag * y_real
        if packed:
            for ref, side in ((out_refs[0], pole), (out_refs[1], 1 - pole)):
                for t in range(rows):
                    at = pl.multiple_of(side * half + (my_row ^ t) * part, part)
                    ref[t, half:, :] = diag_buf[pl.ds(at, part), :]
        else:
            out_refs[1][...] = diag_buf[...]
        if has_next:
            parent = parent_ref[level]
            parent_high, parent_low = parent[:, :wide], parent[:, 2 * wide :]
            follow_real, follow_imag = complex_sum(1)
            y_high, y_low = split(jnp.concatenate([y_real, y_imag], axis=1))
            mixed = mm_t(y_high, parent_high) + mm_t(y_low, parent_high) + mm_t(y_high, parent_low)
            z = -jnp.concatenate(
                [follow_real + mixed[:, :width], follow_imag + mixed[:, width:]], axis=0
            )
            z_high, z_low = split(z)
            back = mm(parent, jnp.concatenate([z_high, z_low, z_high], axis=0))
            next_rest_ref[0] = next_diag_ref[0] * first - back[:width]
            next_rest_ref[1] = next_diag_ref[1] * first - back[width:]

    operands = [place, weights] + slots.operands + [blocks, panels, total, rest]
    specs = [SCALARS, SCALARS] + [WHOLE] * (len(slots.operands) + 4)
    outs = []
    aliases = {}
    if has_next:
        aliases = {len(operands): 0}
        operands += [next_total, parents, next_diag]
        specs += [WHOLE] * 3
        outs += [
            jax.ShapeDtypeStruct((wide, local), F32),
            jax.ShapeDtypeStruct((2, width, width), F32),
        ]
    operands += after
    specs += [ANYWHERE] * len(after)
    if packed:
        outs += [jax.ShapeDtypeStruct((rows, half + part, height), F32)] * 2
    else:
        outs += [
            jax.ShapeDtypeStruct((width, local), F32),
            jax.ShapeDtypeStruct((width, width), F32),
        ]
    return pl.pallas_call(
        kernel,
        out_shape=outs,
        in_specs=specs,
        out_specs=[WHOLE] * len(outs),
        input_output_aliases=aliases,
        scratch_shapes=[
            pltpu.VMEM((wide, count * 2 * height), BF16),
            pltpu.VMEM((wide, kinds * wide), F32),
            pltpu.VMEM((width, width), F32),
        ],
        compiler_params=params(16),
        cost_estimate=large_cost() if has_next else small_cost(),
        name="level_%d" % level,
    )(*operands)


def join(values, after=()):
    def kernel(*refs):
        for n in range(len(values)):
            refs[-1][n] = refs[n][...]

    return pl.pallas_call(
        kernel,
        out_shape=jax.ShapeDtypeStruct((len(values),) + values[0].shape, values[0].dtype),
        in_specs=[WHOLE] * len(values) + [ANYWHERE] * len(after),
        out_specs=WHOLE,
        compiler_params=params(8),
        cost_estimate=small_cost(),
        name="join",
    )(*values, *after)


def add_parts(kept, received):
    levels = len(kept)
    rows = kept[0].shape[0]

    def kernel(*refs):
        for k in range(levels):
            for t in range(rows):
                refs[2 * levels + t][k] = refs[k][t] + refs[levels + k][t]

    return pl.pallas_call(
        kernel,
        out_shape=[jax.ShapeDtypeStruct((levels,) + kept[0].shape[1:], F32)] * rows,
        in_specs=[WHOLE] * (2 * levels),
        out_specs=[WHOLE] * rows,
        compiler_params=params(12),
        cost_estimate=small_cost(),
        name="add_parts",
    )(*kept, *received)


def gather_four(piece, me, axis, after):
    inner = (me == 1) | (me == 2)
    pairs = [(0, 1), (1, 0), (2, 3), (3, 2)]
    middle_pairs = [(1, 2), (2, 1)]
    outer_pairs = [(1, 0), (2, 3)]
    owners = [
        me,
        me ^ 1,
        jnp.where(inner, 3 - me, me ^ 2),
        jnp.where(inner, (3 - me) ^ 1, me ^ 3),
    ]
    near = lax.ppermute(piece, axis, pairs)
    joined = join([piece, near], after)
    middle = lax.ppermute(joined, axis, middle_pairs)
    outer = lax.ppermute(middle, axis, outer_pairs)
    far = [[(middle, n), (outer, n)] for n in range(2)]
    after[:] = [joined]
    return owners, [[(piece, None)], [(near, None)]], far


def gather_line(piece, me, count, axis):
    owners, slots = [me], [[(piece, None)]]
    from_left = from_right = piece
    for step in range(1, count):
        from_left = lax.ppermute(from_left, axis, [(i, i + 1) for i in range(step - 1, count - 1)])
        from_right = lax.ppermute(from_right, axis, [(i, i - 1) for i in range(1, count - step + 1)])
        if 2 * step >= count:
            owners.append(jnp.clip(jnp.where(me >= step, me - step, me + step), 0, count - 1))
            slots.append([(jnp.where(me >= step, from_left, from_right), None)])
        else:
            owners += [jnp.maximum(me - step, 0), jnp.minimum(me + step, count - 1)]
            slots += [[(from_left, None)], [(from_right, None)]]
    return owners, slots[:1], slots[1:]


def gather_rows(value, near, far):
    first = exchange(value, "row", 4, near)
    second = exchange(join([value, first]), "row", 4, far)
    found = {0: (value, None), near: (first, None), far: (second, 0), 3: (second, 1)}
    return [found[t] for t in range(4)]


def gather(piece, me, count, axis, after):
    if count == 4:
        return gather_four(piece, me, axis, after)
    return gather_line(piece, me, count, axis)


def make_per_device(sizes):
    poles, rows, cols = sizes

    def per_device(inverse_block, panels, panel_mask, parent_panels, diag_inverse, pole_weights):
        levels = panels.shape[1]
        height = panels.shape[5]
        width = panels.shape[6]
        half = width // 2
        part = half // rows
        packed = (
            poles == 2
            and rows & (rows - 1) == 0
            and cols & (cols - 1) == 0
            and height == width
            and height % 128 == 0
            and part % 8 == 0
        )
        my_pole = lax.axis_index("pole")
        my_row = lax.axis_index("row")
        my_col = lax.axis_index("col")
        first = ((my_row == 0) & (my_col == 0)).astype(jnp.int32)
        inner = ((my_col == 1) | (my_col == 2)).astype(jnp.int32)
        blocks = inverse_block[0, :, :, 0]
        local_panels = panels[0, :, :, 0, 0]
        flags = panel_mask[:, 0, 0]
        weights = pole_weights[0]
        flipped = (2, width, height)

        def masked(which, after):
            keep = bool(after)
            outs = [jax.ShapeDtypeStruct(flipped, BF16)] * len(which)
            if keep:
                outs += [jax.ShapeDtypeStruct((levels, height, width), BF16)] * 2
            return pl.pallas_call(
                functools.partial(mask_kernel, which, keep),
                out_shape=outs,
                in_specs=[FAR, FAR] + [ANYWHERE] * len(after),
                out_specs=[WHOLE] * len(outs),
                scratch_shapes=[
                    pltpu.VMEM((levels if keep else len(which),) + local_panels.shape[1:], BF16),
                    pltpu.SMEM((levels,), jnp.int32),
                    pltpu.SemaphoreType.DMA((2,)),
                ],
                compiler_params=params(8),
                cost_estimate=small_cost(),
                name="mask_rows" if keep else "mask",
            )(flags, local_panels, *after)

        pieces = list(masked([0], []))
        *more, kept_real, kept_imag = masked(list(range(1, levels)), pieces)
        pieces += more
        parents = pl.pallas_call(
            parent_kernel,
            out_shape=jax.ShapeDtypeStruct((levels - 1, 2 * width, 6 * width), BF16),
            in_specs=[WHOLE],
            out_specs=WHOLE,
            compiler_params=params(12),
            cost_estimate=small_cost(),
            name="parents",
        )(parent_panels[0])
        after = []
        gathered = [gather(piece, my_col, cols, "col", after) for piece in pieces]
        if packed and rows == 4:
            reals = gather_rows(kept_real, 1, 2)
            imags = gather_rows(kept_imag, 2, 1)
        elif packed:
            reals, imags = [
                [(value, None)]
                + [(exchange(value, "row", rows, t), None) for t in range(1, rows)]
                for value in (kept_real, kept_imag)
            ]
        else:
            reals, imags = [
                [(piece, None) for piece in lax.all_gather(value, "row")]
                for value in (kept_real, kept_imag)
            ]

        def sum_rows(stack):
            return tree_sum([stack[0]] + [exchange(stack[t], "row", rows, t) for t in range(1, rows)])

        def spread(piece):
            whole = tree_sum([piece] + [exchange(piece, "col", cols, t) for t in range(1, cols)])
            whole = jnp.stack([whole] + [exchange(whole, "row", rows, t) for t in range(1, rows)])
            whole = xor_order(whole, my_row, rows)
            other = exchange(whole, "pole", 2, 1)
            return xor_order(jnp.stack([whole, other]), my_pole, 2)

        owners = gathered[0][0]
        place = jnp.stack(
            [jnp.asarray(v, jnp.int32) for v in [inner, my_row, my_pole, first] + owners]
        )
        late = len(gathered[0][2])
        *totals, late_blocks = early_products(
            rows,
            width,
            height,
            packed,
            place,
            [g[1] for g in gathered],
            late,
            blocks,
            [],
        )
        row_panels = pack_panels(levels, rows, width, height, packed, reals, imags)
        rest = diag_inverse[0, 0]
        panel_parts = []
        diag_parts = []
        kept = []
        received = []
        sums = []
        first_sum = []
        far_ordered = [s[1][0] for s in gathered[-1][2][:1] if len(s) == 2]
        ordered = [g[2][0][0][0] for g in gathered[1:] if len(g[2][0]) == 2]
        for level in range(levels):
            has_next = level + 1 < levels
            outs = level_products(
                rows,
                width,
                height,
                packed,
                level,
                place,
                weights,
                gathered[level][2],
                late_blocks,
                row_panels,
                totals[level],
                rest,
                totals[level + 1] if has_next else None,
                parents,
                diag_inverse[0, level + 1] if has_next else None,
                ordered if level == 0 else first_sum if not has_next else far_ordered,
            )
            if has_next:
                totals[level + 1] = outs[0]
                rest = outs[1]
                outs = outs[2:]
            if packed:
                kept.append(outs[0])
                received.append(exchange(outs[1], "pole", 2, 1))
                if level == 0 or not has_next:
                    parts = add_parts(kept, received)
                    first_sum = [parts[0]]
                    mine = sum_rows(parts)
                    sums += [mine[n] for n in range(len(kept))]
                    kept, received = [], []
            else:
                mine = lax.psum_scatter(outs[0], "row", scatter_dimension=1, tiled=True)
                mine = lax.psum_scatter(mine, "pole", scatter_dimension=0, tiled=True)
                panel_parts.append(mine.T)
                diag_parts.append(lax.psum(outs[1], ("pole", "row", "col")))
        if packed:
            panel_parts = [mine[:half].T for mine in sums]
            got = spread(jnp.stack([mine[half:] for mine in sums]))
            diag_parts = [got[:, :, n].reshape(width, width) for n in range(levels)]
        return jnp.stack(panel_parts)[:, None, None], jnp.stack(diag_parts)

    return per_device


def solution(mesh):
    placed = (
        P("pole", None, None, "row", None, "col"),
        P("pole", None, None, "col", "row", None, None),
        P(None, "col", "row"),
        P("pole", None, None, None, None),
        P("pole", None, None, None, None),
        P("pole", None),
    )
    return jax.shard_map(
        make_per_device((mesh.shape["pole"], mesh.shape["row"], mesh.shape["col"])),
        mesh=mesh,
        in_specs=placed,
        out_specs=(P(None, "col", "row", None, "pole"), P()),
        check_vma=False,
    )
```

```python
import functools

import jax
import jax.numpy as jnp
from jax import lax
from jax.experimental import pallas as pl
from jax.experimental.pallas import tpu as pltpu
from jax.sharding import PartitionSpec as P

F32 = jnp.float32
BF16 = jnp.bfloat16
WHOLE = pl.BlockSpec(memory_space=pltpu.VMEM)
SCALARS = pl.BlockSpec(memory_space=pltpu.SMEM)
ANYWHERE = pl.BlockSpec(memory_space=pl.ANY)
FAR = pl.BlockSpec(memory_space=pltpu.HBM)


def params(mebibytes):
    return pltpu.CompilerParams(vmem_limit_bytes=mebibytes << 20)


def small_cost():
    return pl.CostEstimate(flops=1, bytes_accessed=1, transcendentals=0)


def large_cost():
    return pl.CostEstimate(flops=10**11, bytes_accessed=1, transcendentals=0)


def mm(left, right):
    return jnp.dot(left, right, preferred_element_type=F32)


def mm_t(left, right):
    return lax.dot_general(left, right, (((1,), (1,)), ((), ())), preferred_element_type=F32)


def split(value):
    high = value.astype(BF16)
    return high, (value - high.astype(F32)).astype(BF16)


def exchange(value, axes, count, distance):
    return lax.ppermute(value, axes, [(i, i ^ distance) for i in range(count)])


def tree_sum(values):
    while len(values) > 1:
        values = [values[i] + values[i + 1] for i in range(0, len(values), 2)]
    return values[0]


def xor_order(stack, me, count):
    bits = count.bit_length() - 1
    rest = stack.shape[1:]
    values = stack.reshape((2,) * bits + rest)
    for axis in range(bits):
        bit = (me >> (bits - 1 - axis)) & 1
        values = jnp.where(bit == 1, jnp.flip(values, axis), values)
    return values.reshape((count,) + rest)


def mask_kernel(levels, keep, flag_ref, panel_ref, *refs):
    refs = list(refs)
    if keep:
        refs.pop(0)
    out_refs = [refs.pop(0) for _ in levels]
    kept_refs = [refs.pop(0) for _ in range(2)] if keep else None
    buf, flags, sems = refs
    first = 0 if keep else levels[0]
    copies = [
        pltpu.make_async_copy(panel_ref.at[pl.ds(first, buf.shape[0])], buf, sems.at[0]),
        pltpu.make_async_copy(flag_ref, flags, sems.at[1]),
    ]
    for copy in copies:
        copy.start()
    for copy in copies:
        copy.wait()
    for k in range(buf.shape[0]):
        flag = flags[first + k].astype(F32)
        for part in range(2):
            value = buf[k, part].astype(F32) * flag
            if keep:
                kept_refs[part][k] = value.astype(BF16)
            if first + k in levels:
                out_refs[levels.index(first + k)][part] = value.T.astype(BF16)


def parent_kernel(parent_ref, out_ref):
    for k in range(parent_ref.shape[0]):
        real_high, real_low = split(parent_ref[k, 0].T)
        imag_high, imag_low = split(parent_ref[k, 1].T)
        high = left_block(real_high, imag_high)
        wide = high.shape[1]
        out_ref[k, :, :wide] = high
        out_ref[k, :, wide : 2 * wide] = high
        out_ref[k, :, 2 * wide :] = left_block(real_low, imag_low)


def left_block(real, imag):
    return jnp.concatenate(
        [jnp.concatenate([real, -imag], axis=1), jnp.concatenate([imag, real], axis=1)], axis=0
    )


class Slots:
    def __init__(self, slots):
        self.operands = []
        self.slots = []
        for slot in slots:
            self.slots.append([(self.place(array), index) for array, index in slot])

    def place(self, array):
        for n, operand in enumerate(self.operands):
            if operand is array:
                return n
        self.operands.append(array)
        return len(self.operands) - 1

    def left(self, refs, n, inner):
        parts = []
        for part in range(2):
            values = [
                refs[at][part] if index is None else refs[at][index, part]
                for at, index in self.slots[n]
            ]
            parts.append(values[0] if len(values) == 1 else jnp.where(inner == 1, *values))
        return left_block(*parts)


def block_copies(block_ref, buf, sem, owners, my_row, rows, height, ordered):
    copies = []
    for n, owner in enumerate(owners):
        if not ordered:
            copies.append([pltpu.make_async_copy(block_ref.at[:, owner], buf.at[n], sem.at[n, 0])])
            continue
        copies.append(
            [
                pltpu.make_async_copy(
                    block_ref.at[
                        :, owner, :, pl.ds(pl.multiple_of((my_row ^ t) * height, height), height)
                    ],
                    buf.at[n, :, :, pl.ds(t * height, height)],
                    sem.at[n, t],
                )
                for t in range(rows)
            ]
        )
    return copies


def early_products(rows, width, height, ordered, place, level_slots, late, blocks, after):
    levels = len(level_slots)
    count = len(level_slots[0])
    slots = Slots([slot for level in level_slots for slot in level])
    local = rows * height
    chunks = rows if ordered else 1
    chunk = height if ordered else local

    def kernel(place_ref, block_ref, *refs):
        piece_refs = refs[: len(slots.operands)]
        out_refs = refs[len(slots.operands) + len(after) :][:levels]
        late_ref, buf, left_buf, sem, late_sem = refs[-5:]
        my_row = place_ref[1]
        owners = [place_ref[4 + n] for n in range(count)]
        copies = block_copies(block_ref, buf, sem, owners, my_row, rows, height, ordered)
        late_copies = []
        for n in range(late):
            owner = place_ref[4 + count + n]
            for t in range(chunks):
                start = pl.multiple_of((my_row ^ t) * chunk, chunk) if ordered else 0
                late_copies.append(
                    pltpu.make_async_copy(
                        block_ref.at[:, owner, :, pl.ds(start, chunk)],
                        late_ref.at[t, n],
                        late_sem.at[n, t],
                    )
                )
        for copy in sum(copies, []) + late_copies:
            copy.start()
        for level in range(levels):
            for n in range(count):
                left_buf[
                    level * 2 * width : (level + 1) * 2 * width,
                    n * 2 * height : (n + 1) * 2 * height,
                ] = slots.left(piece_refs, level * count + n, place_ref[0])
        for copy in sum(copies, []):
            copy.wait()
        right = buf[...].reshape(count * 2 * height, local)
        for level in range(levels):
            left = left_buf[level * 2 * width : (level + 1) * 2 * width, :]
            out_refs[level][...] = mm(left, right)
        for copy in late_copies:
            copy.wait()

    outs = [jax.ShapeDtypeStruct((2 * width, local), F32)] * levels
    outs.append(jax.ShapeDtypeStruct((chunks, late, 2, height, chunk), BF16))
    return pl.pallas_call(
        kernel,
        out_shape=outs,
        in_specs=[SCALARS, FAR] + [WHOLE] * len(slots.operands) + [ANYWHERE] * len(after),
        out_specs=[WHOLE] * len(outs),
        scratch_shapes=[
            pltpu.VMEM((count, 2, height, local), BF16),
            pltpu.VMEM((levels * 2 * width, count * 2 * height), BF16),
            pltpu.SemaphoreType.DMA((count, rows)),
            pltpu.SemaphoreType.DMA((late, chunks)),
        ],
        compiler_params=params(24),
        cost_estimate=large_cost(),
        name="early",
    )(place, blocks, *slots.operands, *after)


def pack_panels(levels, rows, width, height, packed, reals, imags):
    chunks = rows if packed else 1
    chunk = height if packed else rows * height
    slots = Slots([reals, imags])

    def kernel(*refs):
        panel_refs = refs[: len(slots.operands)]
        out_ref, sem = refs[len(slots.operands) :]
        copies = []
        for p in range(2):
            for r in range(rows):
                at, index = slots.slots[p][r]
                source = panel_refs[at] if index is None else panel_refs[at].at[index]
                target = out_ref.at[
                    :, r if packed else 0,
                    pl.ds(0 if packed else r * height, height),
                    pl.ds(p * width, width),
                ]
                copies.append(pltpu.make_async_copy(source, target, sem.at[r, p]))
        for copy in copies:
            copy.start()
        for copy in copies:
            copy.wait()

    return pl.pallas_call(
        kernel,
        out_shape=jax.ShapeDtypeStruct((levels, chunks, chunk, 2 * width), BF16),
        in_specs=[ANYWHERE] * len(slots.operands),
        out_specs=WHOLE,
        scratch_shapes=[pltpu.SemaphoreType.DMA((rows, 2))],
        compiler_params=params(8),
        cost_estimate=large_cost(),
        name="pack_rows",
    )(*slots.operands)


def level_products(
    rows, width, height, packed, level, place, weights, level_slots, blocks, panels,
    total, rest, next_total, parents, next_diag, after,
):
    count = len(level_slots)
    slots = Slots(level_slots)
    has_next = next_total is not None
    chunks = rows if packed else 1
    chunk = height if packed else rows * height
    local = rows * height
    half = width // 2
    part = half // rows
    wide = 2 * width
    kinds = 2 if has_next else 1

    def kernel(*refs):
        refs = list(refs)

        def take(n):
            return [refs.pop(0) for _ in range(n)]

        place_ref, weight_ref = take(2)
        piece_refs = take(len(slots.operands))
        block_ref, panel_ref, total_ref, rest_ref = take(4)
        if has_next:
            next_total_ref, parent_ref, next_diag_ref = take(3)
        take(len(after))
        if has_next:
            next_out_ref, next_rest_ref = take(2)
        out_refs = take(3) if packed else take(2)
        left_buf, sums, diag_buf = take(3)
        assert not refs

        inner, my_row, pole = place_ref[0], place_ref[1], place_ref[2]
        first = place_ref[3].astype(F32)
        weight_real = weight_ref[0]
        weight_imag = weight_ref[1]

        for n in range(count):
            left_buf[:, n * 2 * height : (n + 1) * 2 * height] = slots.left(piece_refs, n, inner)

        def step(t, _):
            columns = pl.ds(pl.multiple_of(t * chunk, chunk), chunk)
            late = mm(left_buf[...], block_ref[t].reshape(count * 2 * height, chunk))
            x = -(total_ref[:, columns] + late)
            term = weight_real * x[width:] + weight_imag * x[:width]
            if packed:
                low, upper = term[:half], term[half:]
                out_refs[0][t, :half, :] = jnp.where(pole == 0, low, upper)
                sent = jnp.where(pole == 0, upper, low)

                @pl.when(t < rows // 2)
                def _():
                    out_refs[1][t, :half, :] = sent

                @pl.when(t >= rows // 2)
                def _():
                    out_refs[2][t - rows // 2, :half, :] = sent

            else:
                out_refs[0][:, columns] = term
            x_high, x_low = split(x)
            x_both = jnp.concatenate([x_high, x_low], axis=0)
            for k in range(kinds):
                both = mm(x_both, panel_ref[level + k, t])
                sums[:, k * wide : (k + 1) * wide] += both[:wide] + both[wide:]
            if has_next:
                stacked = jnp.concatenate([x_high, x_low, x_high], axis=0)
                next_out_ref[:, columns] = next_total_ref[:, columns] + mm(
                    parent_ref[level], stacked
                )
            return 0

        sums[...] = jnp.zeros_like(sums)
        lax.fori_loop(0, chunks, step, 0)

        def complex_sum(k):
            at = k * wide
            real = sums[:width, at : at + width] - sums[width:, at + width : at + wide]
            imag = sums[:width, at + width : at + wide] + sums[width:, at : at + width]
            return real, imag

        own_real, own_imag = complex_sum(0)
        scale = first if level == 0 else 1.0
        y_real = rest_ref[0] * scale - own_real.T
        y_imag = rest_ref[1] * scale - own_imag.T
        diag_buf[...] = weight_real * y_imag + weight_imag * y_real
        if packed:
            for t in range(rows):
                places = ((out_refs[0], t, pole), (out_refs[1 + 2 * t // rows], t % (rows // 2), 1 - pole))
                for ref, n, side in places:
                    at = pl.multiple_of(side * half + (my_row ^ t) * part, part)
                    ref[n, half:, :] = diag_buf[pl.ds(at, part), :]
        else:
            out_refs[1][...] = diag_buf[...]
        if has_next:
            parent = parent_ref[level]
            parent_high, parent_low = parent[:, :wide], parent[:, 2 * wide :]
            follow_real, follow_imag = complex_sum(1)
            y_high, y_low = split(jnp.concatenate([y_real, y_imag], axis=1))
            mixed = mm_t(y_high, parent_high) + mm_t(y_low, parent_high) + mm_t(y_high, parent_low)
            z = -jnp.concatenate(
                [follow_real + mixed[:, :width], follow_imag + mixed[:, width:]], axis=0
            )
            z_high, z_low = split(z)
            back = mm(parent, jnp.concatenate([z_high, z_low, z_high], axis=0))
            next_rest_ref[0] = next_diag_ref[0] * first - back[:width]
            next_rest_ref[1] = next_diag_ref[1] * first - back[width:]

    operands = [place, weights] + slots.operands + [blocks, panels, total, rest]
    specs = [SCALARS, SCALARS] + [WHOLE] * (len(slots.operands) + 4)
    outs = []
    aliases = {}
    if has_next:
        aliases = {len(operands): 0}
        operands += [next_total, parents, next_diag]
        specs += [WHOLE] * 3
        outs += [
            jax.ShapeDtypeStruct((wide, local), F32),
            jax.ShapeDtypeStruct((2, width, width), F32),
        ]
    operands += after
    specs += [ANYWHERE] * len(after)
    if packed:
        outs.append(jax.ShapeDtypeStruct((rows, half + part, height), F32))
        outs += [jax.ShapeDtypeStruct((rows // 2, half + part, height), F32)] * 2
    else:
        outs += [
            jax.ShapeDtypeStruct((width, local), F32),
            jax.ShapeDtypeStruct((width, width), F32),
        ]
    return pl.pallas_call(
        kernel,
        out_shape=outs,
        in_specs=specs,
        out_specs=[WHOLE] * len(outs),
        input_output_aliases=aliases,
        scratch_shapes=[
            pltpu.VMEM((wide, count * 2 * height), BF16),
            pltpu.VMEM((wide, kinds * wide), F32),
            pltpu.VMEM((width, width), F32),
        ],
        compiler_params=params(16),
        cost_estimate=large_cost() if has_next else small_cost(),
        name="level_%d" % level,
    )(*operands)


def join(values, after=()):
    def kernel(*refs):
        for n in range(len(values)):
            refs[-1][n] = refs[n][...]

    return pl.pallas_call(
        kernel,
        out_shape=jax.ShapeDtypeStruct((len(values),) + values[0].shape, values[0].dtype),
        in_specs=[WHOLE] * len(values) + [ANYWHERE] * len(after),
        out_specs=WHOLE,
        compiler_params=params(8),
        cost_estimate=small_cost(),
        name="join",
    )(*values, *after)


def add_parts(kept, received):
    levels = len(kept)
    rows = kept[0].shape[0]

    def kernel(*refs):
        for k in range(levels):
            for t in range(rows):
                got = refs[levels + 2 * k + 2 * t // rows][t % (rows // 2)]
                refs[3 * levels + t][k] = refs[k][t] + got

    return pl.pallas_call(
        kernel,
        out_shape=[jax.ShapeDtypeStruct((levels,) + kept[0].shape[1:], F32)] * rows,
        in_specs=[WHOLE] * (3 * levels),
        out_specs=[WHOLE] * rows,
        compiler_params=params(12),
        cost_estimate=small_cost(),
        name="add_parts",
    )(*kept, *received)


def gather_four(piece, me, axis, after, held):
    inner = (me == 1) | (me == 2)
    pairs = [(0, 1), (1, 0), (2, 3), (3, 2)]
    middle_pairs = [(1, 2), (2, 1)]
    outer_pairs = [(1, 0), (2, 3)]
    owners = [
        me,
        me ^ 1,
        jnp.where(inner, 3 - me, me ^ 2),
        jnp.where(inner, (3 - me) ^ 1, me ^ 3),
    ]
    near = lax.ppermute(piece, axis, pairs)
    joined = join([piece, near], after + held)
    middle = lax.ppermute(joined, axis, middle_pairs)
    outer = lax.ppermute(middle, axis, outer_pairs)
    far = [[(middle, n), (outer, n)] for n in range(2)]
    after[:] = [joined]
    return owners, [[(piece, None)], [(near, None)]], far


def gather_line(piece, me, count, axis):
    owners, slots = [me], [[(piece, None)]]
    from_left = from_right = piece
    for step in range(1, count):
        from_left = lax.ppermute(from_left, axis, [(i, i + 1) for i in range(step - 1, count - 1)])
        from_right = lax.ppermute(from_right, axis, [(i, i - 1) for i in range(1, count - step + 1)])
        if 2 * step >= count:
            owners.append(jnp.clip(jnp.where(me >= step, me - step, me + step), 0, count - 1))
            slots.append([(jnp.where(me >= step, from_left, from_right), None)])
        else:
            owners += [jnp.maximum(me - step, 0), jnp.minimum(me + step, count - 1)]
            slots += [[(from_left, None)], [(from_right, None)]]
    return owners, slots[:1], slots[1:]


def gather_rows(value, near, far):
    first = exchange(value, "row", 4, near)
    joined = join([value, first])
    second = exchange(joined, "row", 4, far)
    found = {0: (value, None), near: (first, None), far: (second, 0), 3: (second, 1)}
    return [found[t] for t in range(4)], first, joined


def gather(piece, me, count, axis, after, held):
    if count == 4:
        return gather_four(piece, me, axis, after, held)
    return gather_line(piece, me, count, axis)


def make_per_device(sizes):
    poles, rows, cols = sizes

    def per_device(inverse_block, panels, panel_mask, parent_panels, diag_inverse, pole_weights):
        levels = panels.shape[1]
        height = panels.shape[5]
        width = panels.shape[6]
        half = width // 2
        part = half // rows
        packed = (
            poles == 2
            and rows & (rows - 1) == 0
            and cols & (cols - 1) == 0
            and height == width
            and height % 128 == 0
            and part % 8 == 0
        )
        my_pole = lax.axis_index("pole")
        my_row = lax.axis_index("row")
        my_col = lax.axis_index("col")
        first = ((my_row == 0) & (my_col == 0)).astype(jnp.int32)
        inner = ((my_col == 1) | (my_col == 2)).astype(jnp.int32)
        blocks = inverse_block[0, :, :, 0]
        local_panels = panels[0, :, :, 0, 0]
        flags = panel_mask[:, 0, 0]
        weights = pole_weights[0]
        flipped = (2, width, height)

        def masked(which, after):
            keep = bool(after)
            outs = [jax.ShapeDtypeStruct(flipped, BF16)] * len(which)
            if keep:
                outs += [jax.ShapeDtypeStruct((levels, height, width), BF16)] * 2
            return pl.pallas_call(
                functools.partial(mask_kernel, which, keep),
                out_shape=outs,
                in_specs=[FAR, FAR] + [ANYWHERE] * len(after),
                out_specs=[WHOLE] * len(outs),
                scratch_shapes=[
                    pltpu.VMEM((levels if keep else len(which),) + local_panels.shape[1:], BF16),
                    pltpu.SMEM((levels,), jnp.int32),
                    pltpu.SemaphoreType.DMA((2,)),
                ],
                compiler_params=params(8),
                cost_estimate=small_cost(),
                name="mask_rows" if keep else "mask",
            )(flags, local_panels, *after)

        pieces = list(masked([0], []))
        *more, kept_real, kept_imag = masked(list(range(1, levels)), pieces)
        pieces += more
        parents = pl.pallas_call(
            parent_kernel,
            out_shape=jax.ShapeDtypeStruct((levels - 1, 2 * width, 6 * width), BF16),
            in_specs=[WHOLE],
            out_specs=WHOLE,
            compiler_params=params(12),
            cost_estimate=small_cost(),
            name="parents",
        )(parent_panels[0])
        held = [[] for _ in pieces]
        if packed and rows == 4:
            reals, *steps_real = gather_rows(kept_real, 1, 2)
            imags, *steps_imag = gather_rows(kept_imag, 2, 1)
            held[1] = [steps_real[0], steps_imag[0]]
            held[2] = [steps_real[1], steps_imag[1]]
        elif packed:
            reals, imags = [
                [(value, None)]
                + [(exchange(value, "row", rows, t), None) for t in range(1, rows)]
                for value in (kept_real, kept_imag)
            ]
        else:
            reals, imags = [
                [(piece, None) for piece in lax.all_gather(value, "row")]
                for value in (kept_real, kept_imag)
            ]

        after = []
        gathered = []
        for k, piece in enumerate(pieces):
            gathered.append(gather(piece, my_col, cols, "col", after, held[k]))

        def sum_rows(stack):
            return tree_sum([stack[0]] + [exchange(stack[t], "row", rows, t) for t in range(1, rows)])

        def spread(piece):
            whole = tree_sum([piece] + [exchange(piece, "col", cols, t) for t in range(1, cols)])
            whole = jnp.stack([whole] + [exchange(whole, "row", rows, t) for t in range(1, rows)])
            whole = xor_order(whole, my_row, rows)
            other = exchange(whole, "pole", 2, 1)
            return xor_order(jnp.stack([whole, other]), my_pole, 2)

        owners = gathered[0][0]
        place = jnp.stack(
            [jnp.asarray(v, jnp.int32) for v in [inner, my_row, my_pole, first] + owners]
        )
        late = len(gathered[0][2])
        *totals, late_blocks = early_products(
            rows,
            width,
            height,
            packed,
            place,
            [g[1] for g in gathered],
            late,
            blocks,
            [g[2][0][0][0] for g in gathered[:-1] if len(g[2][0]) == 2],
        )
        row_panels = pack_panels(levels, rows, width, height, packed, reals, imags)
        rest = diag_inverse[0, 0]
        panel_parts = []
        diag_parts = []
        kept = []
        received = []
        sums = []
        first_sum = []
        far_ordered = [s[1][0] for s in gathered[-1][2][:1] if len(s) == 2]
        ordered = [g[2][0][0][0] for g in gathered[1:-1] if len(g[2][0]) == 2]
        for level in range(levels):
            has_next = level + 1 < levels
            outs = level_products(
                rows,
                width,
                height,
                packed,
                level,
                place,
                weights,
                gathered[level][2],
                late_blocks,
                row_panels,
                totals[level],
                rest,
                totals[level + 1] if has_next else None,
                parents,
                diag_inverse[0, level + 1] if has_next else None,
                ordered if level == 0 else first_sum if not has_next else [],
            )
            if has_next:
                totals[level + 1] = outs[0]
                rest = outs[1]
                outs = outs[2:]
            if packed:
                kept.append(outs[0])
                received += [exchange(value, "pole", 2, 1) for value in outs[1:]]
                if level == 0 or not has_next:
                    parts = add_parts(kept, received)
                    mine = sum_rows(parts)
                    first_sum = [mine]
                    sums += [mine[n] for n in range(len(kept))]
                    kept, received = [], []
            else:
                mine = lax.psum_scatter(outs[0], "row", scatter_dimension=1, tiled=True)
                mine = lax.psum_scatter(mine, "pole", scatter_dimension=0, tiled=True)
                panel_parts.append(mine.T)
                diag_parts.append(lax.psum(outs[1], ("pole", "row", "col")))
        if packed:
            panel_parts = [mine[:half].T for mine in sums]
            got = spread(jnp.stack([mine[half:] for mine in sums]))
            diag_parts = [got[:, :, n].reshape(width, width) for n in range(levels)]
        return jnp.stack(panel_parts)[:, None, None], jnp.stack(diag_parts)

    return per_device


def solution(mesh):
    placed = (
        P("pole", None, None, "row", None, "col"),
        P("pole", None, None, "col", "row", None, None),
        P(None, "col", "row"),
        P("pole", None, None, None, None),
        P("pole", None, None, None, None),
        P("pole", None),
    )
    return jax.shard_map(
        make_per_device((mesh.shape["pole"], mesh.shape["row"], mesh.shape["col"])),
        mesh=mesh,
        in_specs=placed,
        out_specs=(P(None, "col", "row", None, "pole"), P()),
        check_vma=False,
    )
```

```python
import functools

import jax
import jax.numpy as jnp
from jax import lax
from jax.experimental import pallas as pl
from jax.experimental.pallas import tpu as pltpu
from jax.sharding import PartitionSpec as P

F32 = jnp.float32
BF16 = jnp.bfloat16
WHOLE = pl.BlockSpec(memory_space=pltpu.VMEM)
SCALARS = pl.BlockSpec(memory_space=pltpu.SMEM)
ANYWHERE = pl.BlockSpec(memory_space=pl.ANY)
FAR = pl.BlockSpec(memory_space=pltpu.HBM)


def params(mebibytes):
    return pltpu.CompilerParams(vmem_limit_bytes=mebibytes << 20)


def small_cost():
    return pl.CostEstimate(flops=1, bytes_accessed=1, transcendentals=0)


def large_cost():
    return pl.CostEstimate(flops=10**11, bytes_accessed=1, transcendentals=0)


def mm(left, right):
    return jnp.dot(left, right, preferred_element_type=F32)


def mm_t(left, right):
    return lax.dot_general(left, right, (((1,), (1,)), ((), ())), preferred_element_type=F32)


def split(value):
    high = value.astype(BF16)
    return high, (value - high.astype(F32)).astype(BF16)


def exchange(value, axes, count, distance):
    return lax.ppermute(value, axes, [(i, i ^ distance) for i in range(count)])


def tree_sum(values):
    while len(values) > 1:
        values = [values[i] + values[i + 1] for i in range(0, len(values), 2)]
    return values[0]


def xor_order(stack, me, count):
    bits = count.bit_length() - 1
    rest = stack.shape[1:]
    values = stack.reshape((2,) * bits + rest)
    for axis in range(bits):
        bit = (me >> (bits - 1 - axis)) & 1
        values = jnp.where(bit == 1, jnp.flip(values, axis), values)
    return values.reshape((count,) + rest)


def mask_kernel(levels, keep, flag_ref, panel_ref, *refs):
    refs = list(refs)
    if keep:
        refs.pop(0)
    out_refs = [refs.pop(0) for _ in levels]
    kept_refs = [refs.pop(0) for _ in range(2)] if keep else None
    buf, flags, sems = refs
    first = 0 if keep else levels[0]
    copies = [
        pltpu.make_async_copy(panel_ref.at[pl.ds(first, buf.shape[0])], buf, sems.at[0]),
        pltpu.make_async_copy(flag_ref, flags, sems.at[1]),
    ]
    for copy in copies:
        copy.start()
    for copy in copies:
        copy.wait()
    for k in range(buf.shape[0]):
        flag = flags[first + k].astype(F32)
        for part in range(2):
            value = buf[k, part].astype(F32) * flag
            if keep:
                kept_refs[part][k] = value.astype(BF16)
            if first + k in levels:
                out_refs[levels.index(first + k)][part] = value.T.astype(BF16)


def parent_kernel(parent_ref, out_ref):
    for k in range(parent_ref.shape[0]):
        real_high, real_low = split(parent_ref[k, 0].T)
        imag_high, imag_low = split(parent_ref[k, 1].T)
        high = left_block(real_high, imag_high)
        wide = high.shape[1]
        out_ref[k, :, :wide] = high
        out_ref[k, :, wide : 2 * wide] = high
        out_ref[k, :, 2 * wide :] = left_block(real_low, imag_low)


def left_block(real, imag):
    return jnp.concatenate(
        [jnp.concatenate([real, -imag], axis=1), jnp.concatenate([imag, real], axis=1)], axis=0
    )


class Slots:
    def __init__(self, slots):
        self.operands = []
        self.slots = []
        for slot in slots:
            self.slots.append([(self.place(array), index) for array, index in slot])

    def place(self, array):
        for n, operand in enumerate(self.operands):
            if operand is array:
                return n
        self.operands.append(array)
        return len(self.operands) - 1

    def left(self, refs, n, inner):
        parts = []
        for part in range(2):
            values = [
                refs[at][part] if index is None else refs[at][index, part]
                for at, index in self.slots[n]
            ]
            parts.append(values[0] if len(values) == 1 else jnp.where(inner == 1, *values))
        return left_block(*parts)


def block_copies(block_ref, buf, sem, owners, my_row, rows, height, ordered):
    copies = []
    for n, owner in enumerate(owners):
        if not ordered:
            copies.append([pltpu.make_async_copy(block_ref.at[:, owner], buf.at[n], sem.at[n, 0])])
            continue
        copies.append(
            [
                pltpu.make_async_copy(
                    block_ref.at[
                        :, owner, :, pl.ds(pl.multiple_of((my_row ^ t) * height, height), height)
                    ],
                    buf.at[n, :, :, pl.ds(t * height, height)],
                    sem.at[n, t],
                )
                for t in range(rows)
            ]
        )
    return copies


def early_products(rows, width, height, ordered, place, level_slots, late, blocks, after):
    levels = len(level_slots)
    count = len(level_slots[0])
    slots = Slots([slot for level in level_slots for slot in level])
    local = rows * height

    def kernel(place_ref, block_ref, *refs):
        piece_refs = refs[: len(slots.operands)]
        out_refs = refs[len(slots.operands) + len(after) :][:levels]
        late_ref, buf, left_buf, sem, late_sem = refs[-5:]
        my_row = place_ref[1]
        owners = [place_ref[4 + n] for n in range(count)]
        copies = block_copies(block_ref, buf, sem, owners, my_row, rows, height, ordered)
        owners = [place_ref[4 + count + n] for n in range(late)]
        late_copies = sum(
            block_copies(block_ref, late_ref, late_sem, owners, my_row, rows, height, ordered), []
        )
        for copy in sum(copies, []) + late_copies:
            copy.start()
        for level in range(levels):
            for n in range(count):
                left_buf[
                    level * 2 * width : (level + 1) * 2 * width,
                    n * 2 * height : (n + 1) * 2 * height,
                ] = slots.left(piece_refs, level * count + n, place_ref[0])
        for copy in sum(copies, []):
            copy.wait()
        right = buf[...].reshape(count * 2 * height, local)
        for level in range(levels):
            left = left_buf[level * 2 * width : (level + 1) * 2 * width, :]
            out_refs[level][...] = mm(left, right)
        for copy in late_copies:
            copy.wait()

    outs = [jax.ShapeDtypeStruct((2 * width, local), F32)] * levels
    outs.append(jax.ShapeDtypeStruct((late, 2, height, local), BF16))
    return pl.pallas_call(
        kernel,
        out_shape=outs,
        in_specs=[SCALARS, FAR] + [WHOLE] * len(slots.operands) + [ANYWHERE] * len(after),
        out_specs=[WHOLE] * len(outs),
        scratch_shapes=[
            pltpu.VMEM((count, 2, height, local), BF16),
            pltpu.VMEM((levels * 2 * width, count * 2 * height), BF16),
            pltpu.SemaphoreType.DMA((count, rows)),
            pltpu.SemaphoreType.DMA((late, rows)),
        ],
        compiler_params=params(24),
        cost_estimate=large_cost(),
        name="early",
    )(place, blocks, *slots.operands, *after)


def pack_panels(levels, rows, width, height, packed, reals, imags):
    chunks = rows if packed else 1
    chunk = height if packed else rows * height
    slots = Slots([reals, imags])

    def kernel(*refs):
        panel_refs = refs[: len(slots.operands)]
        out_ref, sem = refs[len(slots.operands) :]
        copies = []
        for p in range(2):
            for r in range(rows):
                at, index = slots.slots[p][r]
                source = panel_refs[at] if index is None else panel_refs[at].at[index]
                target = out_ref.at[
                    :, r if packed else 0,
                    pl.ds(0 if packed else r * height, height),
                    pl.ds(p * width, width),
                ]
                copies.append(pltpu.make_async_copy(source, target, sem.at[r, p]))
        for copy in copies:
            copy.start()
        for copy in copies:
            copy.wait()

    return pl.pallas_call(
        kernel,
        out_shape=jax.ShapeDtypeStruct((levels, chunks, chunk, 2 * width), BF16),
        in_specs=[ANYWHERE] * len(slots.operands),
        out_specs=WHOLE,
        scratch_shapes=[pltpu.SemaphoreType.DMA((rows, 2))],
        compiler_params=params(8),
        cost_estimate=large_cost(),
        name="pack_rows",
    )(*slots.operands)


def level_products(
    rows, width, height, packed, level, place, weights, level_slots, blocks, panels,
    total, rest, next_total, parents, next_diag, after,
):
    count = len(level_slots)
    slots = Slots(level_slots)
    has_next = next_total is not None
    local = rows * height
    half = width // 2
    part = half // rows
    wide = 2 * width
    kinds = 2 if has_next else 1

    def kernel(*refs):
        refs = list(refs)

        def take(n):
            return [refs.pop(0) for _ in range(n)]

        place_ref, weight_ref = take(2)
        piece_refs = take(len(slots.operands))
        block_ref, panel_ref, total_ref, rest_ref = take(4)
        if has_next:
            next_total_ref, parent_ref, next_diag_ref = take(3)
        take(len(after))
        if has_next:
            next_out_ref, next_rest_ref = take(2)
        out_refs = take(3) if packed else take(2)
        left_buf, x_buf, sums, diag_buf = take(4)
        assert not refs

        inner, my_row, pole = place_ref[0], place_ref[1], place_ref[2]
        first = place_ref[3].astype(F32)
        weight_real = weight_ref[0]
        weight_imag = weight_ref[1]

        for n in range(count):
            left_buf[:, n * 2 * height : (n + 1) * 2 * height] = slots.left(piece_refs, n, inner)

        late = mm(left_buf[...], block_ref[...].reshape(count * 2 * height, local))
        x = -(total_ref[...] + late)
        term = weight_real * x[width:] + weight_imag * x[:width]
        if packed:
            low, upper = term[:half], term[half:]
            mine = jnp.where(pole == 0, low, upper)
            sent = jnp.where(pole == 0, upper, low)
            for t in range(rows):
                columns = slice(t * height, (t + 1) * height)
                out_refs[0][t, :half, :] = mine[:, columns]
                out_refs[1 + 2 * t // rows][t % (rows // 2), :half, :] = sent[:, columns]
        else:
            out_refs[0][...] = term
        x_high, x_low = split(x)
        x_buf[:wide] = x_high
        x_buf[wide : 2 * wide] = x_low
        if has_next:
            x_buf[2 * wide :] = x_high
        for k in range(kinds):
            both = mm(x_buf[: 2 * wide], panel_ref[level + k].reshape(local, wide))
            sums[:, k * wide : (k + 1) * wide] = both[:wide] + both[wide:]
        if has_next:
            next_out_ref[...] = next_total_ref[...] + mm(parent_ref[level], x_buf[...])

        def complex_sum(k):
            at = k * wide
            real = sums[:width, at : at + width] - sums[width:, at + width : at + wide]
            imag = sums[:width, at + width : at + wide] + sums[width:, at : at + width]
            return real, imag

        own_real, own_imag = complex_sum(0)
        scale = first if level == 0 else 1.0
        y_real = rest_ref[0] * scale - own_real.T
        y_imag = rest_ref[1] * scale - own_imag.T
        diag_buf[...] = weight_real * y_imag + weight_imag * y_real
        if packed:
            for t in range(rows):
                places = ((out_refs[0], t, pole), (out_refs[1 + 2 * t // rows], t % (rows // 2), 1 - pole))
                for ref, n, side in places:
                    at = pl.multiple_of(side * half + (my_row ^ t) * part, part)
                    ref[n, half:, :] = diag_buf[pl.ds(at, part), :]
        else:
            out_refs[1][...] = diag_buf[...]
        if has_next:
            parent = parent_ref[level]
            parent_high, parent_low = parent[:, :wide], parent[:, 2 * wide :]
            follow_real, follow_imag = complex_sum(1)
            y_high, y_low = split(jnp.concatenate([y_real, y_imag], axis=1))
            mixed = mm_t(y_high, parent_high) + mm_t(y_low, parent_high) + mm_t(y_high, parent_low)
            z = -jnp.concatenate(
                [follow_real + mixed[:, :width], follow_imag + mixed[:, width:]], axis=0
            )
            z_high, z_low = split(z)
            back = mm(parent, jnp.concatenate([z_high, z_low, z_high], axis=0))
            next_rest_ref[0] = next_diag_ref[0] * first - back[:width]
            next_rest_ref[1] = next_diag_ref[1] * first - back[width:]

    operands = [place, weights] + slots.operands + [blocks, panels, total, rest]
    specs = [SCALARS, SCALARS] + [WHOLE] * (len(slots.operands) + 4)
    outs = []
    aliases = {}
    if has_next:
        aliases = {len(operands): 0}
        operands += [next_total, parents, next_diag]
        specs += [WHOLE] * 3
        outs += [
            jax.ShapeDtypeStruct((wide, local), F32),
            jax.ShapeDtypeStruct((2, width, width), F32),
        ]
    operands += after
    specs += [ANYWHERE] * len(after)
    if packed:
        outs.append(jax.ShapeDtypeStruct((rows, half + part, height), F32))
        outs += [jax.ShapeDtypeStruct((rows // 2, half + part, height), F32)] * 2
    else:
        outs += [
            jax.ShapeDtypeStruct((width, local), F32),
            jax.ShapeDtypeStruct((width, width), F32),
        ]
    return pl.pallas_call(
        kernel,
        out_shape=outs,
        in_specs=specs,
        out_specs=[WHOLE] * len(outs),
        input_output_aliases=aliases,
        scratch_shapes=[
            pltpu.VMEM((wide, count * 2 * height), BF16),
            pltpu.VMEM(((3 if has_next else 2) * wide, local), BF16),
            pltpu.VMEM((wide, kinds * wide), F32),
            pltpu.VMEM((width, width), F32),
        ],
        compiler_params=params(24),
        cost_estimate=large_cost(),
        name="level_%d" % level,
    )(*operands)


def cut(values, begin, after):
    count, height, width = len(values), values[0].shape[1] - begin, values[0].shape[2]

    def kernel(*refs):
        for n in range(count):
            refs[-1][n] = refs[n][0, begin:]

    return pl.pallas_call(
        kernel,
        out_shape=jax.ShapeDtypeStruct((count, height, width), F32),
        in_specs=[WHOLE] * count + [ANYWHERE] * len(after),
        out_specs=WHOLE,
        compiler_params=params(8),
        cost_estimate=small_cost(),
        name="cut",
    )(*values, *after)


def add_parts(kept, received):
    levels = len(kept)
    rows = kept[0].shape[0]

    def kernel(*refs):
        for k in range(levels):
            for t in range(rows):
                got = refs[levels + 2 * k + 2 * t // rows][t % (rows // 2)]
                refs[3 * levels + t][k] = refs[k][t] + got

    return pl.pallas_call(
        kernel,
        out_shape=[jax.ShapeDtypeStruct((levels,) + kept[0].shape[1:], F32)] * rows,
        in_specs=[WHOLE] * (3 * levels),
        out_specs=[WHOLE] * rows,
        compiler_params=params(12),
        cost_estimate=small_cost(),
        name="add_parts",
    )(*kept, *received)


def gather_four(piece, me, axis):
    inner = (me == 1) | (me == 2)
    pairs = [(0, 1), (1, 0), (2, 3), (3, 2)]
    middle_pairs = [(1, 2), (2, 1)]
    outer_pairs = [(1, 0), (2, 3)]
    owners = [
        me,
        me ^ 1,
        jnp.where(inner, 3 - me, me ^ 2),
        jnp.where(inner, (3 - me) ^ 1, me ^ 3),
    ]
    near = lax.ppermute(piece, axis, pairs)
    middles = [lax.ppermute(value, axis, middle_pairs) for value in (piece, near)]
    outers = [lax.ppermute(value, axis, outer_pairs) for value in middles]
    far = [[(middle, None), (outer, None)] for middle, outer in zip(middles, outers)]
    return owners, [[(piece, None)], [(near, None)]], far


def gather_line(piece, me, count, axis):
    owners, slots = [me], [[(piece, None)]]
    from_left = from_right = piece
    for step in range(1, count):
        from_left = lax.ppermute(from_left, axis, [(i, i + 1) for i in range(step - 1, count - 1)])
        from_right = lax.ppermute(from_right, axis, [(i, i - 1) for i in range(1, count - step + 1)])
        if 2 * step >= count:
            owners.append(jnp.clip(jnp.where(me >= step, me - step, me + step), 0, count - 1))
            slots.append([(jnp.where(me >= step, from_left, from_right), None)])
        else:
            owners += [jnp.maximum(me - step, 0), jnp.minimum(me + step, count - 1)]
            slots += [[(from_left, None)], [(from_right, None)]]
    return owners, slots[:1], slots[1:]


def gather_rows(value, near, far):
    first = exchange(value, "row", 4, near)
    second = exchange(value, "row", 4, far)
    third = exchange(first, "row", 4, far)
    found = {0: value, near: first, far: second, 3: third}
    return [(found[t], None) for t in range(4)]


def gather(piece, me, count, axis):
    if count == 4:
        return gather_four(piece, me, axis)
    return gather_line(piece, me, count, axis)


def make_per_device(sizes):
    poles, rows, cols = sizes

    def per_device(inverse_block, panels, panel_mask, parent_panels, diag_inverse, pole_weights):
        levels = panels.shape[1]
        height = panels.shape[5]
        width = panels.shape[6]
        half = width // 2
        part = half // rows
        packed = (
            poles == 2
            and rows & (rows - 1) == 0
            and cols & (cols - 1) == 0
            and height == width
            and height % 128 == 0
            and part % 8 == 0
        )
        my_pole = lax.axis_index("pole")
        my_row = lax.axis_index("row")
        my_col = lax.axis_index("col")
        first = ((my_row == 0) & (my_col == 0)).astype(jnp.int32)
        inner = ((my_col == 1) | (my_col == 2)).astype(jnp.int32)
        blocks = inverse_block[0, :, :, 0]
        local_panels = panels[0, :, :, 0, 0]
        flags = panel_mask[:, 0, 0]
        weights = pole_weights[0]
        flipped = (2, width, height)

        def masked(which, after):
            keep = bool(after)
            outs = [jax.ShapeDtypeStruct(flipped, BF16)] * len(which)
            if keep:
                outs += [jax.ShapeDtypeStruct((levels, height, width), BF16)] * 2
            return pl.pallas_call(
                functools.partial(mask_kernel, which, keep),
                out_shape=outs,
                in_specs=[FAR, FAR] + [ANYWHERE] * len(after),
                out_specs=[WHOLE] * len(outs),
                scratch_shapes=[
                    pltpu.VMEM((levels if keep else len(which),) + local_panels.shape[1:], BF16),
                    pltpu.SMEM((levels,), jnp.int32),
                    pltpu.SemaphoreType.DMA((2,)),
                ],
                compiler_params=params(8),
                cost_estimate=small_cost(),
                name="mask_rows" if keep else "mask",
            )(flags, local_panels, *after)

        pieces = list(masked([0], []))
        *more, kept_real, kept_imag = masked(list(range(1, levels)), pieces)
        pieces += more
        parents = pl.pallas_call(
            parent_kernel,
            out_shape=jax.ShapeDtypeStruct((levels - 1, 2 * width, 6 * width), BF16),
            in_specs=[WHOLE],
            out_specs=WHOLE,
            compiler_params=params(12),
            cost_estimate=small_cost(),
            name="parents",
        )(parent_panels[0])
        if packed and rows == 4:
            reals = gather_rows(kept_real, 1, 2)
            imags = gather_rows(kept_imag, 2, 1)
        elif packed:
            reals, imags = [
                [(value, None)]
                + [(exchange(value, "row", rows, t), None) for t in range(1, rows)]
                for value in (kept_real, kept_imag)
            ]
        else:
            reals, imags = [
                [(piece, None) for piece in lax.all_gather(value, "row")]
                for value in (kept_real, kept_imag)
            ]

        gathered = [gather(piece, my_col, cols, "col") for piece in pieces]

        def sum_rows(stack):
            return tree_sum([stack[0]] + [exchange(stack[t], "row", rows, t) for t in range(1, rows)])

        def spread(piece):
            whole = tree_sum([piece] + [exchange(piece, "col", cols, t) for t in range(1, cols)])
            whole = jnp.stack([whole] + [exchange(whole, "row", rows, t) for t in range(1, rows)])
            whole = xor_order(whole, my_row, rows)
            other = exchange(whole, "pole", 2, 1)
            return xor_order(jnp.stack([whole, other]), my_pole, 2)

        owners = gathered[0][0]
        place = jnp.stack(
            [jnp.asarray(v, jnp.int32) for v in [inner, my_row, my_pole, first] + owners]
        )
        late = len(gathered[0][2])
        *totals, late_blocks = early_products(
            rows,
            width,
            height,
            packed,
            place,
            [g[1] for g in gathered],
            late,
            blocks,
            [],
        )
        row_panels = pack_panels(levels, rows, width, height, packed, reals, imags)
        rest = diag_inverse[0, 0]
        panel_parts = []
        diag_parts = []
        kept = []
        received = []
        sums = []
        first_sum = []
        ordered = [slot[1][0] for g in gathered[1:] for slot in g[2] if len(slot) == 2]
        for level in range(levels):
            has_next = level + 1 < levels
            outs = level_products(
                rows,
                width,
                height,
                packed,
                level,
                place,
                weights,
                gathered[level][2],
                late_blocks,
                row_panels,
                totals[level],
                rest,
                totals[level + 1] if has_next else None,
                parents,
                diag_inverse[0, level + 1] if has_next else None,
                ordered if level == 0 else first_sum,
            )
            if has_next:
                totals[level + 1] = outs[0]
                rest = outs[1]
                outs = outs[2:]
            if packed:
                kept.append(outs[0])
                received += [exchange(value, "pole", 2, 1) for value in outs[1:]]
                parts = add_parts(kept, received)
                mine = sum_rows(parts)
                first_sum = [parts[0]]
                sums.append(mine)
                kept, received = [], []
            else:
                mine = lax.psum_scatter(outs[0], "row", scatter_dimension=1, tiled=True)
                mine = lax.psum_scatter(mine, "pole", scatter_dimension=0, tiled=True)
                panel_parts.append(mine.T)
                diag_parts.append(lax.psum(outs[1], ("pole", "row", "col")))
        if packed:
            panel_parts = [mine[0, :half].T for mine in sums]
            got = spread(cut(sums, half, []))
            diag_parts = [got[:, :, n].reshape(width, width) for n in range(levels)]
        return jnp.stack(panel_parts)[:, None, None], jnp.stack(diag_parts)

    return per_device


def solution(mesh):
    placed = (
        P("pole", None, None, "row", None, "col"),
        P("pole", None, None, "col", "row", None, None),
        P(None, "col", "row"),
        P("pole", None, None, None, None),
        P("pole", None, None, None, None),
        P("pole", None),
    )
    return jax.shard_map(
        make_per_device((mesh.shape["pole"], mesh.shape["row"], mesh.shape["col"])),
        mesh=mesh,
        in_specs=placed,
        out_specs=(P(None, "col", "row", None, "pole"), P()),
        check_vma=False,
    )
```

```python
import functools

import jax
import jax.numpy as jnp
from jax import lax
from jax.experimental import pallas as pl
from jax.experimental.pallas import tpu as pltpu
from jax.sharding import PartitionSpec as P

F32 = jnp.float32
BF16 = jnp.bfloat16
WHOLE = pl.BlockSpec(memory_space=pltpu.VMEM)
SCALARS = pl.BlockSpec(memory_space=pltpu.SMEM)
ANYWHERE = pl.BlockSpec(memory_space=pl.ANY)
FAR = pl.BlockSpec(memory_space=pltpu.HBM)


def params(mebibytes):
    return pltpu.CompilerParams(vmem_limit_bytes=mebibytes << 20)


def small_cost():
    return pl.CostEstimate(flops=1, bytes_accessed=1, transcendentals=0)


def large_cost():
    return pl.CostEstimate(flops=10**11, bytes_accessed=1, transcendentals=0)


def mm(left, right):
    return jnp.dot(left, right, preferred_element_type=F32)


def mm_t(left, right):
    return lax.dot_general(left, right, (((1,), (1,)), ((), ())), preferred_element_type=F32)


def split(value):
    high = value.astype(BF16)
    return high, (value - high.astype(F32)).astype(BF16)


def exchange(value, axes, count, distance):
    return lax.ppermute(value, axes, [(i, i ^ distance) for i in range(count)])


def tree_sum(values):
    while len(values) > 1:
        values = [values[i] + values[i + 1] for i in range(0, len(values), 2)]
    return values[0]


def xor_order(stack, me, count):
    bits = count.bit_length() - 1
    rest = stack.shape[1:]
    values = stack.reshape((2,) * bits + rest)
    for axis in range(bits):
        bit = (me >> (bits - 1 - axis)) & 1
        values = jnp.where(bit == 1, jnp.flip(values, axis), values)
    return values.reshape((count,) + rest)


def mask_kernel(levels, keep, flag_ref, panel_ref, *refs):
    refs = list(refs)
    if keep:
        refs.pop(0)
    out_refs = [refs.pop(0) for _ in levels]
    kept_refs = [refs.pop(0) for _ in range(2)] if keep else None
    buf, flags, sems = refs
    first = 0 if keep else levels[0]
    copies = [
        pltpu.make_async_copy(panel_ref.at[pl.ds(first, buf.shape[0])], buf, sems.at[0]),
        pltpu.make_async_copy(flag_ref, flags, sems.at[1]),
    ]
    for copy in copies:
        copy.start()
    for copy in copies:
        copy.wait()
    for k in range(buf.shape[0]):
        flag = flags[first + k].astype(F32)
        for part in range(2):
            value = buf[k, part].astype(F32) * flag
            if keep:
                kept_refs[part][k] = value.astype(BF16)
            if first + k in levels:
                out_refs[levels.index(first + k)][part] = value.T.astype(BF16)


def parent_kernel(parent_ref, out_ref):
    for k in range(parent_ref.shape[0]):
        real_high, real_low = split(parent_ref[k, 0].T)
        imag_high, imag_low = split(parent_ref[k, 1].T)
        high = left_block(real_high, imag_high)
        wide = high.shape[1]
        out_ref[k, :, :wide] = high
        out_ref[k, :, wide : 2 * wide] = high
        out_ref[k, :, 2 * wide :] = left_block(real_low, imag_low)


def left_block(real, imag):
    return jnp.concatenate(
        [jnp.concatenate([real, -imag], axis=1), jnp.concatenate([imag, real], axis=1)], axis=0
    )


class Slots:
    def __init__(self, slots):
        self.operands = []
        self.slots = []
        for slot in slots:
            self.slots.append([(self.place(array), index) for array, index in slot])

    def place(self, array):
        for n, operand in enumerate(self.operands):
            if operand is array:
                return n
        self.operands.append(array)
        return len(self.operands) - 1

    def left(self, refs, n, inner):
        parts = []
        for part in range(2):
            values = [
                refs[at][part] if index is None else refs[at][index, part]
                for at, index in self.slots[n]
            ]
            parts.append(values[0] if len(values) == 1 else jnp.where(inner == 1, *values))
        return left_block(*parts)


def block_copies(block_ref, buf, sem, owners, my_row, rows, height, ordered):
    copies = []
    for n, owner in enumerate(owners):
        if not ordered:
            copies.append([pltpu.make_async_copy(block_ref.at[:, owner], buf.at[n], sem.at[n, 0])])
            continue
        copies.append(
            [
                pltpu.make_async_copy(
                    block_ref.at[
                        :, owner, :, pl.ds(pl.multiple_of((my_row ^ t) * height, height), height)
                    ],
                    buf.at[n, :, :, pl.ds(t * height, height)],
                    sem.at[n, t],
                )
                for t in range(rows)
            ]
        )
    return copies


def early_products(rows, width, height, ordered, place, level_slots, late, blocks, after):
    levels = len(level_slots)
    count = len(level_slots[0])
    slots = Slots([slot for level in level_slots for slot in level])
    local = rows * height

    def kernel(place_ref, block_ref, *refs):
        piece_refs = refs[: len(slots.operands)]
        out_refs = refs[len(slots.operands) + len(after) :][:levels]
        late_ref, buf, left_buf, sem, late_sem = refs[-5:]
        my_row = place_ref[1]
        owners = [place_ref[4 + n] for n in range(count)]
        copies = block_copies(block_ref, buf, sem, owners, my_row, rows, height, ordered)
        owners = [place_ref[4 + count + n] for n in range(late)]
        late_copies = sum(
            block_copies(block_ref, late_ref, late_sem, owners, my_row, rows, height, ordered), []
        )
        for copy in sum(copies, []) + late_copies:
            copy.start()
        for level in range(levels):
            for n in range(count):
                left_buf[
                    level * 2 * width : (level + 1) * 2 * width,
                    n * 2 * height : (n + 1) * 2 * height,
                ] = slots.left(piece_refs, level * count + n, place_ref[0])
        for copy in sum(copies, []):
            copy.wait()
        right = buf[...].reshape(count * 2 * height, local)
        for level in range(levels):
            left = left_buf[level * 2 * width : (level + 1) * 2 * width, :]
            out_refs[level][...] = mm(left, right)
        for copy in late_copies:
            copy.wait()

    outs = [jax.ShapeDtypeStruct((2 * width, local), F32)] * levels
    outs.append(jax.ShapeDtypeStruct((late, 2, height, local), BF16))
    return pl.pallas_call(
        kernel,
        out_shape=outs,
        in_specs=[SCALARS, FAR] + [WHOLE] * len(slots.operands) + [ANYWHERE] * len(after),
        out_specs=[WHOLE] * len(outs),
        scratch_shapes=[
            pltpu.VMEM((count, 2, height, local), BF16),
            pltpu.VMEM((levels * 2 * width, count * 2 * height), BF16),
            pltpu.SemaphoreType.DMA((count, rows)),
            pltpu.SemaphoreType.DMA((late, rows)),
        ],
        compiler_params=params(24),
        cost_estimate=large_cost(),
        name="early",
    )(place, blocks, *slots.operands, *after)


def pack_panels(levels, rows, width, height, packed, reals, imags):
    chunks = rows if packed else 1
    chunk = height if packed else rows * height
    slots = Slots([reals, imags])

    def kernel(*refs):
        panel_refs = refs[: len(slots.operands)]
        out_ref, sem = refs[len(slots.operands) :]
        copies = []
        for p in range(2):
            for r in range(rows):
                at, index = slots.slots[p][r]
                source = panel_refs[at] if index is None else panel_refs[at].at[index]
                target = out_ref.at[
                    :, r if packed else 0,
                    pl.ds(0 if packed else r * height, height),
                    pl.ds(p * width, width),
                ]
                copies.append(pltpu.make_async_copy(source, target, sem.at[r, p]))
        for copy in copies:
            copy.start()
        for copy in copies:
            copy.wait()

    return pl.pallas_call(
        kernel,
        out_shape=jax.ShapeDtypeStruct((levels, chunks, chunk, 2 * width), BF16),
        in_specs=[ANYWHERE] * len(slots.operands),
        out_specs=WHOLE,
        scratch_shapes=[pltpu.SemaphoreType.DMA((rows, 2))],
        compiler_params=params(8),
        cost_estimate=large_cost(),
        name="pack_rows",
    )(*slots.operands)


def level_products(
    rows, width, height, packed, level, place, weights, level_slots, blocks, panels,
    total, rest, next_total, parents, next_diag, after,
):
    count = len(level_slots)
    slots = Slots(level_slots)
    has_next = next_total is not None
    local = rows * height
    half = width // 2
    part = half // rows
    wide = 2 * width
    kinds = 2 if has_next else 1

    def kernel(*refs):
        refs = list(refs)

        def take(n):
            return [refs.pop(0) for _ in range(n)]

        place_ref, weight_ref = take(2)
        piece_refs = take(len(slots.operands))
        block_ref, panel_ref, total_ref, rest_ref = take(4)
        if has_next:
            next_total_ref, parent_ref, next_diag_ref = take(3)
        take(len(after))
        if has_next:
            next_out_ref, next_rest_ref = take(2)
        out_refs = take(3) if packed else take(2)
        left_buf, x_buf, sums, diag_buf = take(4)
        assert not refs

        inner, my_row, pole = place_ref[0], place_ref[1], place_ref[2]
        first = place_ref[3].astype(F32)
        weight_real = weight_ref[0]
        weight_imag = weight_ref[1]

        for n in range(count):
            left_buf[:, n * 2 * height : (n + 1) * 2 * height] = slots.left(piece_refs, n, inner)

        late = mm(left_buf[...], block_ref[...].reshape(count * 2 * height, local))
        x = -(total_ref[...] + late)
        term = weight_real * x[width:] + weight_imag * x[:width]
        if packed:
            low, upper = term[:half], term[half:]
            mine = jnp.where(pole == 0, low, upper)
            sent = jnp.where(pole == 0, upper, low)
            for t in range(rows):
                columns = slice(t * height, (t + 1) * height)
                out_refs[0][t, :half, :] = mine[:, columns]
                out_refs[1 + 2 * t // rows][t % (rows // 2), :half, :] = sent[:, columns]
        else:
            out_refs[0][...] = term
        x_high, x_low = split(x)
        x_buf[:wide] = x_high
        x_buf[wide : 2 * wide] = x_low
        if has_next:
            x_buf[2 * wide :] = x_high
        for k in range(kinds):
            both = mm(x_buf[: 2 * wide], panel_ref[level + k].reshape(local, wide))
            sums[:, k * wide : (k + 1) * wide] = both[:wide] + both[wide:]
        if has_next:
            next_out_ref[...] = next_total_ref[...] + mm(parent_ref[level], x_buf[...])

        def complex_sum(k):
            at = k * wide
            real = sums[:width, at : at + width] - sums[width:, at + width : at + wide]
            imag = sums[:width, at + width : at + wide] + sums[width:, at : at + width]
            return real, imag

        own_real, own_imag = complex_sum(0)
        scale = first if level == 0 else 1.0
        y_real = rest_ref[0] * scale - own_real.T
        y_imag = rest_ref[1] * scale - own_imag.T
        diag_buf[...] = weight_real * y_imag + weight_imag * y_real
        if packed:
            for t in range(rows):
                places = ((out_refs[0], t, pole), (out_refs[1 + 2 * t // rows], t % (rows // 2), 1 - pole))
                for ref, n, side in places:
                    at = pl.multiple_of(side * half + (my_row ^ t) * part, part)
                    ref[n, half:, :] = diag_buf[pl.ds(at, part), :]
        else:
            out_refs[1][...] = diag_buf[...]
        if has_next:
            parent = parent_ref[level]
            parent_high, parent_low = parent[:, :wide], parent[:, 2 * wide :]
            follow_real, follow_imag = complex_sum(1)
            y_high, y_low = split(jnp.concatenate([y_real, y_imag], axis=1))
            mixed = mm_t(y_high, parent_high) + mm_t(y_low, parent_high) + mm_t(y_high, parent_low)
            z = -jnp.concatenate(
                [follow_real + mixed[:, :width], follow_imag + mixed[:, width:]], axis=0
            )
            z_high, z_low = split(z)
            back = mm(parent, jnp.concatenate([z_high, z_low, z_high], axis=0))
            next_rest_ref[0] = next_diag_ref[0] * first - back[:width]
            next_rest_ref[1] = next_diag_ref[1] * first - back[width:]

    operands = [place, weights] + slots.operands + [blocks, panels, total, rest]
    specs = [SCALARS, SCALARS] + [WHOLE] * (len(slots.operands) + 4)
    outs = []
    aliases = {}
    if has_next:
        aliases = {len(operands): 0}
        operands += [next_total, parents, next_diag]
        specs += [WHOLE] * 3
        outs += [
            jax.ShapeDtypeStruct((wide, local), F32),
            jax.ShapeDtypeStruct((2, width, width), F32),
        ]
    operands += after
    specs += [ANYWHERE] * len(after)
    if packed:
        outs.append(jax.ShapeDtypeStruct((rows, half + part, height), F32))
        outs += [jax.ShapeDtypeStruct((rows // 2, half + part, height), F32)] * 2
    else:
        outs += [
            jax.ShapeDtypeStruct((width, local), F32),
            jax.ShapeDtypeStruct((width, width), F32),
        ]
    return pl.pallas_call(
        kernel,
        out_shape=outs,
        in_specs=specs,
        out_specs=[WHOLE] * len(outs),
        input_output_aliases=aliases,
        scratch_shapes=[
            pltpu.VMEM((wide, count * 2 * height), BF16),
            pltpu.VMEM(((3 if has_next else 2) * wide, local), BF16),
            pltpu.VMEM((wide, kinds * wide), F32),
            pltpu.VMEM((width, width), F32),
        ],
        compiler_params=params(24),
        cost_estimate=large_cost(),
        name="level_%d" % level,
    )(*operands)


def join(values, after=()):
    def kernel(*refs):
        for n in range(len(values)):
            refs[-1][n] = refs[n][...]

    return pl.pallas_call(
        kernel,
        out_shape=jax.ShapeDtypeStruct((len(values),) + values[0].shape, values[0].dtype),
        in_specs=[WHOLE] * len(values) + [ANYWHERE] * len(after),
        out_specs=WHOLE,
        compiler_params=params(8),
        cost_estimate=small_cost(),
        name="join",
    )(*values, *after)


def cut(values, begin, after):
    count, height, width = len(values), values[0].shape[1] - begin, values[0].shape[2]

    def kernel(*refs):
        for n in range(count):
            refs[-1][n] = refs[n][0, begin:]

    return pl.pallas_call(
        kernel,
        out_shape=jax.ShapeDtypeStruct((count, height, width), F32),
        in_specs=[WHOLE] * count + [ANYWHERE] * len(after),
        out_specs=WHOLE,
        compiler_params=params(8),
        cost_estimate=small_cost(),
        name="cut",
    )(*values, *after)


def gate(values, after):
    count = len(values)
    return pl.pallas_call(
        lambda *refs: None,
        out_shape=[jax.ShapeDtypeStruct(value.shape, value.dtype) for value in values],
        in_specs=[ANYWHERE] * (count + len(after)),
        out_specs=[ANYWHERE] * count,
        input_output_aliases={n: n for n in range(count)},
        cost_estimate=small_cost(),
        name="gate",
    )(*values, *after)


def add_parts(kept, received):
    levels = len(kept)
    rows = kept[0].shape[0]

    def kernel(*refs):
        for k in range(levels):
            for t in range(rows):
                got = refs[levels + 2 * k + 2 * t // rows][t % (rows // 2)]
                refs[3 * levels + t][k] = refs[k][t] + got

    return pl.pallas_call(
        kernel,
        out_shape=[jax.ShapeDtypeStruct((levels,) + kept[0].shape[1:], F32)] * rows,
        in_specs=[WHOLE] * (3 * levels),
        out_specs=[WHOLE] * rows,
        compiler_params=params(12),
        cost_estimate=small_cost(),
        name="add_parts",
    )(*kept, *received)


def gather_four(piece, me, axis, after, held):
    inner = (me == 1) | (me == 2)
    pairs = [(0, 1), (1, 0), (2, 3), (3, 2)]
    middle_pairs = [(1, 2), (2, 1)]
    outer_pairs = [(1, 0), (2, 3)]
    owners = [
        me,
        me ^ 1,
        jnp.where(inner, 3 - me, me ^ 2),
        jnp.where(inner, (3 - me) ^ 1, me ^ 3),
    ]
    near = lax.ppermute(piece, axis, pairs)
    joined = join([piece, near], after + held)
    middle = lax.ppermute(joined, axis, middle_pairs)
    outer = lax.ppermute(middle, axis, outer_pairs)
    far = [[(middle, n), (outer, n)] for n in range(2)]
    after[:] = [joined]
    return owners, [[(piece, None)], [(near, None)]], far


def gather_line(piece, me, count, axis):
    owners, slots = [me], [[(piece, None)]]
    from_left = from_right = piece
    for step in range(1, count):
        from_left = lax.ppermute(from_left, axis, [(i, i + 1) for i in range(step - 1, count - 1)])
        from_right = lax.ppermute(from_right, axis, [(i, i - 1) for i in range(1, count - step + 1)])
        if 2 * step >= count:
            owners.append(jnp.clip(jnp.where(me >= step, me - step, me + step), 0, count - 1))
            slots.append([(jnp.where(me >= step, from_left, from_right), None)])
        else:
            owners += [jnp.maximum(me - step, 0), jnp.minimum(me + step, count - 1)]
            slots += [[(from_left, None)], [(from_right, None)]]
    return owners, slots[:1], slots[1:]


def gather_rows(value, near, far):
    first = exchange(value, "row", 4, near)
    joined = join([value, first])
    second = exchange(joined, "row", 4, far)
    found = {0: (value, None), near: (first, None), far: (second, 0), 3: (second, 1)}
    return [found[t] for t in range(4)], first, joined


def gather(piece, me, count, axis, after, held):
    if count == 4:
        return gather_four(piece, me, axis, after, held)
    return gather_line(piece, me, count, axis)


def make_per_device(sizes):
    poles, rows, cols = sizes

    def per_device(inverse_block, panels, panel_mask, parent_panels, diag_inverse, pole_weights):
        levels = panels.shape[1]
        height = panels.shape[5]
        width = panels.shape[6]
        half = width // 2
        part = half // rows
        packed = (
            poles == 2
            and rows & (rows - 1) == 0
            and cols & (cols - 1) == 0
            and height == width
            and height % 128 == 0
            and part % 8 == 0
        )
        my_pole = lax.axis_index("pole")
        my_row = lax.axis_index("row")
        my_col = lax.axis_index("col")
        first = ((my_row == 0) & (my_col == 0)).astype(jnp.int32)
        inner = ((my_col == 1) | (my_col == 2)).astype(jnp.int32)
        blocks = inverse_block[0, :, :, 0]
        local_panels = panels[0, :, :, 0, 0]
        flags = panel_mask[:, 0, 0]
        weights = pole_weights[0]
        flipped = (2, width, height)

        def masked(which, after):
            keep = bool(after)
            outs = [jax.ShapeDtypeStruct(flipped, BF16)] * len(which)
            if keep:
                outs += [jax.ShapeDtypeStruct((levels, height, width), BF16)] * 2
            return pl.pallas_call(
                functools.partial(mask_kernel, which, keep),
                out_shape=outs,
                in_specs=[FAR, FAR] + [ANYWHERE] * len(after),
                out_specs=[WHOLE] * len(outs),
                scratch_shapes=[
                    pltpu.VMEM((levels if keep else len(which),) + local_panels.shape[1:], BF16),
                    pltpu.SMEM((levels,), jnp.int32),
                    pltpu.SemaphoreType.DMA((2,)),
                ],
                compiler_params=params(8),
                cost_estimate=small_cost(),
                name="mask_rows" if keep else "mask",
            )(flags, local_panels, *after)

        pieces = list(masked([0], []))
        *more, kept_real, kept_imag = masked(list(range(1, levels)), pieces)
        pieces += more
        parents = pl.pallas_call(
            parent_kernel,
            out_shape=jax.ShapeDtypeStruct((levels - 1, 2 * width, 6 * width), BF16),
            in_specs=[WHOLE],
            out_specs=WHOLE,
            compiler_params=params(12),
            cost_estimate=small_cost(),
            name="parents",
        )(parent_panels[0])
        held = [[] for _ in pieces]
        if packed and rows == 4:
            reals, *steps_real = gather_rows(kept_real, 1, 2)
            imags, *steps_imag = gather_rows(kept_imag, 2, 1)
            held[1] = [steps_real[0], steps_imag[0]]
            held[2] = [steps_real[1], steps_imag[1]]
        elif packed:
            reals, imags = [
                [(value, None)]
                + [(exchange(value, "row", rows, t), None) for t in range(1, rows)]
                for value in (kept_real, kept_imag)
            ]
        else:
            reals, imags = [
                [(piece, None) for piece in lax.all_gather(value, "row")]
                for value in (kept_real, kept_imag)
            ]

        after = []
        gathered = []
        for k, piece in enumerate(pieces):
            gathered.append(gather(piece, my_col, cols, "col", after, held[k]))

        def sum_rows(stack):
            return tree_sum([stack[0]] + [exchange(stack[t], "row", rows, t) for t in range(1, rows)])

        def spread(piece):
            whole = tree_sum([piece] + [exchange(piece, "col", cols, t) for t in range(1, cols)])
            whole = jnp.stack([whole] + [exchange(whole, "row", rows, t) for t in range(1, rows)])
            whole = xor_order(whole, my_row, rows)
            other = exchange(whole, "pole", 2, 1)
            return xor_order(jnp.stack([whole, other]), my_pole, 2)

        owners = gathered[0][0]
        place = jnp.stack(
            [jnp.asarray(v, jnp.int32) for v in [inner, my_row, my_pole, first] + owners]
        )
        late = len(gathered[0][2])
        *totals, late_blocks = early_products(
            rows,
            width,
            height,
            packed,
            place,
            [g[1] for g in gathered],
            late,
            blocks,
            [g[2][0][0][0] for g in gathered[:-1] if len(g[2][0]) == 2],
        )
        row_panels = pack_panels(levels, rows, width, height, packed, reals, imags)
        rest = diag_inverse[0, 0]
        panel_parts = []
        diag_parts = []
        kept = []
        received = []
        sums = []
        first_sum = []
        far_ordered = [s[1][0] for s in gathered[-1][2][:1] if len(s) == 2]
        ordered = [g[2][0][0][0] for g in gathered[1:-1] if len(g[2][0]) == 2]
        for level in range(levels):
            has_next = level + 1 < levels
            outs = level_products(
                rows,
                width,
                height,
                packed,
                level,
                place,
                weights,
                gathered[level][2],
                late_blocks,
                row_panels,
                totals[level],
                rest,
                totals[level + 1] if has_next else None,
                parents,
                diag_inverse[0, level + 1] if has_next else None,
                ordered if level == 0 else first_sum,
            )
            if has_next:
                totals[level + 1] = outs[0]
                rest = outs[1]
                outs = outs[2:]
            if packed:
                kept.append(outs[0])
                sent = outs[1:] if has_next else gate(outs[1:], sums)
                received += [exchange(value, "pole", 2, 1) for value in sent]
                parts = add_parts(kept, received)
                mine = sum_rows(parts)
                first_sum = [parts[0]]
                sums.append(mine)
                kept, received = [], []
            else:
                mine = lax.psum_scatter(outs[0], "row", scatter_dimension=1, tiled=True)
                mine = lax.psum_scatter(mine, "pole", scatter_dimension=0, tiled=True)
                panel_parts.append(mine.T)
                diag_parts.append(lax.psum(outs[1], ("pole", "row", "col")))
        if packed:
            panel_parts = [mine[0, :half].T for mine in sums]
            for group, held_back in ((sums[:-1], first_sum), (sums[-1:], [])):
                got = spread(cut(group, half, held_back))
                diag_parts += [got[:, :, n].reshape(width, width) for n in range(len(group))]
        return jnp.stack(panel_parts)[:, None, None], jnp.stack(diag_parts)

    return per_device


def solution(mesh):
    placed = (
        P("pole", None, None, "row", None, "col"),
        P("pole", None, None, "col", "row", None, None),
        P(None, "col", "row"),
        P("pole", None, None, None, None),
        P("pole", None, None, None, None),
        P("pole", None),
    )
    return jax.shard_map(
        make_per_device((mesh.shape["pole"], mesh.shape["row"], mesh.shape["col"])),
        mesh=mesh,
        in_specs=placed,
        out_specs=(P(None, "col", "row", None, "pole"), P()),
        check_vma=False,
    )
```

```python
import functools

import jax
import jax.numpy as jnp
from jax import lax
from jax.experimental import pallas as pl
from jax.experimental.pallas import tpu as pltpu
from jax.sharding import PartitionSpec as P

F32 = jnp.float32
BF16 = jnp.bfloat16
WHOLE = pl.BlockSpec(memory_space=pltpu.VMEM)
SCALARS = pl.BlockSpec(memory_space=pltpu.SMEM)
ANYWHERE = pl.BlockSpec(memory_space=pl.ANY)
FAR = pl.BlockSpec(memory_space=pltpu.HBM)


def params(mebibytes):
    return pltpu.CompilerParams(vmem_limit_bytes=mebibytes << 20)


def small_cost():
    return pl.CostEstimate(flops=1, bytes_accessed=1, transcendentals=0)


def large_cost():
    return pl.CostEstimate(flops=10**11, bytes_accessed=1, transcendentals=0)


def mm(left, right):
    return jnp.dot(left, right, preferred_element_type=F32)


def mm_t(left, right):
    return lax.dot_general(left, right, (((1,), (1,)), ((), ())), preferred_element_type=F32)


def split(value):
    high = value.astype(BF16)
    return high, (value - high.astype(F32)).astype(BF16)


def exchange(value, axes, count, distance):
    return lax.ppermute(value, axes, [(i, i ^ distance) for i in range(count)])


def tree_sum(values):
    while len(values) > 1:
        values = [values[i] + values[i + 1] for i in range(0, len(values), 2)]
    return values[0]


def xor_order(stack, me, count):
    bits = count.bit_length() - 1
    rest = stack.shape[1:]
    values = stack.reshape((2,) * bits + rest)
    for axis in range(bits):
        bit = (me >> (bits - 1 - axis)) & 1
        values = jnp.where(bit == 1, jnp.flip(values, axis), values)
    return values.reshape((count,) + rest)


def mask_kernel(levels, keep, flag_ref, panel_ref, *refs):
    refs = list(refs)
    if keep:
        refs.pop(0)
    out_refs = [refs.pop(0) for _ in levels]
    kept_refs = [refs.pop(0) for _ in range(2)] if keep else None
    buf, flags, sems = refs
    first = 0 if keep else levels[0]
    copies = [
        pltpu.make_async_copy(panel_ref.at[pl.ds(first, buf.shape[0])], buf, sems.at[0]),
        pltpu.make_async_copy(flag_ref, flags, sems.at[1]),
    ]
    for copy in copies:
        copy.start()
    for copy in copies:
        copy.wait()
    for k in range(buf.shape[0]):
        flag = flags[first + k].astype(F32)
        for part in range(2):
            value = buf[k, part].astype(F32) * flag
            if keep:
                kept_refs[part][k] = value.astype(BF16)
            if first + k in levels:
                out_refs[levels.index(first + k)][part] = value.T.astype(BF16)


def parent_kernel(parent_ref, out_ref):
    for k in range(parent_ref.shape[0]):
        real_high, real_low = split(parent_ref[k, 0].T)
        imag_high, imag_low = split(parent_ref[k, 1].T)
        high = left_block(real_high, imag_high)
        wide = high.shape[1]
        out_ref[k, :, :wide] = high
        out_ref[k, :, wide : 2 * wide] = high
        out_ref[k, :, 2 * wide :] = left_block(real_low, imag_low)


def left_block(real, imag):
    return jnp.concatenate(
        [jnp.concatenate([real, -imag], axis=1), jnp.concatenate([imag, real], axis=1)], axis=0
    )


class Slots:
    def __init__(self, slots):
        self.operands = []
        self.slots = []
        for slot in slots:
            self.slots.append([(self.place(array), index) for array, index in slot])

    def place(self, array):
        for n, operand in enumerate(self.operands):
            if operand is array:
                return n
        self.operands.append(array)
        return len(self.operands) - 1

    def left(self, refs, n, inner):
        parts = []
        for part in range(2):
            values = [
                refs[at][part] if index is None else refs[at][index, part]
                for at, index in self.slots[n]
            ]
            parts.append(values[0] if len(values) == 1 else jnp.where(inner == 1, *values))
        return left_block(*parts)


def block_copies(block_ref, buf, sem, owners, my_row, rows, height, ordered):
    copies = []
    for n, owner in enumerate(owners):
        if not ordered:
            copies.append([pltpu.make_async_copy(block_ref.at[:, owner], buf.at[n], sem.at[n, 0])])
            continue
        copies.append(
            [
                pltpu.make_async_copy(
                    block_ref.at[
                        :, owner, :, pl.ds(pl.multiple_of((my_row ^ t) * height, height), height)
                    ],
                    buf.at[n, :, :, pl.ds(t * height, height)],
                    sem.at[n, t],
                )
                for t in range(rows)
            ]
        )
    return copies


def early_products(rows, width, height, ordered, place, level_slots, late, blocks, after):
    levels = len(level_slots)
    count = len(level_slots[0])
    slots = Slots([slot for level in level_slots for slot in level])
    local = rows * height

    def kernel(place_ref, block_ref, *refs):
        piece_refs = refs[: len(slots.operands)]
        out_refs = refs[len(slots.operands) + len(after) :][:levels]
        late_ref, buf, left_buf, sem, late_sem = refs[-5:]
        my_row = place_ref[1]
        owners = [place_ref[4 + n] for n in range(count)]
        copies = block_copies(block_ref, buf, sem, owners, my_row, rows, height, ordered)
        owners = [place_ref[4 + count + n] for n in range(late)]
        late_copies = sum(
            block_copies(block_ref, late_ref, late_sem, owners, my_row, rows, height, ordered), []
        )
        for copy in sum(copies, []) + late_copies:
            copy.start()
        for level in range(levels):
            for n in range(count):
                left_buf[
                    level * 2 * width : (level + 1) * 2 * width,
                    n * 2 * height : (n + 1) * 2 * height,
                ] = slots.left(piece_refs, level * count + n, place_ref[0])
        for copy in sum(copies, []):
            copy.wait()
        right = buf[...].reshape(count * 2 * height, local)
        for level in range(levels):
            left = left_buf[level * 2 * width : (level + 1) * 2 * width, :]
            out_refs[level][...] = mm(left, right)
        for copy in late_copies:
            copy.wait()

    outs = [jax.ShapeDtypeStruct((2 * width, local), F32)] * levels
    outs.append(jax.ShapeDtypeStruct((late, 2, height, local), BF16))
    return pl.pallas_call(
        kernel,
        out_shape=outs,
        in_specs=[SCALARS, FAR] + [WHOLE] * len(slots.operands) + [ANYWHERE] * len(after),
        out_specs=[WHOLE] * len(outs),
        scratch_shapes=[
            pltpu.VMEM((count, 2, height, local), BF16),
            pltpu.VMEM((levels * 2 * width, count * 2 * height), BF16),
            pltpu.SemaphoreType.DMA((count, rows)),
            pltpu.SemaphoreType.DMA((late, rows)),
        ],
        compiler_params=params(24),
        cost_estimate=large_cost(),
        name="early",
    )(place, blocks, *slots.operands, *after)


def pack_panels(levels, rows, width, height, packed, reals, imags):
    chunks = rows if packed else 1
    chunk = height if packed else rows * height
    slots = Slots([reals, imags])

    def kernel(*refs):
        panel_refs = refs[: len(slots.operands)]
        out_ref, sem = refs[len(slots.operands) :]
        copies = []
        for p in range(2):
            for r in range(rows):
                at, index = slots.slots[p][r]
                source = panel_refs[at] if index is None else panel_refs[at].at[index]
                target = out_ref.at[
                    :, r if packed else 0,
                    pl.ds(0 if packed else r * height, height),
                    pl.ds(p * width, width),
                ]
                copies.append(pltpu.make_async_copy(source, target, sem.at[r, p]))
        for copy in copies:
            copy.start()
        for copy in copies:
            copy.wait()

    return pl.pallas_call(
        kernel,
        out_shape=jax.ShapeDtypeStruct((levels, chunks, chunk, 2 * width), BF16),
        in_specs=[ANYWHERE] * len(slots.operands),
        out_specs=WHOLE,
        scratch_shapes=[pltpu.SemaphoreType.DMA((rows, 2))],
        compiler_params=params(8),
        cost_estimate=large_cost(),
        name="pack_rows",
    )(*slots.operands)


def level_products(
    rows, width, height, packed, level, place, weights, level_slots, blocks, panels,
    total, rest, next_total, parents, next_diag, after,
):
    count = len(level_slots)
    slots = Slots(level_slots)
    has_next = next_total is not None
    local = rows * height
    half = width // 2
    part = half // rows
    wide = 2 * width
    kinds = 2 if has_next else 1

    def kernel(*refs):
        refs = list(refs)

        def take(n):
            return [refs.pop(0) for _ in range(n)]

        place_ref, weight_ref = take(2)
        piece_refs = take(len(slots.operands))
        block_ref, panel_ref, total_ref, rest_ref = take(4)
        if has_next:
            next_total_ref, parent_ref, next_diag_ref = take(3)
        take(len(after))
        if has_next:
            next_out_ref, next_rest_ref = take(2)
        out_refs = take(3) if packed else take(2)
        left_buf, x_buf, sums, diag_buf = take(4)
        assert not refs

        inner, my_row, pole = place_ref[0], place_ref[1], place_ref[2]
        first = place_ref[3].astype(F32)
        weight_real = weight_ref[0]
        weight_imag = weight_ref[1]

        for n in range(count):
            left_buf[:, n * 2 * height : (n + 1) * 2 * height] = slots.left(piece_refs, n, inner)

        late = mm(left_buf[...], block_ref[...].reshape(count * 2 * height, local))
        x = -(total_ref[...] + late)
        term = weight_real * x[width:] + weight_imag * x[:width]
        if packed:
            low, upper = term[:half], term[half:]
            mine = jnp.where(pole == 0, low, upper)
            sent = jnp.where(pole == 0, upper, low)
            for t in range(rows):
                columns = slice(t * height, (t + 1) * height)
                out_refs[0][t, :half, :] = mine[:, columns]
                out_refs[1 + 2 * t // rows][t % (rows // 2), :half, :] = sent[:, columns]
        else:
            out_refs[0][...] = term
        x_high, x_low = split(x)
        x_buf[:wide] = x_high
        x_buf[wide : 2 * wide] = x_low
        if has_next:
            x_buf[2 * wide :] = x_high
        for k in range(kinds):
            both = mm(x_buf[: 2 * wide], panel_ref[level + k].reshape(local, wide))
            sums[:, k * wide : (k + 1) * wide] = both[:wide] + both[wide:]
        if has_next:
            next_out_ref[...] = next_total_ref[...] + mm(parent_ref[level], x_buf[...])

        def complex_sum(k):
            at = k * wide
            real = sums[:width, at : at + width] - sums[width:, at + width : at + wide]
            imag = sums[:width, at + width : at + wide] + sums[width:, at : at + width]
            return real, imag

        own_real, own_imag = complex_sum(0)
        scale = first if level == 0 else 1.0
        y_real = rest_ref[0] * scale - own_real.T
        y_imag = rest_ref[1] * scale - own_imag.T
        diag_buf[...] = weight_real * y_imag + weight_imag * y_real
        if packed:
            for t in range(rows):
                places = ((out_refs[0], t, pole), (out_refs[1 + 2 * t // rows], t % (rows // 2), 1 - pole))
                for ref, n, side in places:
                    at = pl.multiple_of(side * half + (my_row ^ t) * part, part)
                    ref[n, half:, :] = diag_buf[pl.ds(at, part), :]
        else:
            out_refs[1][...] = diag_buf[...]
        if has_next:
            parent = parent_ref[level]
            parent_high, parent_low = parent[:, :wide], parent[:, 2 * wide :]
            follow_real, follow_imag = complex_sum(1)
            y_high, y_low = split(jnp.concatenate([y_real, y_imag], axis=1))
            mixed = mm_t(y_high, parent_high) + mm_t(y_low, parent_high) + mm_t(y_high, parent_low)
            z = -jnp.concatenate(
                [follow_real + mixed[:, :width], follow_imag + mixed[:, width:]], axis=0
            )
            z_high, z_low = split(z)
            back = mm(parent, jnp.concatenate([z_high, z_low, z_high], axis=0))
            next_rest_ref[0] = next_diag_ref[0] * first - back[:width]
            next_rest_ref[1] = next_diag_ref[1] * first - back[width:]

    operands = [place, weights] + slots.operands + [blocks, panels, total, rest]
    specs = [SCALARS, SCALARS] + [WHOLE] * (len(slots.operands) + 4)
    outs = []
    aliases = {}
    if has_next:
        aliases = {len(operands): 0}
        operands += [next_total, parents, next_diag]
        specs += [WHOLE] * 3
        outs += [
            jax.ShapeDtypeStruct((wide, local), F32),
            jax.ShapeDtypeStruct((2, width, width), F32),
        ]
    operands += after
    specs += [ANYWHERE] * len(after)
    if packed:
        outs.append(jax.ShapeDtypeStruct((rows, half + part, height), F32))
        outs += [jax.ShapeDtypeStruct((rows // 2, half + part, height), F32)] * 2
    else:
        outs += [
            jax.ShapeDtypeStruct((width, local), F32),
            jax.ShapeDtypeStruct((width, width), F32),
        ]
    return pl.pallas_call(
        kernel,
        out_shape=outs,
        in_specs=specs,
        out_specs=[WHOLE] * len(outs),
        input_output_aliases=aliases,
        scratch_shapes=[
            pltpu.VMEM((wide, count * 2 * height), BF16),
            pltpu.VMEM(((3 if has_next else 2) * wide, local), BF16),
            pltpu.VMEM((wide, kinds * wide), F32),
            pltpu.VMEM((width, width), F32),
        ],
        compiler_params=params(24),
        cost_estimate=large_cost(),
        name="level_%d" % level,
    )(*operands)


def join(values, after=()):
    def kernel(*refs):
        for n in range(len(values)):
            refs[-1][n] = refs[n][...]

    return pl.pallas_call(
        kernel,
        out_shape=jax.ShapeDtypeStruct((len(values),) + values[0].shape, values[0].dtype),
        in_specs=[WHOLE] * len(values) + [ANYWHERE] * len(after),
        out_specs=WHOLE,
        compiler_params=params(8),
        cost_estimate=small_cost(),
        name="join",
    )(*values, *after)


def cut(values, begin, after):
    count, height, width = len(values), values[0].shape[1] - begin, values[0].shape[2]

    def kernel(*refs):
        for n in range(count):
            refs[-1][n] = refs[n][0, begin:]

    return pl.pallas_call(
        kernel,
        out_shape=jax.ShapeDtypeStruct((count, height, width), F32),
        in_specs=[WHOLE] * count + [ANYWHERE] * len(after),
        out_specs=WHOLE,
        compiler_params=params(8),
        cost_estimate=small_cost(),
        name="cut",
    )(*values, *after)


def gate(values, after):
    count = len(values)

    def kernel(*refs):
        for n in range(count):
            refs[n - count][...] = refs[n][...]

    return pl.pallas_call(
        kernel,
        out_shape=[jax.ShapeDtypeStruct(value.shape, value.dtype) for value in values],
        in_specs=[WHOLE] * count + [ANYWHERE] * len(after),
        out_specs=[WHOLE] * count,
        compiler_params=params(8),
        cost_estimate=small_cost(),
        name="gate",
    )(*values, *after)


def add_parts(kept, received):
    levels = len(kept)
    rows = kept[0].shape[0]

    def kernel(*refs):
        for k in range(levels):
            for t in range(rows):
                got = refs[levels + 2 * k + 2 * t // rows][t % (rows // 2)]
                refs[3 * levels + t][k] = refs[k][t] + got

    return pl.pallas_call(
        kernel,
        out_shape=[jax.ShapeDtypeStruct((levels,) + kept[0].shape[1:], F32)] * rows,
        in_specs=[WHOLE] * (3 * levels),
        out_specs=[WHOLE] * rows,
        compiler_params=params(12),
        cost_estimate=small_cost(),
        name="add_parts",
    )(*kept, *received)


def gather_four(piece, me, axis, after, held):
    inner = (me == 1) | (me == 2)
    pairs = [(0, 1), (1, 0), (2, 3), (3, 2)]
    middle_pairs = [(1, 2), (2, 1)]
    outer_pairs = [(1, 0), (2, 3)]
    owners = [
        me,
        me ^ 1,
        jnp.where(inner, 3 - me, me ^ 2),
        jnp.where(inner, (3 - me) ^ 1, me ^ 3),
    ]
    near = lax.ppermute(piece, axis, pairs)
    joined = join([piece, near], after + held)
    middle = lax.ppermute(joined, axis, middle_pairs)
    outer = lax.ppermute(middle, axis, outer_pairs)
    far = [[(middle, n), (outer, n)] for n in range(2)]
    after[:] = [joined]
    return owners, [[(piece, None)], [(near, None)]], far


def gather_line(piece, me, count, axis):
    owners, slots = [me], [[(piece, None)]]
    from_left = from_right = piece
    for step in range(1, count):
        from_left = lax.ppermute(from_left, axis, [(i, i + 1) for i in range(step - 1, count - 1)])
        from_right = lax.ppermute(from_right, axis, [(i, i - 1) for i in range(1, count - step + 1)])
        if 2 * step >= count:
            owners.append(jnp.clip(jnp.where(me >= step, me - step, me + step), 0, count - 1))
            slots.append([(jnp.where(me >= step, from_left, from_right), None)])
        else:
            owners += [jnp.maximum(me - step, 0), jnp.minimum(me + step, count - 1)]
            slots += [[(from_left, None)], [(from_right, None)]]
    return owners, slots[:1], slots[1:]


def gather_rows(value, near, far):
    first = exchange(value, "row", 4, near)
    joined = join([value, first])
    second = exchange(joined, "row", 4, far)
    found = {0: (value, None), near: (first, None), far: (second, 0), 3: (second, 1)}
    return [found[t] for t in range(4)], first, joined


def gather(piece, me, count, axis, after, held):
    if count == 4:
        return gather_four(piece, me, axis, after, held)
    return gather_line(piece, me, count, axis)


def make_per_device(sizes):
    poles, rows, cols = sizes

    def per_device(inverse_block, panels, panel_mask, parent_panels, diag_inverse, pole_weights):
        levels = panels.shape[1]
        height = panels.shape[5]
        width = panels.shape[6]
        half = width // 2
        part = half // rows
        packed = (
            poles == 2
            and rows & (rows - 1) == 0
            and cols & (cols - 1) == 0
            and height == width
            and height % 128 == 0
            and part % 8 == 0
        )
        my_pole = lax.axis_index("pole")
        my_row = lax.axis_index("row")
        my_col = lax.axis_index("col")
        first = ((my_row == 0) & (my_col == 0)).astype(jnp.int32)
        inner = ((my_col == 1) | (my_col == 2)).astype(jnp.int32)
        blocks = inverse_block[0, :, :, 0]
        local_panels = panels[0, :, :, 0, 0]
        flags = panel_mask[:, 0, 0]
        weights = pole_weights[0]
        flipped = (2, width, height)

        def masked(which, after):
            keep = bool(after)
            outs = [jax.ShapeDtypeStruct(flipped, BF16)] * len(which)
            if keep:
                outs += [jax.ShapeDtypeStruct((levels, height, width), BF16)] * 2
            return pl.pallas_call(
                functools.partial(mask_kernel, which, keep),
                out_shape=outs,
                in_specs=[FAR, FAR] + [ANYWHERE] * len(after),
                out_specs=[WHOLE] * len(outs),
                scratch_shapes=[
                    pltpu.VMEM((levels if keep else len(which),) + local_panels.shape[1:], BF16),
                    pltpu.SMEM((levels,), jnp.int32),
                    pltpu.SemaphoreType.DMA((2,)),
                ],
                compiler_params=params(8),
                cost_estimate=small_cost(),
                name="mask_rows" if keep else "mask",
            )(flags, local_panels, *after)

        pieces = list(masked([0], []))
        *more, kept_real, kept_imag = masked(list(range(1, levels)), pieces)
        pieces += more
        parents = pl.pallas_call(
            parent_kernel,
            out_shape=jax.ShapeDtypeStruct((levels - 1, 2 * width, 6 * width), BF16),
            in_specs=[WHOLE],
            out_specs=WHOLE,
            compiler_params=params(12),
            cost_estimate=small_cost(),
            name="parents",
        )(parent_panels[0])
        held = [[] for _ in pieces]
        if packed and rows == 4:
            reals, *steps_real = gather_rows(kept_real, 1, 2)
            imags, *steps_imag = gather_rows(kept_imag, 2, 1)
            held[1] = [steps_real[0], steps_imag[0]]
            held[2] = [steps_real[1], steps_imag[1]]
        elif packed:
            reals, imags = [
                [(value, None)]
                + [(exchange(value, "row", rows, t), None) for t in range(1, rows)]
                for value in (kept_real, kept_imag)
            ]
        else:
            reals, imags = [
                [(piece, None) for piece in lax.all_gather(value, "row")]
                for value in (kept_real, kept_imag)
            ]

        after = []
        gathered = []
        for k, piece in enumerate(pieces):
            gathered.append(gather(piece, my_col, cols, "col", after, held[k]))

        def sum_rows(stack):
            return tree_sum([stack[0]] + [exchange(stack[t], "row", rows, t) for t in range(1, rows)])

        def spread(piece):
            whole = tree_sum([piece] + [exchange(piece, "col", cols, t) for t in range(1, cols)])
            whole = jnp.stack([whole] + [exchange(whole, "row", rows, t) for t in range(1, rows)])
            whole = xor_order(whole, my_row, rows)
            other = exchange(whole, "pole", 2, 1)
            return xor_order(jnp.stack([whole, other]), my_pole, 2)

        owners = gathered[0][0]
        place = jnp.stack(
            [jnp.asarray(v, jnp.int32) for v in [inner, my_row, my_pole, first] + owners]
        )
        late = len(gathered[0][2])
        *totals, late_blocks = early_products(
            rows,
            width,
            height,
            packed,
            place,
            [g[1] for g in gathered],
            late,
            blocks,
            [g[2][0][0][0] for g in gathered[:-1] if len(g[2][0]) == 2],
        )
        row_panels = pack_panels(levels, rows, width, height, packed, reals, imags)
        rest = diag_inverse[0, 0]
        panel_parts = []
        diag_parts = []
        kept = []
        received = []
        sums = []
        first_sum = []
        far_ordered = [s[1][0] for s in gathered[-1][2][:1] if len(s) == 2]
        ordered = [g[2][0][0][0] for g in gathered[1:-1] if len(g[2][0]) == 2]
        for level in range(levels):
            has_next = level + 1 < levels
            outs = level_products(
                rows,
                width,
                height,
                packed,
                level,
                place,
                weights,
                gathered[level][2],
                late_blocks,
                row_panels,
                totals[level],
                rest,
                totals[level + 1] if has_next else None,
                parents,
                diag_inverse[0, level + 1] if has_next else None,
                ordered if level == 0 else first_sum,
            )
            if has_next:
                totals[level + 1] = outs[0]
                rest = outs[1]
                outs = outs[2:]
            if packed:
                kept.append(outs[0])
                sent = outs[1:] if has_next else gate(outs[1:], sums)
                received += [exchange(value, "pole", 2, 1) for value in sent]
                parts = add_parts(kept, received)
                mine = sum_rows(parts)
                first_sum = [parts[0]]
                sums.append(mine)
                kept, received = [], []
            else:
                mine = lax.psum_scatter(outs[0], "row", scatter_dimension=1, tiled=True)
                mine = lax.psum_scatter(mine, "pole", scatter_dimension=0, tiled=True)
                panel_parts.append(mine.T)
                diag_parts.append(lax.psum(outs[1], ("pole", "row", "col")))
        if packed:
            panel_parts = [mine[0, :half].T for mine in sums]
            got = spread(cut(sums, half, []))
            diag_parts = [got[:, :, n].reshape(width, width) for n in range(levels)]
        return jnp.stack(panel_parts)[:, None, None], jnp.stack(diag_parts)

    return per_device


def solution(mesh):
    placed = (
        P("pole", None, None, "row", None, "col"),
        P("pole", None, None, "col", "row", None, None),
        P(None, "col", "row"),
        P("pole", None, None, None, None),
        P("pole", None, None, None, None),
        P("pole", None),
    )
    return jax.shard_map(
        make_per_device((mesh.shape["pole"], mesh.shape["row"], mesh.shape["col"])),
        mesh=mesh,
        in_specs=placed,
        out_specs=(P(None, "col", "row", None, "pole"), P()),
        check_vma=False,
    )
```

```python
import functools

import jax
import jax.numpy as jnp
from jax import lax
from jax.experimental import pallas as pl
from jax.experimental.pallas import tpu as pltpu
from jax.sharding import PartitionSpec as P

F32 = jnp.float32
BF16 = jnp.bfloat16
WHOLE = pl.BlockSpec(memory_space=pltpu.VMEM)
SCALARS = pl.BlockSpec(memory_space=pltpu.SMEM)
ANYWHERE = pl.BlockSpec(memory_space=pl.ANY)
FAR = pl.BlockSpec(memory_space=pltpu.HBM)


def params(mebibytes):
    return pltpu.CompilerParams(vmem_limit_bytes=mebibytes << 20)


def small_cost():
    return pl.CostEstimate(flops=1, bytes_accessed=1, transcendentals=0)


def large_cost():
    return pl.CostEstimate(flops=10**11, bytes_accessed=1, transcendentals=0)


def mm(left, right):
    return jnp.dot(left, right, preferred_element_type=F32)


def mm_t(left, right):
    return lax.dot_general(left, right, (((1,), (1,)), ((), ())), preferred_element_type=F32)


def split(value):
    high = value.astype(BF16)
    return high, (value - high.astype(F32)).astype(BF16)


def exchange(value, axes, count, distance):
    return lax.ppermute(value, axes, [(i, i ^ distance) for i in range(count)])


def tree_sum(values):
    while len(values) > 1:
        values = [values[i] + values[i + 1] for i in range(0, len(values), 2)]
    return values[0]


def xor_order(stack, me, count):
    bits = count.bit_length() - 1
    rest = stack.shape[1:]
    values = stack.reshape((2,) * bits + rest)
    for axis in range(bits):
        bit = (me >> (bits - 1 - axis)) & 1
        values = jnp.where(bit == 1, jnp.flip(values, axis), values)
    return values.reshape((count,) + rest)


def mask_kernel(levels, keep, flag_ref, panel_ref, *refs):
    refs = list(refs)
    if keep:
        refs.pop(0)
    out_refs = [refs.pop(0) for _ in levels]
    kept_refs = [refs.pop(0) for _ in range(2)] if keep else None
    buf, flags, sems = refs
    first = 0 if keep else levels[0]
    copies = [
        pltpu.make_async_copy(panel_ref.at[pl.ds(first, buf.shape[0])], buf, sems.at[0]),
        pltpu.make_async_copy(flag_ref, flags, sems.at[1]),
    ]
    for copy in copies:
        copy.start()
    for copy in copies:
        copy.wait()
    for k in range(buf.shape[0]):
        flag = flags[first + k].astype(F32)
        for part in range(2):
            value = buf[k, part].astype(F32) * flag
            if keep:
                kept_refs[part][k] = value.astype(BF16)
            if first + k in levels:
                out_refs[levels.index(first + k)][part] = value.T.astype(BF16)


def parent_kernel(parent_ref, out_ref):
    for k in range(parent_ref.shape[0]):
        real_high, real_low = split(parent_ref[k, 0].T)
        imag_high, imag_low = split(parent_ref[k, 1].T)
        high = left_block(real_high, imag_high)
        wide = high.shape[1]
        out_ref[k, :, :wide] = high
        out_ref[k, :, wide : 2 * wide] = high
        out_ref[k, :, 2 * wide :] = left_block(real_low, imag_low)


def left_block(real, imag):
    return jnp.concatenate(
        [jnp.concatenate([real, -imag], axis=1), jnp.concatenate([imag, real], axis=1)], axis=0
    )


class Slots:
    def __init__(self, slots):
        self.operands = []
        self.slots = []
        for slot in slots:
            self.slots.append([(self.place(array), index) for array, index in slot])

    def place(self, array):
        for n, operand in enumerate(self.operands):
            if operand is array:
                return n
        self.operands.append(array)
        return len(self.operands) - 1

    def left(self, refs, n, inner):
        parts = []
        for part in range(2):
            values = [
                refs[at][part] if index is None else refs[at][index, part]
                for at, index in self.slots[n]
            ]
            parts.append(values[0] if len(values) == 1 else jnp.where(inner == 1, *values))
        return left_block(*parts)


def block_copies(block_ref, buf, sem, owners, my_row, rows, height, ordered):
    copies = []
    for n, owner in enumerate(owners):
        if not ordered:
            copies.append([pltpu.make_async_copy(block_ref.at[:, owner], buf.at[n], sem.at[n, 0])])
            continue
        copies.append(
            [
                pltpu.make_async_copy(
                    block_ref.at[
                        :, owner, :, pl.ds(pl.multiple_of((my_row ^ t) * height, height), height)
                    ],
                    buf.at[n, :, :, pl.ds(t * height, height)],
                    sem.at[n, t],
                )
                for t in range(rows)
            ]
        )
    return copies


def early_products(rows, width, height, ordered, place, level_slots, late, blocks, after):
    levels = len(level_slots)
    count = len(level_slots[0])
    slots = Slots([slot for level in level_slots for slot in level])
    local = rows * height

    def kernel(place_ref, block_ref, *refs):
        piece_refs = refs[: len(slots.operands)]
        out_refs = refs[len(slots.operands) + len(after) :][:levels]
        late_ref, buf, left_buf, sem, late_sem = refs[-5:]
        my_row = place_ref[1]
        owners = [place_ref[4 + n] for n in range(count)]
        copies = block_copies(block_ref, buf, sem, owners, my_row, rows, height, ordered)
        owners = [place_ref[4 + count + n] for n in range(late)]
        late_copies = sum(
            block_copies(block_ref, late_ref, late_sem, owners, my_row, rows, height, ordered), []
        )
        for copy in sum(copies, []) + late_copies:
            copy.start()
        for level in range(levels):
            for n in range(count):
                left_buf[
                    level * 2 * width : (level + 1) * 2 * width,
                    n * 2 * height : (n + 1) * 2 * height,
                ] = slots.left(piece_refs, level * count + n, place_ref[0])
        for copy in sum(copies, []):
            copy.wait()
        right = buf[...].reshape(count * 2 * height, local)
        for level in range(levels):
            left = left_buf[level * 2 * width : (level + 1) * 2 * width, :]
            out_refs[level][...] = mm(left, right)
        for copy in late_copies:
            copy.wait()

    outs = [jax.ShapeDtypeStruct((2 * width, local), F32)] * levels
    outs.append(jax.ShapeDtypeStruct((late, 2, height, local), BF16))
    return pl.pallas_call(
        kernel,
        out_shape=outs,
        in_specs=[SCALARS, FAR] + [WHOLE] * len(slots.operands) + [ANYWHERE] * len(after),
        out_specs=[WHOLE] * len(outs),
        scratch_shapes=[
            pltpu.VMEM((count, 2, height, local), BF16),
            pltpu.VMEM((levels * 2 * width, count * 2 * height), BF16),
            pltpu.SemaphoreType.DMA((count, rows)),
            pltpu.SemaphoreType.DMA((late, rows)),
        ],
        compiler_params=params(24),
        cost_estimate=large_cost(),
        name="early",
    )(place, blocks, *slots.operands, *after)


def pack_panels(levels, rows, width, height, packed, reals, imags):
    chunks = rows if packed else 1
    chunk = height if packed else rows * height
    slots = Slots([reals, imags])

    def kernel(*refs):
        panel_refs = refs[: len(slots.operands)]
        out_ref, sem = refs[len(slots.operands) :]
        copies = []
        for p in range(2):
            for r in range(rows):
                at, index = slots.slots[p][r]
                source = panel_refs[at] if index is None else panel_refs[at].at[index]
                target = out_ref.at[
                    :, r if packed else 0,
                    pl.ds(0 if packed else r * height, height),
                    pl.ds(p * width, width),
                ]
                copies.append(pltpu.make_async_copy(source, target, sem.at[r, p]))
        for copy in copies:
            copy.start()
        for copy in copies:
            copy.wait()

    return pl.pallas_call(
        kernel,
        out_shape=jax.ShapeDtypeStruct((levels, chunks, chunk, 2 * width), BF16),
        in_specs=[ANYWHERE] * len(slots.operands),
        out_specs=WHOLE,
        scratch_shapes=[pltpu.SemaphoreType.DMA((rows, 2))],
        compiler_params=params(8),
        cost_estimate=large_cost(),
        name="pack_rows",
    )(*slots.operands)


def level_products(
    rows, width, height, packed, level, place, weights, level_slots, blocks, panels,
    total, rest, next_total, parents, next_diag, after,
):
    count = len(level_slots)
    slots = Slots(level_slots)
    has_next = next_total is not None
    local = rows * height
    half = width // 2
    part = half // rows
    wide = 2 * width
    kinds = 2 if has_next else 1

    def kernel(*refs):
        refs = list(refs)

        def take(n):
            return [refs.pop(0) for _ in range(n)]

        place_ref, weight_ref = take(2)
        piece_refs = take(len(slots.operands))
        block_ref, panel_ref, total_ref, rest_ref = take(4)
        if has_next:
            next_total_ref, parent_ref, next_diag_ref = take(3)
        take(len(after))
        if has_next:
            next_out_ref, next_rest_ref = take(2)
        out_refs = take(3) if packed else take(2)
        left_buf, x_buf, sums, diag_buf = take(4)
        assert not refs

        inner, my_row, pole = place_ref[0], place_ref[1], place_ref[2]
        first = place_ref[3].astype(F32)
        weight_real = weight_ref[0]
        weight_imag = weight_ref[1]

        for n in range(count):
            left_buf[:, n * 2 * height : (n + 1) * 2 * height] = slots.left(piece_refs, n, inner)

        late = mm(left_buf[...], block_ref[...].reshape(count * 2 * height, local))
        x = -(total_ref[...] + late)
        term = weight_real * x[width:] + weight_imag * x[:width]
        if packed:
            low, upper = term[:half], term[half:]
            mine = jnp.where(pole == 0, low, upper)
            sent = jnp.where(pole == 0, upper, low)
            for t in range(rows):
                columns = slice(t * height, (t + 1) * height)
                out_refs[0][t, :half, :] = mine[:, columns]
                out_refs[1 + 2 * t // rows][t % (rows // 2), :half, :] = sent[:, columns]
        else:
            out_refs[0][...] = term
        x_high, x_low = split(x)
        x_buf[:wide] = x_high
        x_buf[wide : 2 * wide] = x_low
        if has_next:
            x_buf[2 * wide :] = x_high
        for k in range(kinds):
            both = mm(x_buf[: 2 * wide], panel_ref[level + k].reshape(local, wide))
            sums[:, k * wide : (k + 1) * wide] = both[:wide] + both[wide:]
        if has_next:
            next_out_ref[...] = next_total_ref[...] + mm(parent_ref[level], x_buf[...])

        def complex_sum(k):
            at = k * wide
            real = sums[:width, at : at + width] - sums[width:, at + width : at + wide]
            imag = sums[:width, at + width : at + wide] + sums[width:, at : at + width]
            return real, imag

        own_real, own_imag = complex_sum(0)
        scale = first if level == 0 else 1.0
        y_real = rest_ref[0] * scale - own_real.T
        y_imag = rest_ref[1] * scale - own_imag.T
        diag_buf[...] = weight_real * y_imag + weight_imag * y_real
        if packed:
            for t in range(rows):
                places = ((out_refs[0], t, pole), (out_refs[1 + 2 * t // rows], t % (rows // 2), 1 - pole))
                for ref, n, side in places:
                    at = pl.multiple_of(side * half + (my_row ^ t) * part, part)
                    ref[n, half:, :] = diag_buf[pl.ds(at, part), :]
        else:
            out_refs[1][...] = diag_buf[...]
        if has_next:
            parent = parent_ref[level]
            parent_high, parent_low = parent[:, :wide], parent[:, 2 * wide :]
            follow_real, follow_imag = complex_sum(1)
            y_high, y_low = split(jnp.concatenate([y_real, y_imag], axis=1))
            mixed = mm_t(y_high, parent_high) + mm_t(y_low, parent_high) + mm_t(y_high, parent_low)
            z = -jnp.concatenate(
                [follow_real + mixed[:, :width], follow_imag + mixed[:, width:]], axis=0
            )
            z_high, z_low = split(z)
            back = mm(parent, jnp.concatenate([z_high, z_low, z_high], axis=0))
            next_rest_ref[0] = next_diag_ref[0] * first - back[:width]
            next_rest_ref[1] = next_diag_ref[1] * first - back[width:]

    operands = [place, weights] + slots.operands + [blocks, panels, total, rest]
    specs = [SCALARS, SCALARS] + [WHOLE] * (len(slots.operands) + 4)
    outs = []
    aliases = {}
    if has_next:
        aliases = {len(operands): 0}
        operands += [next_total, parents, next_diag]
        specs += [WHOLE] * 3
        outs += [
            jax.ShapeDtypeStruct((wide, local), F32),
            jax.ShapeDtypeStruct((2, width, width), F32),
        ]
    operands += after
    specs += [ANYWHERE] * len(after)
    if packed:
        outs.append(jax.ShapeDtypeStruct((rows, half + part, height), F32))
        outs += [jax.ShapeDtypeStruct((rows // 2, half + part, height), F32)] * 2
    else:
        outs += [
            jax.ShapeDtypeStruct((width, local), F32),
            jax.ShapeDtypeStruct((width, width), F32),
        ]
    return pl.pallas_call(
        kernel,
        out_shape=outs,
        in_specs=specs,
        out_specs=[WHOLE] * len(outs),
        input_output_aliases=aliases,
        scratch_shapes=[
            pltpu.VMEM((wide, count * 2 * height), BF16),
            pltpu.VMEM(((3 if has_next else 2) * wide, local), BF16),
            pltpu.VMEM((wide, kinds * wide), F32),
            pltpu.VMEM((width, width), F32),
        ],
        compiler_params=params(24),
        cost_estimate=large_cost(),
        name="level_%d" % level,
    )(*operands)


def join(values, after=()):
    def kernel(*refs):
        for n in range(len(values)):
            refs[-1][n] = refs[n][...]

    return pl.pallas_call(
        kernel,
        out_shape=jax.ShapeDtypeStruct((len(values),) + values[0].shape, values[0].dtype),
        in_specs=[WHOLE] * len(values) + [ANYWHERE] * len(after),
        out_specs=WHOLE,
        compiler_params=params(8),
        cost_estimate=small_cost(),
        name="join",
    )(*values, *after)


def cut(values, begin, after):
    count, height, width = len(values), values[0].shape[1] - begin, values[0].shape[2]

    def kernel(*refs):
        for n in range(count):
            refs[-1][n] = refs[n][0, begin:]

    return pl.pallas_call(
        kernel,
        out_shape=jax.ShapeDtypeStruct((count, height, width), F32),
        in_specs=[WHOLE] * count + [ANYWHERE] * len(after),
        out_specs=WHOLE,
        compiler_params=params(8),
        cost_estimate=small_cost(),
        name="cut",
    )(*values, *after)


def gate(values, after):
    count = len(values)

    def kernel(*refs):
        for n in range(count):
            refs[n - count][...] = refs[n][...]

    return pl.pallas_call(
        kernel,
        out_shape=[jax.ShapeDtypeStruct(value.shape, value.dtype) for value in values],
        in_specs=[WHOLE] * count + [ANYWHERE] * len(after),
        out_specs=[WHOLE] * count,
        compiler_params=params(8),
        cost_estimate=small_cost(),
        name="gate",
    )(*values, *after)


def add_parts(kept, received):
    levels = len(kept)
    rows = kept[0].shape[0]

    def kernel(*refs):
        for k in range(levels):
            for t in range(rows):
                got = refs[levels + 2 * k + 2 * t // rows][t % (rows // 2)]
                refs[3 * levels + t][k] = refs[k][t] + got

    return pl.pallas_call(
        kernel,
        out_shape=[jax.ShapeDtypeStruct((levels,) + kept[0].shape[1:], F32)] * rows,
        in_specs=[WHOLE] * (3 * levels),
        out_specs=[WHOLE] * rows,
        compiler_params=params(12),
        cost_estimate=small_cost(),
        name="add_parts",
    )(*kept, *received)


def gather_four(piece, me, axis, after, held):
    inner = (me == 1) | (me == 2)
    pairs = [(0, 1), (1, 0), (2, 3), (3, 2)]
    middle_pairs = [(1, 2), (2, 1)]
    outer_pairs = [(1, 0), (2, 3)]
    owners = [
        me,
        me ^ 1,
        jnp.where(inner, 3 - me, me ^ 2),
        jnp.where(inner, (3 - me) ^ 1, me ^ 3),
    ]
    near = lax.ppermute(piece, axis, pairs)
    joined = join([piece, near], after + held)
    middle = lax.ppermute(joined, axis, middle_pairs)
    outer = lax.ppermute(middle, axis, outer_pairs)
    far = [[(middle, n), (outer, n)] for n in range(2)]
    after[:] = [joined]
    return owners, [[(piece, None)], [(near, None)]], far


def gather_line(piece, me, count, axis):
    owners, slots = [me], [[(piece, None)]]
    from_left = from_right = piece
    for step in range(1, count):
        from_left = lax.ppermute(from_left, axis, [(i, i + 1) for i in range(step - 1, count - 1)])
        from_right = lax.ppermute(from_right, axis, [(i, i - 1) for i in range(1, count - step + 1)])
        if 2 * step >= count:
            owners.append(jnp.clip(jnp.where(me >= step, me - step, me + step), 0, count - 1))
            slots.append([(jnp.where(me >= step, from_left, from_right), None)])
        else:
            owners += [jnp.maximum(me - step, 0), jnp.minimum(me + step, count - 1)]
            slots += [[(from_left, None)], [(from_right, None)]]
    return owners, slots[:1], slots[1:]


def gather_rows(value, near, far):
    first = exchange(value, "row", 4, near)
    joined = join([value, first])
    second = exchange(joined, "row", 4, far)
    found = {0: (value, None), near: (first, None), far: (second, 0), 3: (second, 1)}
    return [found[t] for t in range(4)], first, joined


def gather(piece, me, count, axis, after, held):
    if count == 4:
        return gather_four(piece, me, axis, after, held)
    return gather_line(piece, me, count, axis)


def make_per_device(sizes):
    poles, rows, cols = sizes

    def per_device(inverse_block, panels, panel_mask, parent_panels, diag_inverse, pole_weights):
        levels = panels.shape[1]
        height = panels.shape[5]
        width = panels.shape[6]
        half = width // 2
        part = half // rows
        packed = (
            poles == 2
            and rows & (rows - 1) == 0
            and cols & (cols - 1) == 0
            and height == width
            and height % 128 == 0
            and part % 8 == 0
        )
        my_pole = lax.axis_index("pole")
        my_row = lax.axis_index("row")
        my_col = lax.axis_index("col")
        first = ((my_row == 0) & (my_col == 0)).astype(jnp.int32)
        inner = ((my_col == 1) | (my_col == 2)).astype(jnp.int32)
        blocks = inverse_block[0, :, :, 0]
        local_panels = panels[0, :, :, 0, 0]
        flags = panel_mask[:, 0, 0]
        weights = pole_weights[0]
        flipped = (2, width, height)

        def masked(which, after):
            keep = bool(after)
            outs = [jax.ShapeDtypeStruct(flipped, BF16)] * len(which)
            if keep:
                outs += [jax.ShapeDtypeStruct((levels, height, width), BF16)] * 2
            return pl.pallas_call(
                functools.partial(mask_kernel, which, keep),
                out_shape=outs,
                in_specs=[FAR, FAR] + [ANYWHERE] * len(after),
                out_specs=[WHOLE] * len(outs),
                scratch_shapes=[
                    pltpu.VMEM((levels if keep else len(which),) + local_panels.shape[1:], BF16),
                    pltpu.SMEM((levels,), jnp.int32),
                    pltpu.SemaphoreType.DMA((2,)),
                ],
                compiler_params=params(8),
                cost_estimate=small_cost(),
                name="mask_rows" if keep else "mask",
            )(flags, local_panels, *after)

        pieces = list(masked([0], []))
        *more, kept_real, kept_imag = masked(list(range(1, levels)), pieces)
        pieces += more
        parents = pl.pallas_call(
            parent_kernel,
            out_shape=jax.ShapeDtypeStruct((levels - 1, 2 * width, 6 * width), BF16),
            in_specs=[WHOLE],
            out_specs=WHOLE,
            compiler_params=params(12),
            cost_estimate=small_cost(),
            name="parents",
        )(parent_panels[0])
        held = [[] for _ in pieces]
        if packed and rows == 4:
            reals, *steps_real = gather_rows(kept_real, 1, 2)
            imags, *steps_imag = gather_rows(kept_imag, 2, 1)
            held[1] = [steps_real[0], steps_imag[0]]
            held[2] = [steps_real[1], steps_imag[1]]
        elif packed:
            reals, imags = [
                [(value, None)]
                + [(exchange(value, "row", rows, t), None) for t in range(1, rows)]
                for value in (kept_real, kept_imag)
            ]
        else:
            reals, imags = [
                [(piece, None) for piece in lax.all_gather(value, "row")]
                for value in (kept_real, kept_imag)
            ]

        after = []
        gathered = []
        for k, piece in enumerate(pieces):
            gathered.append(gather(piece, my_col, cols, "col", after, held[k]))

        def sum_rows(stack):
            return tree_sum([stack[0]] + [exchange(stack[t], "row", rows, t) for t in range(1, rows)])

        def spread(piece):
            whole = tree_sum([piece] + [exchange(piece, "col", cols, t) for t in range(1, cols)])
            whole = jnp.stack([whole] + [exchange(whole, "row", rows, t) for t in range(1, rows)])
            whole = xor_order(whole, my_row, rows)
            other = exchange(whole, "pole", 2, 1)
            return xor_order(jnp.stack([whole, other]), my_pole, 2)

        owners = gathered[0][0]
        place = jnp.stack(
            [jnp.asarray(v, jnp.int32) for v in [inner, my_row, my_pole, first] + owners]
        )
        late = len(gathered[0][2])
        *totals, late_blocks = early_products(
            rows,
            width,
            height,
            packed,
            place,
            [g[1] for g in gathered],
            late,
            blocks,
            [g[2][0][0][0] for g in gathered[:1] if len(g[2][0]) == 2],
        )
        row_panels = pack_panels(levels, rows, width, height, packed, reals, imags)
        rest = diag_inverse[0, 0]
        panel_parts = []
        diag_parts = []
        kept = []
        received = []
        sums = []
        first_sum = []
        far_ordered = [s[1][0] for s in gathered[-1][2][:1] if len(s) == 2]
        ordered = [g[2][0][0][0] for g in gathered[1:-1] if len(g[2][0]) == 2]
        for level in range(levels):
            has_next = level + 1 < levels
            outs = level_products(
                rows,
                width,
                height,
                packed,
                level,
                place,
                weights,
                gathered[level][2],
                late_blocks,
                row_panels,
                totals[level],
                rest,
                totals[level + 1] if has_next else None,
                parents,
                diag_inverse[0, level + 1] if has_next else None,
                ordered if level == 0 else first_sum,
            )
            if has_next:
                totals[level + 1] = outs[0]
                rest = outs[1]
                outs = outs[2:]
            if packed:
                kept.append(outs[0])
                sent = outs[1:] if has_next else gate(outs[1:], sums)
                received += [exchange(value, "pole", 2, 1) for value in sent]
                parts = add_parts(kept, received)
                mine = sum_rows(parts)
                first_sum = [parts[0]]
                sums.append(mine)
                kept, received = [], []
            else:
                mine = lax.psum_scatter(outs[0], "row", scatter_dimension=1, tiled=True)
                mine = lax.psum_scatter(mine, "pole", scatter_dimension=0, tiled=True)
                panel_parts.append(mine.T)
                diag_parts.append(lax.psum(outs[1], ("pole", "row", "col")))
        if packed:
            panel_parts = [mine[0, :half].T for mine in sums]
            got = spread(cut(sums, half, []))
            diag_parts = [got[:, :, n].reshape(width, width) for n in range(levels)]
        return jnp.stack(panel_parts)[:, None, None], jnp.stack(diag_parts)

    return per_device


def solution(mesh):
    placed = (
        P("pole", None, None, "row", None, "col"),
        P("pole", None, None, "col", "row", None, None),
        P(None, "col", "row"),
        P("pole", None, None, None, None),
        P("pole", None, None, None, None),
        P("pole", None),
    )
    return jax.shard_map(
        make_per_device((mesh.shape["pole"], mesh.shape["row"], mesh.shape["col"])),
        mesh=mesh,
        in_specs=placed,
        out_specs=(P(None, "col", "row", None, "pole"), P()),
        check_vma=False,
    )
```

```python
import functools

import jax
import jax.numpy as jnp
from jax import lax
from jax.experimental import pallas as pl
from jax.experimental.pallas import tpu as pltpu
from jax.sharding import PartitionSpec as P

F32 = jnp.float32
BF16 = jnp.bfloat16
WHOLE = pl.BlockSpec(memory_space=pltpu.VMEM)
SCALARS = pl.BlockSpec(memory_space=pltpu.SMEM)
ANYWHERE = pl.BlockSpec(memory_space=pl.ANY)
FAR = pl.BlockSpec(memory_space=pltpu.HBM)


def params(mebibytes):
    return pltpu.CompilerParams(vmem_limit_bytes=mebibytes << 20)


def small_cost():
    return pl.CostEstimate(flops=1, bytes_accessed=1, transcendentals=0)


def large_cost():
    return pl.CostEstimate(flops=10**11, bytes_accessed=1, transcendentals=0)


def mm(left, right):
    return jnp.dot(left, right, preferred_element_type=F32)


def mm_t(left, right):
    return lax.dot_general(left, right, (((1,), (1,)), ((), ())), preferred_element_type=F32)


def split(value):
    high = value.astype(BF16)
    return high, (value - high.astype(F32)).astype(BF16)


def exchange(value, axes, count, distance):
    return lax.ppermute(value, axes, [(i, i ^ distance) for i in range(count)])


def tree_sum(values):
    while len(values) > 1:
        values = [values[i] + values[i + 1] for i in range(0, len(values), 2)]
    return values[0]


def xor_order(stack, me, count):
    bits = count.bit_length() - 1
    rest = stack.shape[1:]
    values = stack.reshape((2,) * bits + rest)
    for axis in range(bits):
        bit = (me >> (bits - 1 - axis)) & 1
        values = jnp.where(bit == 1, jnp.flip(values, axis), values)
    return values.reshape((count,) + rest)


def mask_kernel(levels, keep, flag_ref, panel_ref, *refs):
    refs = list(refs)
    if keep:
        refs.pop(0)
    out_refs = [refs.pop(0) for _ in levels]
    kept_refs = [refs.pop(0) for _ in range(2)] if keep else None
    buf, flags, sems = refs
    first = 0 if keep else levels[0]
    copies = [
        pltpu.make_async_copy(panel_ref.at[pl.ds(first, buf.shape[0])], buf, sems.at[0]),
        pltpu.make_async_copy(flag_ref, flags, sems.at[1]),
    ]
    for copy in copies:
        copy.start()
    for copy in copies:
        copy.wait()
    for k in range(buf.shape[0]):
        flag = flags[first + k].astype(F32)
        for part in range(2):
            value = buf[k, part].astype(F32) * flag
            if keep:
                kept_refs[part][k] = value.astype(BF16)
            if first + k in levels:
                out_refs[levels.index(first + k)][part] = value.T.astype(BF16)


def parent_kernel(parent_ref, out_ref):
    for k in range(parent_ref.shape[0]):
        real_high, real_low = split(parent_ref[k, 0].T)
        imag_high, imag_low = split(parent_ref[k, 1].T)
        high = left_block(real_high, imag_high)
        wide = high.shape[1]
        out_ref[k, :, :wide] = high
        out_ref[k, :, wide : 2 * wide] = high
        out_ref[k, :, 2 * wide :] = left_block(real_low, imag_low)


def left_block(real, imag):
    return jnp.concatenate(
        [jnp.concatenate([real, -imag], axis=1), jnp.concatenate([imag, real], axis=1)], axis=0
    )


class Slots:
    def __init__(self, slots):
        self.operands = []
        self.slots = []
        for slot in slots:
            self.slots.append([(self.place(array), index) for array, index in slot])

    def place(self, array):
        for n, operand in enumerate(self.operands):
            if operand is array:
                return n
        self.operands.append(array)
        return len(self.operands) - 1

    def left(self, refs, n, inner):
        parts = []
        for part in range(2):
            values = [
                refs[at][part] if index is None else refs[at][index, part]
                for at, index in self.slots[n]
            ]
            parts.append(values[0] if len(values) == 1 else jnp.where(inner == 1, *values))
        return left_block(*parts)


def block_copies(block_ref, buf, sem, owners, my_row, rows, height, ordered):
    copies = []
    for n, owner in enumerate(owners):
        if not ordered:
            copies.append([pltpu.make_async_copy(block_ref.at[:, owner], buf.at[n], sem.at[n, 0])])
            continue
        copies.append(
            [
                pltpu.make_async_copy(
                    block_ref.at[
                        :, owner, :, pl.ds(pl.multiple_of((my_row ^ t) * height, height), height)
                    ],
                    buf.at[n, :, :, pl.ds(t * height, height)],
                    sem.at[n, t],
                )
                for t in range(rows)
            ]
        )
    return copies


def early_products(rows, width, height, ordered, place, level_slots, late, blocks, after):
    levels = len(level_slots)
    count = len(level_slots[0])
    slots = Slots([slot for level in level_slots for slot in level])
    local = rows * height

    def kernel(place_ref, block_ref, *refs):
        piece_refs = refs[: len(slots.operands)]
        out_refs = refs[len(slots.operands) + len(after) :][:levels]
        late_ref, buf, left_buf, sem, late_sem = refs[-5:]
        my_row = place_ref[1]
        owners = [place_ref[4 + n] for n in range(count)]
        copies = block_copies(block_ref, buf, sem, owners, my_row, rows, height, ordered)
        owners = [place_ref[4 + count + n] for n in range(late)]
        late_copies = sum(
            block_copies(block_ref, late_ref, late_sem, owners, my_row, rows, height, ordered), []
        )
        for copy in sum(copies, []) + late_copies:
            copy.start()
        for level in range(levels):
            for n in range(count):
                left_buf[
                    level * 2 * width : (level + 1) * 2 * width,
                    n * 2 * height : (n + 1) * 2 * height,
                ] = slots.left(piece_refs, level * count + n, place_ref[0])
        for copy in sum(copies, []):
            copy.wait()
        right = buf[...].reshape(count * 2 * height, local)
        for level in range(levels):
            left = left_buf[level * 2 * width : (level + 1) * 2 * width, :]
            out_refs[level][...] = mm(left, right)
        for copy in late_copies:
            copy.wait()

    outs = [jax.ShapeDtypeStruct((2 * width, local), F32)] * levels
    outs.append(jax.ShapeDtypeStruct((late, 2, height, local), BF16))
    return pl.pallas_call(
        kernel,
        out_shape=outs,
        in_specs=[SCALARS, FAR] + [WHOLE] * len(slots.operands) + [ANYWHERE] * len(after),
        out_specs=[WHOLE] * len(outs),
        scratch_shapes=[
            pltpu.VMEM((count, 2, height, local), BF16),
            pltpu.VMEM((levels * 2 * width, count * 2 * height), BF16),
            pltpu.SemaphoreType.DMA((count, rows)),
            pltpu.SemaphoreType.DMA((late, rows)),
        ],
        compiler_params=params(24),
        cost_estimate=large_cost(),
        name="early",
    )(place, blocks, *slots.operands, *after)


def pack_panels(levels, rows, width, height, packed, reals, imags):
    chunks = rows if packed else 1
    chunk = height if packed else rows * height
    slots = Slots([reals, imags])

    def kernel(*refs):
        panel_refs = refs[: len(slots.operands)]
        out_ref, sem = refs[len(slots.operands) :]
        copies = []
        for p in range(2):
            for r in range(rows):
                at, index = slots.slots[p][r]
                source = panel_refs[at] if index is None else panel_refs[at].at[index]
                target = out_ref.at[
                    :, r if packed else 0,
                    pl.ds(0 if packed else r * height, height),
                    pl.ds(p * width, width),
                ]
                copies.append(pltpu.make_async_copy(source, target, sem.at[r, p]))
        for copy in copies:
            copy.start()
        for copy in copies:
            copy.wait()

    return pl.pallas_call(
        kernel,
        out_shape=jax.ShapeDtypeStruct((levels, chunks, chunk, 2 * width), BF16),
        in_specs=[ANYWHERE] * len(slots.operands),
        out_specs=WHOLE,
        scratch_shapes=[pltpu.SemaphoreType.DMA((rows, 2))],
        compiler_params=params(8),
        cost_estimate=large_cost(),
        name="pack_rows",
    )(*slots.operands)


def level_products(
    rows, width, height, packed, level, place, weights, level_slots, blocks, panels,
    total, rest, next_total, parents, next_diag, after,
):
    count = len(level_slots)
    slots = Slots(level_slots)
    has_next = next_total is not None
    local = rows * height
    half = width // 2
    part = half // rows
    wide = 2 * width
    kinds = 2 if has_next else 1

    def kernel(*refs):
        refs = list(refs)

        def take(n):
            return [refs.pop(0) for _ in range(n)]

        place_ref, weight_ref = take(2)
        piece_refs = take(len(slots.operands))
        block_ref, panel_ref, total_ref, rest_ref = take(4)
        if has_next:
            next_total_ref, parent_ref, next_diag_ref = take(3)
        take(len(after))
        if has_next:
            next_out_ref, next_rest_ref = take(2)
        out_refs = take(3) if packed else take(2)
        left_buf, x_buf, sums, diag_buf = take(4)
        assert not refs

        inner, my_row, pole = place_ref[0], place_ref[1], place_ref[2]
        first = place_ref[3].astype(F32)
        weight_real = weight_ref[0]
        weight_imag = weight_ref[1]

        for n in range(count):
            left_buf[:, n * 2 * height : (n + 1) * 2 * height] = slots.left(piece_refs, n, inner)

        late = mm(left_buf[...], block_ref[...].reshape(count * 2 * height, local))
        x = -(total_ref[...] + late)
        term = weight_real * x[width:] + weight_imag * x[:width]
        if packed:
            low, upper = term[:half], term[half:]
            mine = jnp.where(pole == 0, low, upper)
            sent = jnp.where(pole == 0, upper, low)
            for t in range(rows):
                columns = slice(t * height, (t + 1) * height)
                out_refs[0][t, :half, :] = mine[:, columns]
                out_refs[1 + 2 * t // rows][t % (rows // 2), :half, :] = sent[:, columns]
        else:
            out_refs[0][...] = term
        x_high, x_low = split(x)
        x_buf[:wide] = x_high
        x_buf[wide : 2 * wide] = x_low
        if has_next:
            x_buf[2 * wide :] = x_high
        for k in range(kinds):
            both = mm(x_buf[: 2 * wide], panel_ref[level + k].reshape(local, wide))
            sums[:, k * wide : (k + 1) * wide] = both[:wide] + both[wide:]
        if has_next:
            next_out_ref[...] = next_total_ref[...] + mm(parent_ref[level], x_buf[...])

        def complex_sum(k):
            at = k * wide
            real = sums[:width, at : at + width] - sums[width:, at + width : at + wide]
            imag = sums[:width, at + width : at + wide] + sums[width:, at : at + width]
            return real, imag

        own_real, own_imag = complex_sum(0)
        scale = first if level == 0 else 1.0
        y_real = rest_ref[0] * scale - own_real.T
        y_imag = rest_ref[1] * scale - own_imag.T
        diag_buf[...] = weight_real * y_imag + weight_imag * y_real
        if packed:
            for t in range(rows):
                places = ((out_refs[0], t, pole), (out_refs[1 + 2 * t // rows], t % (rows // 2), 1 - pole))
                for ref, n, side in places:
                    at = pl.multiple_of(side * half + (my_row ^ t) * part, part)
                    ref[n, half:, :] = diag_buf[pl.ds(at, part), :]
        else:
            out_refs[1][...] = diag_buf[...]
        if has_next:
            parent = parent_ref[level]
            parent_high, parent_low = parent[:, :wide], parent[:, 2 * wide :]
            follow_real, follow_imag = complex_sum(1)
            y_high, y_low = split(jnp.concatenate([y_real, y_imag], axis=1))
            mixed = mm_t(y_high, parent_high) + mm_t(y_low, parent_high) + mm_t(y_high, parent_low)
            z = -jnp.concatenate(
                [follow_real + mixed[:, :width], follow_imag + mixed[:, width:]], axis=0
            )
            z_high, z_low = split(z)
            back = mm(parent, jnp.concatenate([z_high, z_low, z_high], axis=0))
            next_rest_ref[0] = next_diag_ref[0] * first - back[:width]
            next_rest_ref[1] = next_diag_ref[1] * first - back[width:]

    operands = [place, weights] + slots.operands + [blocks, panels, total, rest]
    specs = [SCALARS, SCALARS] + [WHOLE] * (len(slots.operands) + 4)
    outs = []
    aliases = {}
    if has_next:
        aliases = {len(operands): 0}
        operands += [next_total, parents, next_diag]
        specs += [WHOLE] * 3
        outs += [
            jax.ShapeDtypeStruct((wide, local), F32),
            jax.ShapeDtypeStruct((2, width, width), F32),
        ]
    operands += after
    specs += [ANYWHERE] * len(after)
    if packed:
        outs.append(jax.ShapeDtypeStruct((rows, half + part, height), F32))
        outs += [jax.ShapeDtypeStruct((rows // 2, half + part, height), F32)] * 2
    else:
        outs += [
            jax.ShapeDtypeStruct((width, local), F32),
            jax.ShapeDtypeStruct((width, width), F32),
        ]
    return pl.pallas_call(
        kernel,
        out_shape=outs,
        in_specs=specs,
        out_specs=[WHOLE] * len(outs),
        input_output_aliases=aliases,
        scratch_shapes=[
            pltpu.VMEM((wide, count * 2 * height), BF16),
            pltpu.VMEM(((3 if has_next else 2) * wide, local), BF16),
            pltpu.VMEM((wide, kinds * wide), F32),
            pltpu.VMEM((width, width), F32),
        ],
        compiler_params=params(24),
        cost_estimate=large_cost(),
        name="level_%d" % level,
    )(*operands)


def join(values, after=()):
    def kernel(*refs):
        for n in range(len(values)):
            refs[-1][n] = refs[n][...]

    return pl.pallas_call(
        kernel,
        out_shape=jax.ShapeDtypeStruct((len(values),) + values[0].shape, values[0].dtype),
        in_specs=[WHOLE] * len(values) + [ANYWHERE] * len(after),
        out_specs=WHOLE,
        compiler_params=params(8),
        cost_estimate=small_cost(),
        name="join",
    )(*values, *after)


def cut(values, begin, after):
    count, height, width = len(values), values[0].shape[1] - begin, values[0].shape[2]

    def kernel(*refs):
        for n in range(count):
            refs[-1][n] = refs[n][0, begin:]

    return pl.pallas_call(
        kernel,
        out_shape=jax.ShapeDtypeStruct((count, height, width), F32),
        in_specs=[WHOLE] * count + [ANYWHERE] * len(after),
        out_specs=WHOLE,
        compiler_params=params(8),
        cost_estimate=small_cost(),
        name="cut",
    )(*values, *after)


def gate(values, after):
    count = len(values)

    def kernel(*refs):
        for n in range(count):
            refs[n - count][...] = refs[n][...]

    return pl.pallas_call(
        kernel,
        out_shape=[jax.ShapeDtypeStruct(value.shape, value.dtype) for value in values],
        in_specs=[WHOLE] * count + [ANYWHERE] * len(after),
        out_specs=[WHOLE] * count,
        compiler_params=params(8),
        cost_estimate=small_cost(),
        name="gate",
    )(*values, *after)


def add_parts(kept, received):
    levels = len(kept)
    rows = kept[0].shape[0]

    def kernel(*refs):
        for k in range(levels):
            for t in range(rows):
                got = refs[levels + 2 * k + 2 * t // rows][t % (rows // 2)]
                refs[3 * levels + t][k] = refs[k][t] + got

    return pl.pallas_call(
        kernel,
        out_shape=[jax.ShapeDtypeStruct((levels,) + kept[0].shape[1:], F32)] * rows,
        in_specs=[WHOLE] * (3 * levels),
        out_specs=[WHOLE] * rows,
        compiler_params=params(12),
        cost_estimate=small_cost(),
        name="add_parts",
    )(*kept, *received)


def gather_four(piece, me, axis, after, held, level):
    inner = (me == 1) | (me == 2)
    pairs = [(0, 1), (1, 0), (2, 3), (3, 2)]
    middle_pairs = [(1, 2), (2, 1)]
    outer_pairs = [(1, 0), (2, 3)]
    owners = [
        me,
        me ^ 1,
        jnp.where(inner, 3 - me, me ^ 2),
        jnp.where(inner, (3 - me) ^ 1, me ^ 3),
    ]
    near = lax.ppermute(piece, axis, pairs)
    joined = join([piece, near], after + held)
    middle = lax.ppermute(joined, axis, middle_pairs)
    if level == 0:
        outers = [(lax.ppermute(middle[n], axis, outer_pairs), None) for n in range(2)]
    else:
        outer = lax.ppermute(middle, axis, outer_pairs)
        outers = [(outer, n) for n in range(2)]
    far = [[(middle, n), outers[n]] for n in range(2)]
    after[:] = [joined]
    return owners, [[(piece, None)], [(near, None)]], far


def gather_line(piece, me, count, axis):
    owners, slots = [me], [[(piece, None)]]
    from_left = from_right = piece
    for step in range(1, count):
        from_left = lax.ppermute(from_left, axis, [(i, i + 1) for i in range(step - 1, count - 1)])
        from_right = lax.ppermute(from_right, axis, [(i, i - 1) for i in range(1, count - step + 1)])
        if 2 * step >= count:
            owners.append(jnp.clip(jnp.where(me >= step, me - step, me + step), 0, count - 1))
            slots.append([(jnp.where(me >= step, from_left, from_right), None)])
        else:
            owners += [jnp.maximum(me - step, 0), jnp.minimum(me + step, count - 1)]
            slots += [[(from_left, None)], [(from_right, None)]]
    return owners, slots[:1], slots[1:]


def gather_rows(value, near, far):
    first = exchange(value, "row", 4, near)
    joined = join([value, first])
    second = exchange(joined, "row", 4, far)
    found = {0: (value, None), near: (first, None), far: (second, 0), 3: (second, 1)}
    return [found[t] for t in range(4)], first, joined


def gather(piece, me, count, axis, after, held, level):
    if count == 4:
        return gather_four(piece, me, axis, after, held, level)
    return gather_line(piece, me, count, axis)


def make_per_device(sizes):
    poles, rows, cols = sizes

    def per_device(inverse_block, panels, panel_mask, parent_panels, diag_inverse, pole_weights):
        levels = panels.shape[1]
        height = panels.shape[5]
        width = panels.shape[6]
        half = width // 2
        part = half // rows
        packed = (
            poles == 2
            and rows & (rows - 1) == 0
            and cols & (cols - 1) == 0
            and height == width
            and height % 128 == 0
            and part % 8 == 0
        )
        my_pole = lax.axis_index("pole")
        my_row = lax.axis_index("row")
        my_col = lax.axis_index("col")
        first = ((my_row == 0) & (my_col == 0)).astype(jnp.int32)
        inner = ((my_col == 1) | (my_col == 2)).astype(jnp.int32)
        blocks = inverse_block[0, :, :, 0]
        local_panels = panels[0, :, :, 0, 0]
        flags = panel_mask[:, 0, 0]
        weights = pole_weights[0]
        flipped = (2, width, height)

        def masked(which, after):
            keep = bool(after)
            outs = [jax.ShapeDtypeStruct(flipped, BF16)] * len(which)
            if keep:
                outs += [jax.ShapeDtypeStruct((levels, height, width), BF16)] * 2
            return pl.pallas_call(
                functools.partial(mask_kernel, which, keep),
                out_shape=outs,
                in_specs=[FAR, FAR] + [ANYWHERE] * len(after),
                out_specs=[WHOLE] * len(outs),
                scratch_shapes=[
                    pltpu.VMEM((levels if keep else len(which),) + local_panels.shape[1:], BF16),
                    pltpu.SMEM((levels,), jnp.int32),
                    pltpu.SemaphoreType.DMA((2,)),
                ],
                compiler_params=params(8),
                cost_estimate=small_cost(),
                name="mask_rows" if keep else "mask",
            )(flags, local_panels, *after)

        pieces = list(masked([0], []))
        *more, kept_real, kept_imag = masked(list(range(1, levels)), pieces)
        pieces += more
        parents = pl.pallas_call(
            parent_kernel,
            out_shape=jax.ShapeDtypeStruct((levels - 1, 2 * width, 6 * width), BF16),
            in_specs=[WHOLE],
            out_specs=WHOLE,
            compiler_params=params(12),
            cost_estimate=small_cost(),
            name="parents",
        )(parent_panels[0])
        held = [[] for _ in pieces]
        if packed and rows == 4:
            reals, *steps_real = gather_rows(kept_real, 1, 2)
            imags, *steps_imag = gather_rows(kept_imag, 2, 1)
            held[1] = [steps_real[0], steps_imag[0]]
            held[2] = [steps_real[1], steps_imag[1]]
        elif packed:
            reals, imags = [
                [(value, None)]
                + [(exchange(value, "row", rows, t), None) for t in range(1, rows)]
                for value in (kept_real, kept_imag)
            ]
        else:
            reals, imags = [
                [(piece, None) for piece in lax.all_gather(value, "row")]
                for value in (kept_real, kept_imag)
            ]

        after = []
        gathered = []
        for k, piece in enumerate(pieces):
            gathered.append(gather(piece, my_col, cols, "col", after, held[k], k))

        def sum_rows(stack):
            return tree_sum([stack[0]] + [exchange(stack[t], "row", rows, t) for t in range(1, rows)])

        def spread(piece):
            whole = tree_sum([piece] + [exchange(piece, "col", cols, t) for t in range(1, cols)])
            whole = jnp.stack([whole] + [exchange(whole, "row", rows, t) for t in range(1, rows)])
            whole = xor_order(whole, my_row, rows)
            other = exchange(whole, "pole", 2, 1)
            return xor_order(jnp.stack([whole, other]), my_pole, 2)

        owners = gathered[0][0]
        place = jnp.stack(
            [jnp.asarray(v, jnp.int32) for v in [inner, my_row, my_pole, first] + owners]
        )
        late = len(gathered[0][2])
        *totals, late_blocks = early_products(
            rows,
            width,
            height,
            packed,
            place,
            [g[1] for g in gathered],
            late,
            blocks,
            [g[2][0][0][0] for g in gathered[:-1] if len(g[2][0]) == 2],
        )
        row_panels = pack_panels(levels, rows, width, height, packed, reals, imags)
        rest = diag_inverse[0, 0]
        panel_parts = []
        diag_parts = []
        kept = []
        received = []
        sums = []
        first_sum = []
        far_ordered = [s[1][0] for s in gathered[-1][2][:1] if len(s) == 2]
        ordered = [g[2][0][0][0] for g in gathered[1:-1] if len(g[2][0]) == 2]
        for level in range(levels):
            has_next = level + 1 < levels
            outs = level_products(
                rows,
                width,
                height,
                packed,
                level,
                place,
                weights,
                gathered[level][2],
                late_blocks,
                row_panels,
                totals[level],
                rest,
                totals[level + 1] if has_next else None,
                parents,
                diag_inverse[0, level + 1] if has_next else None,
                ordered if level == 0 else first_sum,
            )
            if has_next:
                totals[level + 1] = outs[0]
                rest = outs[1]
                outs = outs[2:]
            if packed:
                kept.append(outs[0])
                sent = outs[1:] if has_next else gate(outs[1:], sums)
                received += [exchange(value, "pole", 2, 1) for value in sent]
                parts = add_parts(kept, received)
                mine = sum_rows(parts)
                first_sum = [parts[0]]
                sums.append(mine)
                kept, received = [], []
            else:
                mine = lax.psum_scatter(outs[0], "row", scatter_dimension=1, tiled=True)
                mine = lax.psum_scatter(mine, "pole", scatter_dimension=0, tiled=True)
                panel_parts.append(mine.T)
                diag_parts.append(lax.psum(outs[1], ("pole", "row", "col")))
        if packed:
            panel_parts = [mine[0, :half].T for mine in sums]
            got = spread(cut(sums, half, []))
            diag_parts = [got[:, :, n].reshape(width, width) for n in range(levels)]
        return jnp.stack(panel_parts)[:, None, None], jnp.stack(diag_parts)

    return per_device


def solution(mesh):
    placed = (
        P("pole", None, None, "row", None, "col"),
        P("pole", None, None, "col", "row", None, None),
        P(None, "col", "row"),
        P("pole", None, None, None, None),
        P("pole", None, None, None, None),
        P("pole", None),
    )
    return jax.shard_map(
        make_per_device((mesh.shape["pole"], mesh.shape["row"], mesh.shape["col"])),
        mesh=mesh,
        in_specs=placed,
        out_specs=(P(None, "col", "row", None, "pole"), P()),
        check_vma=False,
    )
```

```python
import functools

import jax
import jax.numpy as jnp
from jax import lax
from jax.experimental import pallas as pl
from jax.experimental.pallas import tpu as pltpu
from jax.sharding import PartitionSpec as P

F32 = jnp.float32
BF16 = jnp.bfloat16
WHOLE = pl.BlockSpec(memory_space=pltpu.VMEM)
SCALARS = pl.BlockSpec(memory_space=pltpu.SMEM)
ANYWHERE = pl.BlockSpec(memory_space=pl.ANY)
FAR = pl.BlockSpec(memory_space=pltpu.HBM)


def params(mebibytes):
    return pltpu.CompilerParams(vmem_limit_bytes=mebibytes << 20)


def small_cost():
    return pl.CostEstimate(flops=1, bytes_accessed=1, transcendentals=0)


def large_cost():
    return pl.CostEstimate(flops=10**11, bytes_accessed=1, transcendentals=0)


def mm(left, right):
    return jnp.dot(left, right, preferred_element_type=F32)


def mm_t(left, right):
    return lax.dot_general(left, right, (((1,), (1,)), ((), ())), preferred_element_type=F32)


def split(value):
    high = value.astype(BF16)
    return high, (value - high.astype(F32)).astype(BF16)


def exchange(value, axes, count, distance):
    return lax.ppermute(value, axes, [(i, i ^ distance) for i in range(count)])


def tree_sum(values):
    while len(values) > 1:
        values = [values[i] + values[i + 1] for i in range(0, len(values), 2)]
    return values[0]


def xor_order(stack, me, count):
    bits = count.bit_length() - 1
    rest = stack.shape[1:]
    values = stack.reshape((2,) * bits + rest)
    for axis in range(bits):
        bit = (me >> (bits - 1 - axis)) & 1
        values = jnp.where(bit == 1, jnp.flip(values, axis), values)
    return values.reshape((count,) + rest)


def mask_kernel(levels, keep, flag_ref, panel_ref, *refs):
    refs = list(refs)
    if keep:
        refs.pop(0)
    out_refs = [refs.pop(0) for _ in levels]
    kept_refs = [refs.pop(0) for _ in range(2)] if keep else None
    buf, flags, sems = refs
    first = 0 if keep else levels[0]
    copies = [
        pltpu.make_async_copy(panel_ref.at[pl.ds(first, buf.shape[0])], buf, sems.at[0]),
        pltpu.make_async_copy(flag_ref, flags, sems.at[1]),
    ]
    for copy in copies:
        copy.start()
    for copy in copies:
        copy.wait()
    for k in range(buf.shape[0]):
        flag = flags[first + k].astype(F32)
        for part in range(2):
            value = buf[k, part].astype(F32) * flag
            if keep:
                kept_refs[part][k] = value.astype(BF16)
            if first + k in levels:
                out_refs[levels.index(first + k)][part] = value.T.astype(BF16)


def parent_kernel(parent_ref, out_ref):
    for k in range(parent_ref.shape[0]):
        real_high, real_low = split(parent_ref[k, 0].T)
        imag_high, imag_low = split(parent_ref[k, 1].T)
        high = left_block(real_high, imag_high)
        wide = high.shape[1]
        out_ref[k, :, :wide] = high
        out_ref[k, :, wide : 2 * wide] = high
        out_ref[k, :, 2 * wide :] = left_block(real_low, imag_low)


def left_block(real, imag):
    return jnp.concatenate(
        [jnp.concatenate([real, -imag], axis=1), jnp.concatenate([imag, real], axis=1)], axis=0
    )


class Slots:
    def __init__(self, slots):
        self.operands = []
        self.slots = []
        for slot in slots:
            self.slots.append([(self.place(array), index) for array, index in slot])

    def place(self, array):
        for n, operand in enumerate(self.operands):
            if operand is array:
                return n
        self.operands.append(array)
        return len(self.operands) - 1

    def left(self, refs, n, inner):
        parts = []
        for part in range(2):
            values = [
                refs[at][part] if index is None else refs[at][index, part]
                for at, index in self.slots[n]
            ]
            parts.append(values[0] if len(values) == 1 else jnp.where(inner == 1, *values))
        return left_block(*parts)


def block_copies(block_ref, buf, sem, owners, my_row, rows, height, ordered):
    copies = []
    for n, owner in enumerate(owners):
        if not ordered:
            copies.append([pltpu.make_async_copy(block_ref.at[:, owner], buf.at[n], sem.at[n, 0])])
            continue
        copies.append(
            [
                pltpu.make_async_copy(
                    block_ref.at[
                        :, owner, :, pl.ds(pl.multiple_of((my_row ^ t) * height, height), height)
                    ],
                    buf.at[n, :, :, pl.ds(t * height, height)],
                    sem.at[n, t],
                )
                for t in range(rows)
            ]
        )
    return copies


def early_products(rows, width, height, ordered, place, level_slots, late, blocks, after):
    levels = len(level_slots)
    count = len(level_slots[0])
    slots = Slots([slot for level in level_slots for slot in level])
    local = rows * height

    def kernel(place_ref, block_ref, *refs):
        piece_refs = refs[: len(slots.operands)]
        out_refs = refs[len(slots.operands) + len(after) :][:levels]
        late_ref, buf, left_buf, sem, late_sem = refs[-5:]
        my_row = place_ref[1]
        owners = [place_ref[4 + n] for n in range(count)]
        copies = block_copies(block_ref, buf, sem, owners, my_row, rows, height, ordered)
        owners = [place_ref[4 + count + n] for n in range(late)]
        late_copies = sum(
            block_copies(block_ref, late_ref, late_sem, owners, my_row, rows, height, ordered), []
        )
        for copy in sum(copies, []) + late_copies:
            copy.start()
        for level in range(levels):
            for n in range(count):
                left_buf[
                    level * 2 * width : (level + 1) * 2 * width,
                    n * 2 * height : (n + 1) * 2 * height,
                ] = slots.left(piece_refs, level * count + n, place_ref[0])
        for copy in sum(copies, []):
            copy.wait()
        right = buf[...].reshape(count * 2 * height, local)
        for level in range(levels):
            left = left_buf[level * 2 * width : (level + 1) * 2 * width, :]
            out_refs[level][...] = mm(left, right)
        for copy in late_copies:
            copy.wait()

    outs = [jax.ShapeDtypeStruct((2 * width, local), F32)] * levels
    outs.append(jax.ShapeDtypeStruct((late, 2, height, local), BF16))
    return pl.pallas_call(
        kernel,
        out_shape=outs,
        in_specs=[SCALARS, FAR] + [WHOLE] * len(slots.operands) + [ANYWHERE] * len(after),
        out_specs=[WHOLE] * len(outs),
        scratch_shapes=[
            pltpu.VMEM((count, 2, height, local), BF16),
            pltpu.VMEM((levels * 2 * width, count * 2 * height), BF16),
            pltpu.SemaphoreType.DMA((count, rows)),
            pltpu.SemaphoreType.DMA((late, rows)),
        ],
        compiler_params=params(24),
        cost_estimate=large_cost(),
        name="early",
    )(place, blocks, *slots.operands, *after)


def pack_panels(levels, rows, width, height, packed, reals, imags):
    chunks = rows if packed else 1
    chunk = height if packed else rows * height
    slots = Slots([reals, imags])

    def kernel(*refs):
        panel_refs = refs[: len(slots.operands)]
        out_ref, sem = refs[len(slots.operands) :]
        copies = []
        for p in range(2):
            for r in range(rows):
                at, index = slots.slots[p][r]
                source = panel_refs[at] if index is None else panel_refs[at].at[index]
                target = out_ref.at[
                    :, r if packed else 0,
                    pl.ds(0 if packed else r * height, height),
                    pl.ds(p * width, width),
                ]
                copies.append(pltpu.make_async_copy(source, target, sem.at[r, p]))
        for copy in copies:
            copy.start()
        for copy in copies:
            copy.wait()

    return pl.pallas_call(
        kernel,
        out_shape=jax.ShapeDtypeStruct((levels, chunks, chunk, 2 * width), BF16),
        in_specs=[ANYWHERE] * len(slots.operands),
        out_specs=WHOLE,
        scratch_shapes=[pltpu.SemaphoreType.DMA((rows, 2))],
        compiler_params=params(8),
        cost_estimate=large_cost(),
        name="pack_rows",
    )(*slots.operands)


def level_products(
    rows, width, height, packed, level, place, weights, level_slots, blocks, panels,
    total, rest, next_total, parents, next_diag, after,
):
    count = len(level_slots)
    slots = Slots(level_slots)
    has_next = next_total is not None
    local = rows * height
    half = width // 2
    part = half // rows
    wide = 2 * width
    kinds = 2 if has_next else 1

    def kernel(*refs):
        refs = list(refs)

        def take(n):
            return [refs.pop(0) for _ in range(n)]

        place_ref, weight_ref = take(2)
        piece_refs = take(len(slots.operands))
        block_ref, panel_ref, total_ref, rest_ref = take(4)
        if has_next:
            next_total_ref, parent_ref, next_diag_ref = take(3)
        take(len(after))
        if has_next:
            next_out_ref, next_rest_ref = take(2)
        out_refs = take(3) if packed else take(2)
        left_buf, x_buf, sums, diag_buf = take(4)
        assert not refs

        inner, my_row, pole = place_ref[0], place_ref[1], place_ref[2]
        first = place_ref[3].astype(F32)
        weight_real = weight_ref[0]
        weight_imag = weight_ref[1]

        for n in range(count):
            left_buf[:, n * 2 * height : (n + 1) * 2 * height] = slots.left(piece_refs, n, inner)

        late = mm(left_buf[...], block_ref[...].reshape(count * 2 * height, local))
        x = -(total_ref[...] + late)
        term = weight_real * x[width:] + weight_imag * x[:width]
        if packed:
            low, upper = term[:half], term[half:]
            mine = jnp.where(pole == 0, low, upper)
            sent = jnp.where(pole == 0, upper, low)
            for t in range(rows):
                columns = slice(t * height, (t + 1) * height)
                out_refs[0][t, :half, :] = mine[:, columns]
                out_refs[1 + 2 * t // rows][t % (rows // 2), :half, :] = sent[:, columns]
        else:
            out_refs[0][...] = term
        x_high, x_low = split(x)
        x_buf[:wide] = x_high
        x_buf[wide : 2 * wide] = x_low
        if has_next:
            x_buf[2 * wide :] = x_high
        for k in range(kinds):
            both = mm(x_buf[: 2 * wide], panel_ref[level + k].reshape(local, wide))
            sums[:, k * wide : (k + 1) * wide] = both[:wide] + both[wide:]
        if has_next:
            next_out_ref[...] = next_total_ref[...] + mm(parent_ref[level], x_buf[...])

        def complex_sum(k):
            at = k * wide
            real = sums[:width, at : at + width] - sums[width:, at + width : at + wide]
            imag = sums[:width, at + width : at + wide] + sums[width:, at : at + width]
            return real, imag

        own_real, own_imag = complex_sum(0)
        scale = first if level == 0 else 1.0
        y_real = rest_ref[0] * scale - own_real.T
        y_imag = rest_ref[1] * scale - own_imag.T
        diag_buf[...] = weight_real * y_imag + weight_imag * y_real
        if packed:
            for t in range(rows):
                places = ((out_refs[0], t, pole), (out_refs[1 + 2 * t // rows], t % (rows // 2), 1 - pole))
                for ref, n, side in places:
                    at = pl.multiple_of(side * half + (my_row ^ t) * part, part)
                    ref[n, half:, :] = diag_buf[pl.ds(at, part), :]
        else:
            out_refs[1][...] = diag_buf[...]
        if has_next:
            parent = parent_ref[level]
            parent_high, parent_low = parent[:, :wide], parent[:, 2 * wide :]
            follow_real, follow_imag = complex_sum(1)
            y_high, y_low = split(jnp.concatenate([y_real, y_imag], axis=1))
            mixed = mm_t(y_high, parent_high) + mm_t(y_low, parent_high) + mm_t(y_high, parent_low)
            z = -jnp.concatenate(
                [follow_real + mixed[:, :width], follow_imag + mixed[:, width:]], axis=0
            )
            z_high, z_low = split(z)
            back = mm(parent, jnp.concatenate([z_high, z_low, z_high], axis=0))
            next_rest_ref[0] = next_diag_ref[0] * first - back[:width]
            next_rest_ref[1] = next_diag_ref[1] * first - back[width:]

    operands = [place, weights] + slots.operands + [blocks, panels, total, rest]
    specs = [SCALARS, SCALARS] + [WHOLE] * (len(slots.operands) + 4)
    outs = []
    aliases = {}
    if has_next:
        aliases = {len(operands): 0}
        operands += [next_total, parents, next_diag]
        specs += [WHOLE] * 3
        outs += [
            jax.ShapeDtypeStruct((wide, local), F32),
            jax.ShapeDtypeStruct((2, width, width), F32),
        ]
    operands += after
    specs += [ANYWHERE] * len(after)
    if packed:
        outs.append(jax.ShapeDtypeStruct((rows, half + part, height), F32))
        outs += [jax.ShapeDtypeStruct((rows // 2, half + part, height), F32)] * 2
    else:
        outs += [
            jax.ShapeDtypeStruct((width, local), F32),
            jax.ShapeDtypeStruct((width, width), F32),
        ]
    return pl.pallas_call(
        kernel,
        out_shape=outs,
        in_specs=specs,
        out_specs=[WHOLE] * len(outs),
        input_output_aliases=aliases,
        scratch_shapes=[
            pltpu.VMEM((wide, count * 2 * height), BF16),
            pltpu.VMEM(((3 if has_next else 2) * wide, local), BF16),
            pltpu.VMEM((wide, kinds * wide), F32),
            pltpu.VMEM((width, width), F32),
        ],
        compiler_params=params(24),
        cost_estimate=large_cost(),
        name="level_%d" % level,
    )(*operands)


def join(values, after=()):
    def kernel(*refs):
        for n in range(len(values)):
            refs[-1][n] = refs[n][...]

    return pl.pallas_call(
        kernel,
        out_shape=jax.ShapeDtypeStruct((len(values),) + values[0].shape, values[0].dtype),
        in_specs=[WHOLE] * len(values) + [ANYWHERE] * len(after),
        out_specs=WHOLE,
        compiler_params=params(8),
        cost_estimate=small_cost(),
        name="join",
    )(*values, *after)


def cut(values, begin, after):
    count, height, width = len(values), values[0].shape[1] - begin, values[0].shape[2]

    def kernel(*refs):
        for n in range(count):
            refs[-1][n] = refs[n][0, begin:]

    return pl.pallas_call(
        kernel,
        out_shape=jax.ShapeDtypeStruct((count, height, width), F32),
        in_specs=[WHOLE] * count + [ANYWHERE] * len(after),
        out_specs=WHOLE,
        compiler_params=params(8),
        cost_estimate=small_cost(),
        name="cut",
    )(*values, *after)


def gate(values, after):
    count = len(values)

    def kernel(*refs):
        for n in range(count):
            refs[n - count][...] = refs[n][...]

    return pl.pallas_call(
        kernel,
        out_shape=[jax.ShapeDtypeStruct(value.shape, value.dtype) for value in values],
        in_specs=[WHOLE] * count + [ANYWHERE] * len(after),
        out_specs=[WHOLE] * count,
        compiler_params=params(8),
        cost_estimate=small_cost(),
        name="gate",
    )(*values, *after)


def add_parts(kept, received):
    levels = len(kept)
    rows = kept[0].shape[0]

    def kernel(*refs):
        for k in range(levels):
            for t in range(rows):
                got = refs[levels + 2 * k + 2 * t // rows][t % (rows // 2)]
                refs[3 * levels + t][k] = refs[k][t] + got

    return pl.pallas_call(
        kernel,
        out_shape=[jax.ShapeDtypeStruct((levels,) + kept[0].shape[1:], F32)] * rows,
        in_specs=[WHOLE] * (3 * levels),
        out_specs=[WHOLE] * rows,
        compiler_params=params(12),
        cost_estimate=small_cost(),
        name="add_parts",
    )(*kept, *received)


def gather_four(piece, me, axis, after, held, level):
    inner = (me == 1) | (me == 2)
    pairs = [(0, 1), (1, 0), (2, 3), (3, 2)]
    middle_pairs = [(1, 2), (2, 1)]
    outer_pairs = [(1, 0), (2, 3)]
    owners = [
        me,
        me ^ 1,
        jnp.where(inner, 3 - me, me ^ 2),
        jnp.where(inner, (3 - me) ^ 1, me ^ 3),
    ]
    near = lax.ppermute(piece, axis, pairs)
    joined = join([piece, near], after + held)
    middle = lax.ppermute(joined, axis, middle_pairs)
    if level == 0:
        outers = [(lax.ppermute(middle[n], axis, outer_pairs), None) for n in range(2)]
    else:
        outer = lax.ppermute(middle, axis, outer_pairs)
        outers = [(outer, n) for n in range(2)]
    far = [[(middle, n), outers[n]] for n in range(2)]
    after[:] = [joined]
    return owners, [[(piece, None)], [(near, None)]], far


def gather_line(piece, me, count, axis):
    owners, slots = [me], [[(piece, None)]]
    from_left = from_right = piece
    for step in range(1, count):
        from_left = lax.ppermute(from_left, axis, [(i, i + 1) for i in range(step - 1, count - 1)])
        from_right = lax.ppermute(from_right, axis, [(i, i - 1) for i in range(1, count - step + 1)])
        if 2 * step >= count:
            owners.append(jnp.clip(jnp.where(me >= step, me - step, me + step), 0, count - 1))
            slots.append([(jnp.where(me >= step, from_left, from_right), None)])
        else:
            owners += [jnp.maximum(me - step, 0), jnp.minimum(me + step, count - 1)]
            slots += [[(from_left, None)], [(from_right, None)]]
    return owners, slots[:1], slots[1:]


def gather_rows(value, near, far):
    first = exchange(value, "row", 4, near)
    joined = join([value, first])
    second = exchange(joined, "row", 4, far)
    found = {0: (value, None), near: (first, None), far: (second, 0), 3: (second, 1)}
    return [found[t] for t in range(4)], first, joined


def gather(piece, me, count, axis, after, held, level):
    if count == 4:
        return gather_four(piece, me, axis, after, held, level)
    return gather_line(piece, me, count, axis)


def make_per_device(sizes):
    poles, rows, cols = sizes

    def per_device(inverse_block, panels, panel_mask, parent_panels, diag_inverse, pole_weights):
        levels = panels.shape[1]
        height = panels.shape[5]
        width = panels.shape[6]
        half = width // 2
        part = half // rows
        packed = (
            poles == 2
            and rows & (rows - 1) == 0
            and cols & (cols - 1) == 0
            and height == width
            and height % 128 == 0
            and part % 8 == 0
        )
        my_pole = lax.axis_index("pole")
        my_row = lax.axis_index("row")
        my_col = lax.axis_index("col")
        first = ((my_row == 0) & (my_col == 0)).astype(jnp.int32)
        inner = ((my_col == 1) | (my_col == 2)).astype(jnp.int32)
        blocks = inverse_block[0, :, :, 0]
        local_panels = panels[0, :, :, 0, 0]
        flags = panel_mask[:, 0, 0]
        weights = pole_weights[0]
        flipped = (2, width, height)

        def masked(which, after):
            keep = bool(after)
            outs = [jax.ShapeDtypeStruct(flipped, BF16)] * len(which)
            if keep:
                outs += [jax.ShapeDtypeStruct((levels, height, width), BF16)] * 2
            return pl.pallas_call(
                functools.partial(mask_kernel, which, keep),
                out_shape=outs,
                in_specs=[FAR, FAR] + [ANYWHERE] * len(after),
                out_specs=[WHOLE] * len(outs),
                scratch_shapes=[
                    pltpu.VMEM((levels if keep else len(which),) + local_panels.shape[1:], BF16),
                    pltpu.SMEM((levels,), jnp.int32),
                    pltpu.SemaphoreType.DMA((2,)),
                ],
                compiler_params=params(8),
                cost_estimate=small_cost(),
                name="mask_rows" if keep else "mask",
            )(flags, local_panels, *after)

        pieces = list(masked([0], []))
        *more, kept_real, kept_imag = masked(list(range(1, levels)), pieces)
        pieces += more
        parents = pl.pallas_call(
            parent_kernel,
            out_shape=jax.ShapeDtypeStruct((levels - 1, 2 * width, 6 * width), BF16),
            in_specs=[WHOLE],
            out_specs=WHOLE,
            compiler_params=params(12),
            cost_estimate=small_cost(),
            name="parents",
        )(parent_panels[0])
        held = [[] for _ in pieces]
        if packed and rows == 4:
            reals, *steps_real = gather_rows(kept_real, 1, 2)
            imags, *steps_imag = gather_rows(kept_imag, 2, 1)
            held[1] = [steps_real[0], steps_imag[0]]
            held[2] = [steps_real[1], steps_imag[1]]
        elif packed:
            reals, imags = [
                [(value, None)]
                + [(exchange(value, "row", rows, t), None) for t in range(1, rows)]
                for value in (kept_real, kept_imag)
            ]
        else:
            reals, imags = [
                [(piece, None) for piece in lax.all_gather(value, "row")]
                for value in (kept_real, kept_imag)
            ]

        after = []
        gathered = []
        for k, piece in enumerate(pieces):
            gathered.append(gather(piece, my_col, cols, "col", after, held[k], k))

        def sum_rows(stack):
            return tree_sum([stack[0]] + [exchange(stack[t], "row", rows, t) for t in range(1, rows)])

        def spread(piece):
            whole = tree_sum([piece] + [exchange(piece, "col", cols, t) for t in range(1, cols)])
            whole = jnp.stack([whole] + [exchange(whole, "row", rows, t) for t in range(1, rows)])
            whole = xor_order(whole, my_row, rows)
            other = exchange(whole, "pole", 2, 1)
            return xor_order(jnp.stack([whole, other]), my_pole, 2)

        owners = gathered[0][0]
        place = jnp.stack(
            [jnp.asarray(v, jnp.int32) for v in [inner, my_row, my_pole, first] + owners]
        )
        late = len(gathered[0][2])
        *totals, late_blocks = early_products(
            rows,
            width,
            height,
            packed,
            place,
            [g[1] for g in gathered],
            late,
            blocks,
            [g[2][0][0][0] for g in gathered[:-1] if len(g[2][0]) == 2],
        )
        row_panels = pack_panels(levels, rows, width, height, packed, reals, imags)
        rest = diag_inverse[0, 0]
        panel_parts = []
        diag_parts = []
        kept = []
        received = []
        sums = []
        first_sum = []
        far_ordered = [s[1][0] for s in gathered[-1][2][:1] if len(s) == 2]
        ordered = [g[2][0][0][0] for g in gathered[1:-1] if len(g[2][0]) == 2]
        for level in range(levels):
            has_next = level + 1 < levels
            outs = level_products(
                rows,
                width,
                height,
                packed,
                level,
                place,
                weights,
                gathered[level][2],
                late_blocks,
                row_panels,
                totals[level],
                rest,
                totals[level + 1] if has_next else None,
                parents,
                diag_inverse[0, level + 1] if has_next else None,
                ordered if level == 0 else first_sum,
            )
            if has_next:
                totals[level + 1] = outs[0]
                rest = outs[1]
                outs = outs[2:]
            if packed:
                kept.append(outs[0])
                sent = outs[1:] if has_next else gate(outs[1:], sums)
                received += [exchange(value, "pole", 2, 1) for value in sent]
                parts = add_parts(kept, received)
                mine = sum_rows(parts)
                first_sum = [parts[0]]
                sums.append(mine)
                kept, received = [], []
            else:
                mine = lax.psum_scatter(outs[0], "row", scatter_dimension=1, tiled=True)
                mine = lax.psum_scatter(mine, "pole", scatter_dimension=0, tiled=True)
                panel_parts.append(mine.T)
                diag_parts.append(lax.psum(outs[1], ("pole", "row", "col")))
        if packed:
            panel_parts = [mine[0, :half].T for mine in sums]
            got = spread(cut(sums, half, []))
            diag = jnp.moveaxis(got, 2, 0).reshape(levels, width, width)
            return jnp.stack(panel_parts)[:, None, None], diag
        return jnp.stack(panel_parts)[:, None, None], jnp.stack(diag_parts)

    return per_device


def solution(mesh):
    placed = (
        P("pole", None, None, "row", None, "col"),
        P("pole", None, None, "col", "row", None, None),
        P(None, "col", "row"),
        P("pole", None, None, None, None),
        P("pole", None, None, None, None),
        P("pole", None),
    )
    return jax.shard_map(
        make_per_device((mesh.shape["pole"], mesh.shape["row"], mesh.shape["col"])),
        mesh=mesh,
        in_specs=placed,
        out_specs=(P(None, "col", "row", None, "pole"), P()),
        check_vma=False,
    )
```
